128 devices in a mesh: scen: 4 (over x), arc: 32 (over z, y, core).
Axes of the slice: x: 4, y: 4, z: 4, core: 2. Of those that a mesh axis runs over, the one named last changes fastest.
Arguments:
- tiles: bfloat16 [65536, 128, 128], P(('scen', 'arc'))
- tile_rows: int32 [65536], P(('scen', 'arc')), may hold values from 0 to 511, as said below
- tile_cols: int32 [65536], P(('scen', 'arc')), may hold values from 0 to 31, as said below
- design: int32 [131072], P('arc'), may hold values 0 or 1
- cost: float32 [16, 131072], P('scen', 'arc')
- rhs: float32 [262144], P('scen'), may hold values from -6 to 6
- primal: float32 [16, 131072], P('scen', 'arc'), may hold values from 0 to 2
- dual: float32 [262144], P('scen'), may hold values from 0 to 1
- step_size: float32 [], replicated, may hold values from 0.3 to 0.9
Outputs:
- new_primal: float32 [16, 131072], P('scen', 'arc')
- new_dual: float32 [262144], P(('scen', 'arc'))
- movement: float32 [], replicated
- interaction: float32 [], replicated
The draws below stay inside these ranges and needn't reach their ends.
Inputs may be any that keep to these rules, and one draw needn't show every extreme that they name: `tile_rows`: on each device the 512 blocks lie in distinct block rows, one in every block row of the device; block rows k * 128 to (k + 1) * 128 - 1 hold the device's k-th scenario. `tile_cols`: within each scenario of a device, every one of the 32 block columns holds the same number of blocks.
All inputs are finite; a program needn't handle non-finite values. No bound on the sum of `design` on one device may be relied on, other than what follows from the above.
Results may differ from the reference program's by a relative error of at most 0.0034.
Values sent between devices are 32-bit elements; how exact they have to be, the bound alone decides.
No kernel may reach another device: no remote copies, remote signals or barrier semaphores. Data moves between devices by JAX's collectives and lax.ppermute only.
A program may use at most 128 MiB of HBM per device.

```python
import math
import jax
import jax.numpy as jnp
from jax import lax

TILE = 128
SWEEPS = 2
SCEN_DEV = 4
ROW_TILES = 128
COL_TILES = 32
SCENARIOS = 16
ARCS = 131072
ROWS = 262144
TILES = 65536
N_SCEN = 4
N_ARC = 32


def tile_pattern(key):
    ndev = N_SCEN * N_ARC
    row_tiles_dev = SCEN_DEV * ROW_TILES
    groups = row_tiles_dev // COL_TILES
    first, second = jax.random.split(key)
    order = jax.vmap(lambda k: jax.random.permutation(k, row_tiles_dev))(jax.random.split(first, ndev))
    column_sets = jax.vmap(lambda k: jax.random.permutation(k, COL_TILES))(jax.random.split(second, ndev * groups))
    column_sets = column_sets.reshape(ndev, row_tiles_dev)
    columns = jnp.take_along_axis(column_sets, order, axis=1)
    return (order.reshape(-1).astype(jnp.int32), columns.reshape(-1).astype(jnp.int32))


def draw_tile_rows(key, part):
    shared = tile_pattern(key)
    return shared[0]


def draw_tile_cols(key, part):
    shared = tile_pattern(key)
    return shared[1]


def draw_tiles(key, part):
    key = jax.random.fold_in(key, 11)
    first, second, third = jax.random.split(key, 3)
    count = TILES
    base = jax.random.normal(first, (count, TILE, TILE), jnp.float32)
    top = math.log(10.0)
    row_factor = jnp.exp(jax.random.uniform(second, (count, TILE, 1), jnp.float32) * top)
    col_factor = jnp.exp(jax.random.uniform(third, (count, 1, TILE), jnp.float32) * top)
    return (base * row_factor * col_factor).astype(jnp.bfloat16)


def draw_cost(key, part):
    key = jax.random.fold_in(key, 5)
    first, second = jax.random.split(key)
    shape = (SCENARIOS, ARCS)
    rise = 1.0 + 2.0 * jnp.arange(ARCS, dtype=jnp.float32) / (ARCS - 1)
    magnitude = jnp.exp(jax.random.uniform(second, shape, jnp.float32) * math.log(10.0))
    base = jax.random.normal(first, shape, jnp.float32) + 0.3
    return base * magnitude * rise[None, :]


def place_ends(result, rng, smallest, high):
    extent = result.shape
    spot = [jax.random.randint(jax.random.fold_in(rng, axis), (), 0, extent[axis]) for axis in range(len(extent))]
    result = result.at[tuple(spot)].set(smallest)
    longest = extent.index(max(extent))
    spot[longest] = (spot[longest] + 1) % extent[longest]
    return result.at[tuple(spot)].set(high)


def shard_levels(key, dims, shards, least, top_value):
    factor_of, own = 1.0, jax.random.fold_in(key, 6)
    for position, blocks in shards:
        draws = jnp.exp(jax.random.uniform(jax.random.fold_in(own, position), (blocks,), jnp.float32, least / len(shards), top_value / len(shards)))
        factor_of = factor_of * jnp.repeat(draws, dims[position] // blocks).reshape([-1 if axis == position else 1 for axis in range(len(dims))])
    return factor_of


def centred(own_key, extent, width, limit, cuts=(), kind=jnp.bfloat16):
    result = width * jax.random.normal(own_key, extent, jnp.float32)
    if cuts:
        result = result * shard_levels(own_key, extent, cuts, -0.22, 0.18)
    return jnp.clip(result, -limit, limit).astype(kind)


def setup_inputs(seed: int = 0) -> dict:
    arg_keys = jax.random.split(jax.random.key(seed), 10)
    return {
        "tiles": draw_tiles(jax.random.fold_in(arg_keys[9], 71), 0),
        "tile_rows": draw_tile_rows(jax.random.fold_in(arg_keys[9], 71), 0),
        "tile_cols": draw_tile_cols(jax.random.fold_in(arg_keys[9], 71), 0),
        "design": place_ends((jax.random.randint(arg_keys[3], (ARCS,), 0, 2) < 1).astype(jnp.int32), jax.random.fold_in(arg_keys[3], 1), 0, 1),
        "cost": draw_cost(jax.random.fold_in(arg_keys[9], 71), 0),
        "rhs": centred(arg_keys[5], (ROWS,), 1.0, 6.0, ((0, 4),), jnp.float32),
        "primal": jnp.clip(2.0 * jax.random.uniform(arg_keys[6], (SCENARIOS, ARCS), jnp.float32) ** shard_levels(arg_keys[6], (SCENARIOS, ARCS), ((0, 4), (1, 32)), -0.2, 0.2), 0.0, 2.0),
        "dual": jnp.clip(1.0 * jax.random.uniform(arg_keys[7], (ROWS,), jnp.float32) ** shard_levels(arg_keys[7], (ROWS,), ((0, 4),), -0.2, 0.2), 0.0, 1.0),
        "step_size": jnp.clip(jax.random.uniform(arg_keys[8], (), jnp.float32, 0.3, 0.9), 0.3, 0.9),
    }


def reference(tiles, tile_rows, tile_cols, design, cost, rhs, primal, dual, step_size):
    ndev = N_SCEN * N_ARC
    row_tiles_dev = SCEN_DEV * ROW_TILES
    copies = SCEN_DEV * COL_TILES
    tiles_dev = tiles.reshape(ndev, row_tiles_dev, TILE, TILE)
    rows_dev = tile_rows.reshape(ndev, row_tiles_dev).astype(jnp.int32)
    cols_dev = tile_cols.reshape(ndev, row_tiles_dev).astype(jnp.int32)
    copy_dev = rows_dev // ROW_TILES * COL_TILES + cols_dev
    is_design = design == 1
    device_ids = jnp.arange(ndev, dtype=jnp.int32)

    def to_dev_cols(values):
        shaped = values.reshape(N_SCEN, SCEN_DEV, N_ARC, COL_TILES, TILE)
        return shaped.transpose(0, 2, 1, 3, 4).reshape(ndev, copies, TILE)

    def from_dev_cols(values):
        shaped = values.reshape(N_SCEN, N_ARC, SCEN_DEV, COL_TILES, TILE)
        return shaped.transpose(0, 2, 1, 3, 4).reshape(SCENARIOS, ARCS)
    row_scale = jnp.ones((ROWS,), jnp.float32)
    col_scale = jnp.ones((SCENARIOS, ARCS), jnp.float32)
    for sweep in range(SWEEPS):
        row_view = row_scale.reshape(N_SCEN, row_tiles_dev, TILE)
        col_view = to_dev_cols(col_scale)

        def peaks(device):
            magnitude = jnp.abs(tiles_dev[device])
            row_part = row_view[device // N_ARC][rows_dev[device]]
            col_part = col_view[device][copy_dev[device]]
            row_vals = row_part * lax.optimization_barrier(jnp.max(magnitude * col_part[:, None, :], axis=2))
            col_vals = col_part * lax.optimization_barrier(jnp.max(magnitude * row_part[:, :, None], axis=1))
            row_peak = jnp.zeros((row_tiles_dev, TILE), jnp.float32).at[rows_dev[device]].max(row_vals)
            col_peak = jnp.zeros((copies, TILE), jnp.float32).at[copy_dev[device]].max(col_vals)
            return (row_peak, col_peak)
        row_parts, col_parts = lax.map(peaks, device_ids)
        row_peak = lax.optimization_barrier(jnp.max(row_parts.reshape(N_SCEN, N_ARC, row_tiles_dev * TILE), axis=1)).reshape(ROWS)
        col_peak = from_dev_cols(col_parts)
        col_peak = jnp.where(is_design[None, :], lax.optimization_barrier(jnp.max(col_peak, axis=0))[None, :], col_peak)
        row_scale = row_scale / jnp.sqrt(row_peak)
        col_scale = col_scale / jnp.sqrt(col_peak)
    cost_total = jnp.sum((col_scale * cost) ** 2)
    rhs_total = jnp.sum((row_scale * rhs) ** 2)
    omega = jnp.sqrt(cost_total + 1e-06) / jnp.sqrt(rhs_total + 1e-06)
    tau = step_size / omega
    sigma = step_size * omega
    dual_low = dual.astype(jnp.bfloat16).reshape(N_SCEN, row_tiles_dev, TILE)

    def back_terms(device):
        picked = dual_low[device // N_ARC][rows_dev[device]].astype(jnp.float32)
        terms = jnp.einsum('tij,ti->tj', tiles_dev[device].astype(jnp.float32), picked)
        return jax.ops.segment_sum(terms, copy_dev[device], num_segments=copies)
    back = from_dev_cols(lax.map(back_terms, device_ids))
    half = primal - tau * col_scale * col_scale * (cost - back)
    mean = lax.optimization_barrier(jnp.sum(half, axis=0)) / SCENARIOS
    new_primal = jnp.maximum(jnp.where(is_design[None, :], mean[None, :], half), 0.0)
    primal_step = new_primal - primal
    primal_view = to_dev_cols(primal.astype(jnp.bfloat16))
    step_view = to_dev_cols(primal_step.astype(jnp.bfloat16))

    def products(device):
        picked = jnp.stack((primal_view[device][copy_dev[device]], step_view[device][copy_dev[device]])).astype(jnp.float32)
        images = jnp.einsum('tij,ktj->kti', tiles_dev[device].astype(jnp.float32), picked)
        return jax.vmap(lambda part: jax.ops.segment_sum(part, rows_dev[device], num_segments=row_tiles_dev))(images)
    parts = lax.map(products, device_ids)
    totals = lax.optimization_barrier(jnp.sum(parts.reshape(N_SCEN, N_ARC, 2, row_tiles_dev * TILE), axis=1))
    old_image = totals[:, 0].reshape(ROWS)
    step_image = totals[:, 1].reshape(ROWS)
    new_dual = jnp.maximum(dual + sigma * row_scale * row_scale * (rhs - old_image - 2.0 * step_image), 0.0)
    dual_step = new_dual - dual
    movement = omega * jnp.sum((primal_step / col_scale) ** 2) + jnp.sum((dual_step / row_scale) ** 2) / omega
    interaction = jnp.sum(dual_step * step_image)
    return (new_primal, new_dual, movement, interaction)
```

```python
import functools

import jax
import jax.numpy as jnp
from jax import lax
from jax.experimental import pallas as pl
from jax.experimental.pallas import tpu as pltpu
from jax.sharding import PartitionSpec as P

TILE = 128
RING = 16
STEP = 4
NT = (((1,), (1,)), ((), ()))
F32 = jnp.float32
BF16 = jnp.bfloat16


def identity():
    rows = lax.broadcasted_iota(jnp.int32, (TILE, TILE), 0)
    cols = lax.broadcasted_iota(jnp.int32, (TILE, TILE), 1)
    return jnp.where(rows == cols, 1.0, 0.0).astype(BF16)


def sweep(order, tiles, ring, sems, per_copy, copies, body):
    ahead = RING - STEP

    def fetch(copy, b):
        slot = lax.rem(copy, RING)
        return pltpu.make_async_copy(
            tiles.at[order[copy * per_copy + b]],
            ring.at[slot, pl.ds(b * TILE, TILE)],
            sems.at[slot, b],
        )

    @pl.loop(0, ahead)
    def _(copy):
        for b in range(per_copy):
            fetch(copy, b).start()

    @pl.loop(0, copies // STEP)
    def _(step):
        first = step * STEP

        @pl.when(first + ahead < copies)
        def _():
            for u in range(STEP):
                for b in range(per_copy):
                    fetch(first + ahead + u, b).start()

        for u in range(STEP):
            for b in range(per_copy):
                fetch(first + u, b).wait()
        for u in range(STEP):
            body(u, first + u, ring.at[lax.rem(first + u, RING)])


def split_cols(values):
    return [values[:, k * TILE : (k + 1) * TILE] for k in range(values.shape[1] // TILE)]


def first_kernel(per_copy, order, rows, tiles, dual, primal, row_peak, old, col_peak, back, ring, sems, lhs):
    copies = col_peak.shape[0]
    for u in range(STEP):
        lhs[u, :TILE] = identity()

    def body(u, copy, blocks):
        place = [rows[copy * per_copy + b] for b in range(per_copy)]
        lhs[u, TILE:] = jnp.broadcast_to(primal[pl.ds(copy, 1), :], (16, TILE)).astype(BF16)
        high = jnp.max(jnp.abs(blocks[...]).reshape(per_copy * TILE // 16, 16, TILE), axis=0)
        col_peak[pl.ds(copy, 1), :] = jnp.max(high.astype(F32), axis=0, keepdims=True)
        picked = jnp.concatenate([dual[pl.ds(r, 1), :] for r in place], axis=1)
        picked = jnp.broadcast_to(picked, (16, per_copy * TILE)).astype(BF16)
        terms = jnp.dot(picked, blocks[...], preferred_element_type=F32)
        back[pl.ds(copy, 1), :] = terms[:1]
        for b in range(0, per_copy, 2):
            pair = blocks[b * TILE : (b + 2) * TILE, :]
            turned = lax.dot_general(lhs[u], pair, NT, preferred_element_type=F32)
            peaks = jnp.max(jnp.abs(turned[:TILE]), axis=0, keepdims=True)
            for k in range(2):
                here = pl.ds(place[b + k], 1)
                row_peak[here, :] = peaks[:, k * TILE : (k + 1) * TILE]
                old[here, :] = turned[TILE : TILE + 1, k * TILE : (k + 1) * TILE]

    sweep(order, tiles, ring, sems, per_copy, copies, body)


def row_kernel(per_copy, order, rows, tiles, col_scale, row_peak, ring, sems):
    eye = identity()

    def body(u, copy, blocks):
        spread = jnp.transpose(jnp.broadcast_to(col_scale[pl.ds(copy, 1), :], (TILE, TILE)))
        for b in range(0, per_copy, 2):
            pair = blocks[b * TILE : (b + 2) * TILE, :]
            turned = jnp.abs(lax.dot_general(eye, pair, NT, preferred_element_type=F32))
            for k in range(2):
                part = turned[:, k * TILE : (k + 1) * TILE] * spread
                here = pl.ds(rows[copy * per_copy + b + k], 1)
                row_peak[here, :] = jnp.max(part, axis=0, keepdims=True)

    sweep(order, tiles, ring, sems, per_copy, col_scale.shape[0], body)


def col_kernel(per_copy, order, rows, tiles, row_scale, col_peak, ring, sems):
    eye = identity()

    def body(u, copy, blocks):
        best = None
        for b in range(0, per_copy, 2):
            pair = blocks[b * TILE : (b + 2) * TILE, :]
            turned = jnp.abs(lax.dot_general(eye, pair, NT, preferred_element_type=F32))
            for k in range(2):
                scale = row_scale[pl.ds(rows[copy * per_copy + b + k], 1), :]
                part = turned[:, k * TILE : (k + 1) * TILE] * scale
                best = part if best is None else jnp.maximum(best, part)
        col_peak[pl.ds(copy, 1), :] = jnp.max(jnp.transpose(best), axis=0, keepdims=True)

    sweep(order, tiles, ring, sems, per_copy, col_peak.shape[0], body)


def image_kernel(per_copy, order, rows, tiles, step, image, ring, sems):
    def body(u, copy, blocks):
        lhs = jnp.broadcast_to(step[pl.ds(copy, 1), :], (16, TILE)).astype(BF16)
        for b in range(0, per_copy, 2):
            pair = blocks[b * TILE : (b + 2) * TILE, :]
            out = lax.dot_general(lhs, pair, NT, preferred_element_type=F32)
            for k in range(2):
                here = pl.ds(rows[copy * per_copy + b + k], 1)
                image[here, :] = out[:1, k * TILE : (k + 1) * TILE]

    sweep(order, tiles, ring, sems, per_copy, step.shape[0], body)


def run(kernel, order, rows, tiles, vectors, outs, extra=(), cost=None):
    blocks = tiles.shape[0]
    per_copy = 4
    vmem = pl.BlockSpec(memory_space=pltpu.VMEM)
    smem = pl.BlockSpec(memory_space=pltpu.SMEM)
    scratch = [
        pltpu.VMEM((RING, per_copy * TILE, TILE), BF16),
        pltpu.SemaphoreType.DMA((RING, per_copy)),
        *extra,
    ]
    return pl.pallas_call(
        functools.partial(kernel, per_copy),
        out_shape=[jax.ShapeDtypeStruct(s, F32) for s in outs],
        in_specs=[smem, smem, pl.BlockSpec(memory_space=pl.ANY)] + [vmem] * len(vectors),
        out_specs=[vmem] * len(outs),
        scratch_shapes=scratch,
        compiler_params=pltpu.CompilerParams(vmem_limit_bytes=24 * 1024 * 1024),
        cost_estimate=pl.CostEstimate(
            flops=2 * blocks * TILE**3, bytes_accessed=2 * blocks * TILE**2, transcendentals=0
        ),
    )(order, rows, tiles, *vectors)


def visiting_order(tile_rows, tile_cols, per_scen, col_tiles):
    count = tile_rows.shape[0]
    copy = tile_rows // per_scen * col_tiles + tile_cols
    ids = jnp.arange(count, dtype=jnp.int32)
    before = (copy[None, :] < copy[:, None]) | (
        (copy[None, :] == copy[:, None]) & (ids[None, :] < ids[:, None])
    )
    rank = jnp.sum(before.astype(jnp.int32), axis=1)
    hit = rank[None, :] == ids[:, None]
    order = jnp.sum(jnp.where(hit, ids[None, :], 0), axis=1)
    rows = jnp.sum(jnp.where(hit, tile_rows[None, :], 0), axis=1)
    return order, rows


def per_device(tiles, tile_rows, tile_cols, design, cost, rhs, primal, dual, step_size):
    tile = tiles.shape[1]
    scen_dev, cols_dev = primal.shape
    col_tiles = cols_dev // tile
    rows_here = dual.shape[0]
    row_tiles = rows_here // tile
    copies = scen_dev * col_tiles
    n_scen, n_arc = lax.axis_size("scen"), lax.axis_size("arc")
    scenarios = scen_dev * n_scen
    share = row_tiles // n_arc
    arc_pos = lax.axis_index("arc")
    is_design = (design == 1).reshape(1, col_tiles, tile)
    cost = cost.reshape(scen_dev, col_tiles, tile)
    primal = primal.reshape(scen_dev, col_tiles, tile)
    dual = dual.reshape(row_tiles, tile)
    rhs = rhs.reshape(row_tiles, tile)

    def own(values):
        return lax.dynamic_slice_in_dim(values, arc_pos * share, share)

    def over_scen(values):
        spread = jnp.broadcast_to(values[None], (n_scen, *values.shape))
        return lax.all_to_all(spread, "scen", 0, 0, tiled=True)

    def to_owners(values):
        k = values.shape[0]
        parts = values.reshape(k, n_arc, share, tile).transpose(1, 0, 2, 3)
        return lax.all_to_all(parts, "arc", 0, 0, tiled=True)

    def total(values):
        row = jnp.stack(values)
        spread = jnp.broadcast_to(
            jnp.pad(row, (0, tile - row.shape[0]))[None], (n_scen * n_arc, tile)
        )
        got = lax.all_to_all(spread, ("scen", "arc"), 0, 0, tiled=True)
        sums = jnp.sum(got, axis=0)
        return [sums[i] for i in range(len(values))]

    square = (row_tiles, tile)
    wide = (copies, tile)
    order, rows = visiting_order(tile_rows, tile_cols, row_tiles // scen_dev, col_tiles)

    row_peak, old, col_peak, back = run(
        first_kernel, order, rows, tiles, (dual, primal.reshape(wide)),
        (square, square, wide, wide), [pltpu.VMEM((STEP, TILE + 16, TILE), BF16)],
    )
    col_peak = col_peak.reshape(scen_dev, col_tiles, tile)
    gap = cost - back.reshape(scen_dev, col_tiles, tile)
    shared = over_scen(
        jnp.stack(
            (
                jnp.max(col_peak, axis=0),
                jnp.sum(gap / scenarios, axis=0),
                jnp.sum(primal / scenarios, axis=0),
            )
        )
    )
    shared_peak = jnp.max(shared[:, 0], axis=0)
    mean_gap = jnp.sum(shared[:, 1], axis=0)
    mean_primal = jnp.sum(shared[:, 2], axis=0)
    col_scale = 1.0 / jnp.sqrt(jnp.where(is_design, shared_peak[None], col_peak))

    (row_high,) = run(row_kernel, order, rows, tiles, (col_scale.reshape(wide),), (square,))
    got = to_owners(jnp.stack((row_peak, old, row_high)))
    own_peak = jnp.max(got[:, 0], axis=0)
    old_image = jnp.sum(got[:, 1], axis=0)
    own_high = jnp.max(got[:, 2], axis=0)
    own_scale = 1.0 / jnp.sqrt(own_peak)
    row_scale = lax.all_to_all(
        jnp.broadcast_to(own_scale[None], (n_arc, share, tile)), "arc", 0, 0, tiled=True
    ).reshape(square)
    row_own = own_scale / jnp.sqrt(own_scale * own_high)
    own_rhs = own(rhs)
    rhs_part = jnp.sum((row_own * own_rhs) ** 2)

    (col_high,) = run(col_kernel, order, rows, tiles, (row_scale,), (wide,))
    col_peak = col_scale * col_high.reshape(col_scale.shape)
    shared_peak = jnp.max(over_scen(jnp.max(col_peak, axis=0)), axis=0)
    col_scale = col_scale / jnp.sqrt(jnp.where(is_design, shared_peak[None], col_peak))
    cost_part = jnp.sum((col_scale * cost) ** 2)
    cost_total, rhs_total = total((cost_part, rhs_part))
    omega = jnp.sqrt(cost_total + 1e-06) / jnp.sqrt(rhs_total + 1e-06)
    tau = step_size / omega
    sigma = step_size * omega

    weight = tau * col_scale * col_scale
    half = primal - weight * gap
    mean = mean_primal[None] - weight * mean_gap[None]
    new_primal = jnp.maximum(jnp.where(is_design, mean, half), 0.0)
    primal_step = new_primal - primal
    (image,) = run(image_kernel, order, rows, tiles, (primal_step.reshape(wide),), (square,))
    step_image = jnp.sum(to_owners(image[None])[:, 0], axis=0)
    dual_own = own(dual)
    new_dual = jnp.maximum(
        dual_own + sigma * row_own * row_own * (own_rhs - old_image - 2.0 * step_image), 0.0
    )
    dual_step = new_dual - dual_own
    primal_total, dual_total, interaction = total(
        (
            jnp.sum((primal_step / col_scale) ** 2),
            jnp.sum((dual_step / row_own) ** 2),
            jnp.sum(dual_step * step_image),
        )
    )
    movement = omega * primal_total + dual_total / omega
    return (
        new_primal.reshape(scen_dev, cols_dev),
        new_dual.reshape(share * tile),
        movement,
        interaction,
    )


def solution(mesh):
    placed = (
        P(("scen", "arc"), None, None),
        P(("scen", "arc")),
        P(("scen", "arc")),
        P("arc"),
        P("scen", "arc"),
        P("scen"),
        P("scen", "arc"),
        P("scen"),
        P(),
    )
    return jax.shard_map(
        per_device,
        mesh=mesh,
        in_specs=placed,
        out_specs=(P("scen", "arc"), P(("scen", "arc")), P(), P()),
        check_vma=False,
    )
```

```python
import functools

import jax
import jax.numpy as jnp
from jax import lax
from jax.experimental import pallas as pl
from jax.experimental.pallas import tpu as pltpu
from jax.sharding import PartitionSpec as P

TILE = 128
PER_COPY = 4
RING = 16
STEP = 4
F32 = jnp.float32
BF16 = jnp.bfloat16


def first_kernel(
    order, rows, tiles, dual, primal, turned, row_peak, old, col_peak, back, ring, sems
):
    copies = col_peak.shape[0]
    ahead = RING - STEP

    def fetch(copy, b):
        slot = lax.rem(copy, RING)
        return pltpu.make_async_copy(
            tiles.at[order[copy * PER_COPY + b]],
            ring.at[slot, pl.ds(b * TILE, TILE)],
            sems.at[slot, b],
        )

    def one(copy):
        blocks = ring.at[lax.rem(copy, RING)]
        place = [rows[copy * PER_COPY + b] for b in range(PER_COPY)]
        high = jnp.max(jnp.abs(blocks[...]).reshape(-1, 16, TILE), axis=0)
        col_peak[pl.ds(copy, 1), :] = jnp.max(high.astype(F32), axis=0, keepdims=True)
        picked = jnp.concatenate([dual[pl.ds(r, 1), :] for r in place], axis=1)
        picked = jnp.broadcast_to(picked, (16, PER_COPY * TILE)).astype(BF16)
        terms = jnp.dot(picked, blocks[...], preferred_element_type=F32)
        back[pl.ds(copy, 1), :] = terms[:1]
        for b, r in enumerate(place):
            block = jnp.transpose(blocks[b * TILE : (b + 1) * TILE, :])
            turned[copy, :, b * TILE : (b + 1) * TILE] = block
            high = jnp.max(jnp.abs(block).reshape(-1, 16, TILE), axis=0)
            row_peak[pl.ds(r, 1), :] = jnp.max(high.astype(F32), axis=0, keepdims=True)
        values = jnp.broadcast_to(primal[pl.ds(copy, 1), :], (16, TILE)).astype(BF16)
        images = jnp.dot(values, turned[copy], preferred_element_type=F32)
        for b, r in enumerate(place):
            old[pl.ds(r, 1), :] = images[:1, b * TILE : (b + 1) * TILE]

    @pl.loop(0, ahead)
    def _(copy):
        for b in range(PER_COPY):
            fetch(copy, b).start()

    @pl.loop(0, copies // STEP)
    def _(step):
        first = step * STEP

        @pl.when(first + ahead < copies)
        def _():
            for u in range(STEP):
                for b in range(PER_COPY):
                    fetch(first + ahead + u, b).start()

        for u in range(STEP):
            for b in range(PER_COPY):
                fetch(first + u, b).wait()
        for u in range(STEP):
            one(first + u)


def each_copy(copies, one):
    @pl.loop(0, copies // STEP)
    def _(step):
        for u in range(STEP):
            one(step * STEP + u)


def row_kernel(rows, turned, col_scale, row_peak):
    def one(copy):
        spread = jnp.transpose(jnp.broadcast_to(col_scale[pl.ds(copy, 1), :], (TILE, TILE)))
        for b in range(PER_COPY):
            block = jnp.abs(turned[copy, :, b * TILE : (b + 1) * TILE].astype(F32))
            here = pl.ds(rows[copy * PER_COPY + b], 1)
            row_peak[here, :] = jnp.max(block * spread, axis=0, keepdims=True)

    each_copy(turned.shape[0], one)


def col_kernel(rows, turned, row_scale, col_peak):
    def one(copy):
        best = None
        for b in range(PER_COPY):
            scale = row_scale[pl.ds(rows[copy * PER_COPY + b], 1), :]
            part = jnp.abs(turned[copy, :, b * TILE : (b + 1) * TILE].astype(F32)) * scale
            best = part if best is None else jnp.maximum(best, part)
        col_peak[pl.ds(copy, 1), :] = jnp.max(jnp.transpose(best), axis=0, keepdims=True)

    each_copy(turned.shape[0], one)


def image_kernel(rows, turned, step, image):
    def one(copy):
        values = jnp.broadcast_to(step[pl.ds(copy, 1), :], (16, TILE)).astype(BF16)
        out = jnp.dot(values, turned[copy], preferred_element_type=F32)
        for b in range(PER_COPY):
            here = pl.ds(rows[copy * PER_COPY + b], 1)
            image[here, :] = out[:1, b * TILE : (b + 1) * TILE]

    each_copy(turned.shape[0], one)


VMEM = pl.BlockSpec(memory_space=pltpu.VMEM)
SMEM = pl.BlockSpec(memory_space=pltpu.SMEM)


def start(order, rows, tiles, dual, primal):
    square = jax.ShapeDtypeStruct(dual.shape, F32)
    wide = jax.ShapeDtypeStruct(primal.shape, F32)
    copies = primal.shape[0]
    return pl.pallas_call(
        first_kernel,
        out_shape=[
            pltpu.VMEM((copies, TILE, PER_COPY * TILE), BF16), square, square, wide, wide
        ],
        in_specs=[SMEM, SMEM, pl.BlockSpec(memory_space=pltpu.HBM), VMEM, VMEM],
        out_specs=[VMEM] * 5,
        scratch_shapes=[
            pltpu.VMEM((RING, PER_COPY * TILE, TILE), BF16),
            pltpu.SemaphoreType.DMA((RING, PER_COPY)),
        ],
        compiler_params=pltpu.CompilerParams(vmem_limit_bytes=28 * 1024 * 1024),
    )(order, rows, tiles, dual, primal)


def again(kernel, rows, turned, vector, out):
    return pl.pallas_call(
        kernel,
        out_shape=jax.ShapeDtypeStruct(out, F32),
        in_specs=[SMEM, VMEM, VMEM],
        out_specs=VMEM,
        compiler_params=pltpu.CompilerParams(vmem_limit_bytes=28 * 1024 * 1024),
    )(rows, pltpu.with_memory_space_constraint(turned, pltpu.VMEM), vector)


def visiting_order(tile_rows, tile_cols, per_scen, col_tiles):
    count = tile_rows.shape[0]
    copy = tile_rows // per_scen * col_tiles + tile_cols
    ids = jnp.arange(count, dtype=jnp.int32)
    before = (copy[None, :] < copy[:, None]) | (
        (copy[None, :] == copy[:, None]) & (ids[None, :] < ids[:, None])
    )
    rank = jnp.sum(before.astype(jnp.int32), axis=1)
    hit = rank[None, :] == ids[:, None]
    order = jnp.sum(jnp.where(hit, ids[None, :], 0), axis=1)
    rows = jnp.sum(jnp.where(hit, tile_rows[None, :], 0), axis=1)
    return order, rows


def per_device(tiles, tile_rows, tile_cols, design, cost, rhs, primal, dual, step_size):
    tile = tiles.shape[1]
    scen_dev, cols_dev = primal.shape
    col_tiles = cols_dev // tile
    rows_here = dual.shape[0]
    row_tiles = rows_here // tile
    copies = scen_dev * col_tiles
    n_scen, n_arc = lax.axis_size("scen"), lax.axis_size("arc")
    scenarios = scen_dev * n_scen
    share = row_tiles // n_arc
    arc_pos = lax.axis_index("arc")
    is_design = (design == 1).reshape(1, col_tiles, tile)
    cost = cost.reshape(scen_dev, col_tiles, tile)
    primal = primal.reshape(scen_dev, col_tiles, tile)
    dual = dual.reshape(row_tiles, tile)
    rhs = rhs.reshape(row_tiles, tile)

    def own(values):
        return lax.dynamic_slice_in_dim(values, arc_pos * share, share)

    def over_scen(values):
        spread = jnp.broadcast_to(values[None], (n_scen, *values.shape))
        return lax.all_to_all(spread, "scen", 0, 0, tiled=True)

    def to_owners(values):
        k = values.shape[0]
        parts = values.reshape(k, n_arc, share, tile).transpose(1, 0, 2, 3)
        return lax.all_to_all(parts, "arc", 0, 0, tiled=True)

    def total(values):
        row = jnp.stack(values)
        spread = jnp.broadcast_to(
            jnp.pad(row, (0, tile - row.shape[0]))[None], (n_scen * n_arc, tile)
        )
        got = lax.all_to_all(spread, ("scen", "arc"), 0, 0, tiled=True)
        sums = jnp.sum(got, axis=0)
        return [sums[i] for i in range(len(values))]

    square = (row_tiles, tile)
    wide = (copies, tile)
    order, rows = visiting_order(tile_rows, tile_cols, row_tiles // scen_dev, col_tiles)

    turned, row_peak, old, col_peak, back = start(
        order, rows, tiles, dual, primal.reshape(wide)
    )
    col_peak = col_peak.reshape(scen_dev, col_tiles, tile)
    gap = cost - back.reshape(scen_dev, col_tiles, tile)
    shared = over_scen(
        jnp.stack(
            (
                jnp.max(col_peak, axis=0),
                jnp.sum(gap / scenarios, axis=0),
                jnp.sum(primal / scenarios, axis=0),
            )
        )
    )
    shared_peak = jnp.max(shared[:, 0], axis=0)
    mean_gap = jnp.sum(shared[:, 1], axis=0)
    mean_primal = jnp.sum(shared[:, 2], axis=0)
    col_scale = 1.0 / jnp.sqrt(jnp.where(is_design, shared_peak[None], col_peak))

    row_high = again(row_kernel, rows, turned, col_scale.reshape(wide), square)
    got = to_owners(jnp.stack((row_peak, old, row_high)))
    own_peak = jnp.max(got[:, 0], axis=0)
    old_image = jnp.sum(got[:, 1], axis=0)
    own_high = jnp.max(got[:, 2], axis=0)
    own_scale = 1.0 / jnp.sqrt(own_peak)
    row_scale = lax.all_to_all(
        jnp.broadcast_to(own_scale[None], (n_arc, share, tile)), "arc", 0, 0, tiled=True
    ).reshape(square)
    row_own = own_scale / jnp.sqrt(own_scale * own_high)
    own_rhs = own(rhs)
    rhs_part = jnp.sum((row_own * own_rhs) ** 2)

    col_high = again(col_kernel, rows, turned, row_scale, wide)
    col_peak = col_scale * col_high.reshape(col_scale.shape)
    shared_peak = jnp.max(over_scen(jnp.max(col_peak, axis=0)), axis=0)
    col_scale = col_scale / jnp.sqrt(jnp.where(is_design, shared_peak[None], col_peak))
    cost_part = jnp.sum((col_scale * cost) ** 2)
    cost_total, rhs_total = total((cost_part, rhs_part))
    omega = jnp.sqrt(cost_total + 1e-06) / jnp.sqrt(rhs_total + 1e-06)
    tau = step_size / omega
    sigma = step_size * omega

    weight = tau * col_scale * col_scale
    half = primal - weight * gap
    mean = mean_primal[None] - weight * mean_gap[None]
    new_primal = jnp.maximum(jnp.where(is_design, mean, half), 0.0)
    primal_step = new_primal - primal
    image = again(image_kernel, rows, turned, primal_step.reshape(wide), square)
    step_image = jnp.sum(to_owners(image[None])[:, 0], axis=0)
    dual_own = own(dual)
    new_dual = jnp.maximum(
        dual_own + sigma * row_own * row_own * (own_rhs - old_image - 2.0 * step_image), 0.0
    )
    dual_step = new_dual - dual_own
    primal_total, dual_total, interaction = total(
        (
            jnp.sum((primal_step / col_scale) ** 2),
            jnp.sum((dual_step / row_own) ** 2),
            jnp.sum(dual_step * step_image),
        )
    )
    movement = omega * primal_total + dual_total / omega
    return (
        new_primal.reshape(scen_dev, cols_dev),
        new_dual.reshape(share * tile),
        movement,
        interaction,
    )


def solution(mesh):
    placed = (
        P(("scen", "arc"), None, None),
        P(("scen", "arc")),
        P(("scen", "arc")),
        P("arc"),
        P("scen", "arc"),
        P("scen"),
        P("scen", "arc"),
        P("scen"),
        P(),
    )
    return jax.shard_map(
        per_device,
        mesh=mesh,
        in_specs=placed,
        out_specs=(P("scen", "arc"), P(("scen", "arc")), P(), P()),
        check_vma=False,
    )
```

```python
import functools

import jax
import jax.numpy as jnp
from jax import lax
from jax.experimental import pallas as pl
from jax.experimental.pallas import tpu as pltpu
from jax.sharding import PartitionSpec as P

TILE = 128
PER_COPY = 4
RING = 16
STEP = 4
F32 = jnp.float32
BF16 = jnp.bfloat16


def first_kernel(
    order, rows, spots, tiles, dual, primal, turned, sums, col_peak, back, ring, sems
):
    copies = col_peak.shape[0]
    ahead = RING - STEP

    def fetch(copy, b):
        slot = lax.rem(copy, RING)
        return pltpu.make_async_copy(
            tiles.at[order[copy * PER_COPY + b]],
            ring.at[slot, pl.ds(b * TILE, TILE)],
            sems.at[slot, b],
        )

    def one(copy):
        blocks = ring.at[lax.rem(copy, RING)]
        place = [rows[copy * PER_COPY + b] for b in range(PER_COPY)]
        spot = [spots[copy * PER_COPY + b] for b in range(PER_COPY)]
        high = jnp.max(jnp.abs(blocks[...]).reshape(-1, 16, TILE), axis=0)
        col_peak[pl.ds(copy, 1), :] = jnp.max(high.astype(F32), axis=0, keepdims=True)
        picked = jnp.concatenate([dual[pl.ds(r, 1), :] for r in place], axis=1)
        picked = jnp.broadcast_to(picked, (16, PER_COPY * TILE)).astype(BF16)
        terms = jnp.dot(picked, blocks[...], preferred_element_type=F32)
        back[pl.ds(copy, 1), :] = terms[:1]
        for b, r in enumerate(spot):
            block = jnp.transpose(blocks[b * TILE : (b + 1) * TILE, :])
            turned[copy, :, b * TILE : (b + 1) * TILE] = block
            high = jnp.max(jnp.abs(block).reshape(-1, 16, TILE), axis=0)
            sums[0, pl.ds(r, 1), :] = jnp.max(high.astype(F32), axis=0, keepdims=True)
        values = jnp.broadcast_to(primal[pl.ds(copy, 1), :], (16, TILE)).astype(BF16)
        images = jnp.dot(values, turned[copy], preferred_element_type=F32)
        for b, r in enumerate(spot):
            sums[1, pl.ds(r, 1), :] = images[:1, b * TILE : (b + 1) * TILE]

    @pl.loop(0, ahead)
    def _(copy):
        for b in range(PER_COPY):
            fetch(copy, b).start()

    @pl.loop(0, copies // STEP)
    def _(step):
        first = step * STEP

        @pl.when(first + ahead < copies)
        def _():
            for u in range(STEP):
                for b in range(PER_COPY):
                    fetch(first + ahead + u, b).start()

        for u in range(STEP):
            for b in range(PER_COPY):
                fetch(first + u, b).wait()
        for u in range(STEP):
            one(first + u)


def each_copy(copies, one):
    @pl.loop(0, copies // STEP)
    def _(step):
        for u in range(STEP):
            one(step * STEP + u)


def row_kernel(spots, turned, col_scale, row_peak):
    def one(copy):
        spread = jnp.transpose(jnp.broadcast_to(col_scale[pl.ds(copy, 1), :], (TILE, TILE)))
        for b in range(PER_COPY):
            block = jnp.abs(turned[copy, :, b * TILE : (b + 1) * TILE].astype(F32))
            here = pl.ds(spots[copy * PER_COPY + b], 1)
            row_peak[here, :] = jnp.max(block * spread, axis=0, keepdims=True)

    each_copy(turned.shape[0], one)


def col_kernel(spots, turned, row_scale, col_peak):
    def one(copy):
        best = None
        for b in range(PER_COPY):
            scale = row_scale[pl.ds(spots[copy * PER_COPY + b], 1), :]
            part = jnp.abs(turned[copy, :, b * TILE : (b + 1) * TILE].astype(F32)) * scale
            best = part if best is None else jnp.maximum(best, part)
        col_peak[pl.ds(copy, 1), :] = jnp.max(jnp.transpose(best), axis=0, keepdims=True)

    each_copy(turned.shape[0], one)


def image_kernel(spots, turned, step, image):
    def one(copy):
        values = jnp.broadcast_to(step[pl.ds(copy, 1), :], (16, TILE)).astype(BF16)
        out = jnp.dot(values, turned[copy], preferred_element_type=F32)
        for b in range(PER_COPY):
            here = pl.ds(spots[copy * PER_COPY + b], 1)
            image[here, :] = out[:1, b * TILE : (b + 1) * TILE]

    each_copy(turned.shape[0], one)


VMEM = pl.BlockSpec(memory_space=pltpu.VMEM)
SMEM = pl.BlockSpec(memory_space=pltpu.SMEM)


def start(order, rows, spots, tiles, dual, primal):
    pair = jax.ShapeDtypeStruct((2, *dual.shape), F32)
    wide = jax.ShapeDtypeStruct(primal.shape, F32)
    copies = primal.shape[0]
    return pl.pallas_call(
        first_kernel,
        out_shape=[
            pltpu.VMEM((copies, TILE, PER_COPY * TILE), BF16), pair, wide, wide
        ],
        in_specs=[SMEM, SMEM, SMEM, pl.BlockSpec(memory_space=pltpu.HBM), VMEM, VMEM],
        out_specs=[VMEM] * 4,
        scratch_shapes=[
            pltpu.VMEM((RING, PER_COPY * TILE, TILE), BF16),
            pltpu.SemaphoreType.DMA((RING, PER_COPY)),
        ],
        compiler_params=pltpu.CompilerParams(vmem_limit_bytes=20 * 1024 * 1024),
    )(order, rows, spots, tiles, dual, primal)


def again(kernel, spots, turned, vector, out):
    return pl.pallas_call(
        kernel,
        out_shape=jax.ShapeDtypeStruct(out, F32),
        in_specs=[SMEM, VMEM, VMEM],
        out_specs=VMEM,
        compiler_params=pltpu.CompilerParams(vmem_limit_bytes=20 * 1024 * 1024),
        cost_estimate=pl.CostEstimate(flops=7 * 10**9, bytes_accessed=2**24, transcendentals=0),
    )(spots, pltpu.with_memory_space_constraint(turned, pltpu.VMEM), vector)


def visiting_order(tile_rows, tile_cols, spots, per_scen, col_tiles):
    count = tile_rows.shape[0]
    copy = tile_rows // per_scen * col_tiles + tile_cols
    ids = jnp.arange(count, dtype=jnp.int32)
    before = (copy[None, :] < copy[:, None]) | (
        (copy[None, :] == copy[:, None]) & (ids[None, :] < ids[:, None])
    )
    rank = jnp.sum(before.astype(jnp.int32), axis=1)
    hit = rank[None, :] == ids[:, None]
    order = jnp.sum(jnp.where(hit, ids[None, :], 0), axis=1)
    rows = jnp.sum(jnp.where(hit, tile_rows[None, :], 0), axis=1)
    spots = jnp.sum(jnp.where(hit, spots[None, :], 0), axis=1)
    return order, rows, spots


Z, Y, CORE = 4, 4, 2
ARC = [(z, y, c) for z in range(Z) for y in range(Y) for c in range(CORE)]


def index(z, y, c):
    return (z % Z * Y + y % Y) * CORE + c % CORE


def send(values, **by):
    dz, dy, dc = by.get("z", 0), by.get("y", 0), by.get("c", 0)
    pairs = [(index(z, y, c), index(z + dz, y + dy, c + dc)) for z, y, c in ARC]
    return lax.ppermute(values, "arc", pairs)


def swap_scen(values):
    n = lax.axis_size("scen")
    return [values] + [
        lax.ppermute(values, "scen", [(i, (i + k) % n) for i in range(n)]) for k in range(1, n)
    ]


def to_owners(values, join):
    values = join([values[:, 0], send(values[:, 1], c=1)])
    values = join([values[:, 0]] + [send(values[:, k], y=k) for k in range(1, Y)])
    return join([values[:, 0]] + [send(values[:, k], z=k) for k in range(1, Z)])


def from_owners(values):
    values = jnp.stack([values] + [send(values, z=-k) for k in range(1, Z)])
    values = jnp.stack([values] + [send(values, y=-k) for k in range(1, Y)])
    return jnp.stack([values, send(values, c=1)])


def add(parts):
    return functools.reduce(jnp.add, parts)


def high(parts):
    return functools.reduce(jnp.maximum, parts)


def high_and_add(parts):
    return jnp.stack([high([p[0] for p in parts]), add([p[1] for p in parts])])


def per_device(tiles, tile_rows, tile_cols, design, cost, rhs, primal, dual, step_size):
    tile = tiles.shape[1]
    scen_dev, cols_dev = primal.shape
    col_tiles = cols_dev // tile
    rows_here = dual.shape[0]
    row_tiles = rows_here // tile
    copies = scen_dev * col_tiles
    n_scen, n_arc = lax.axis_size("scen"), lax.axis_size("arc")
    scenarios = scen_dev * n_scen
    share = row_tiles // n_arc
    arc_pos = lax.axis_index("arc")
    dual = dual.reshape(row_tiles, tile)
    rhs = rhs.reshape(row_tiles, tile)
    is_design = (design == 1).reshape(1, col_tiles, tile)
    def own(values):
        return lax.dynamic_slice_in_dim(values, arc_pos * share, share)

    cost, primal, step_size, own_rhs, dual_own = lax.optimization_barrier(
        (
            cost.reshape(copies, tile),
            primal.reshape(copies, tile),
            jnp.full((1, tile), step_size),
            own(rhs),
            own(dual),
        )
    )
    cost = cost.reshape(scen_dev, col_tiles, tile)
    primal = primal.reshape(scen_dev, col_tiles, tile)

    def total(values, held):
        row = jnp.stack(values)
        spread = jnp.broadcast_to(
            jnp.pad(row, (0, tile - row.shape[0]))[None], (n_scen * n_arc, tile)
        )
        (spread, held) = lax.optimization_barrier((spread, held))
        got = lax.all_to_all(spread, ("scen", "arc"), 0, 0, tiled=True)
        (got, held) = lax.optimization_barrier((got, held))
        half = got.shape[0] // 2
        sums = jnp.sum(got[:half] + got[half:], axis=0)
        return [sums[i] for i in range(len(values))], held

    square = (row_tiles, tile)
    wide = (copies, tile)
    by_spot = (CORE, Y, Z, share, tile)
    owner = tile_rows // share
    away_z = ((owner >> 3) - (arc_pos >> 3)) & (Z - 1)
    away_y = ((owner >> 1) - (arc_pos >> 1)) & (Y - 1)
    away_c = (owner - arc_pos) & (CORE - 1)
    spots = ((away_c * Y + away_y) * Z + away_z) * share + tile_rows % share
    order, rows, spots = visiting_order(
        tile_rows, tile_cols, spots, row_tiles // scen_dev, col_tiles
    )

    turned, sums, col_peak, back = start(order, rows, spots, tiles, dual, primal.reshape(wide))
    col_peak = col_peak.reshape(scen_dev, col_tiles, tile)
    gap = cost - back.reshape(scen_dev, col_tiles, tile)
    shared = swap_scen(
        jnp.stack(
            (
                high([*col_peak]),
                add([*(gap / scenarios)]),
                add([*(primal / scenarios)]),
            )
        )
    )
    shared_peak = high([s[0] for s in shared])
    mean_gap = add([s[1] for s in shared])
    mean_primal = add([s[2] for s in shared])
    col_scale = 1.0 / jnp.sqrt(jnp.where(is_design, shared_peak[None], col_peak))

    own_peak, old_image = to_owners(sums.reshape(2, *by_spot), high_and_add)
    row_high = again(row_kernel, spots, turned, col_scale.reshape(wide), square)
    own_high = to_owners(row_high.reshape(1, *by_spot), high)[0]
    own_scale = 1.0 / jnp.sqrt(own_peak)
    row_scale = from_owners(own_scale).reshape(square)
    row_own = own_scale / jnp.sqrt(own_scale * own_high)
    rhs_part = jnp.sum((row_own * own_rhs) ** 2)

    col_high = again(col_kernel, spots, turned, row_scale, wide)
    col_peak = col_scale * col_high.reshape(col_scale.shape)
    shared_peak = high(swap_scen(high([*col_peak])))
    col_scale = col_scale / jnp.sqrt(jnp.where(is_design, shared_peak[None], col_peak))
    cost_part = jnp.sum((col_scale * cost) ** 2)
    held = (turned, col_scale, gap, mean_gap, mean_primal, primal, step_size, old_image, row_own, own_rhs, dual_own)
    (cost_total, rhs_total), held = total((cost_part, rhs_part), held)
    turned, col_scale, gap, mean_gap, mean_primal, primal, step_size, old_image, row_own, own_rhs, dual_own = held
    omega = jnp.sqrt(cost_total + 1e-06) / jnp.sqrt(rhs_total + 1e-06)
    tau = step_size[None] / omega
    sigma = step_size * omega

    weight = tau * col_scale * col_scale
    half = primal - weight * gap
    mean = mean_primal[None] - weight * mean_gap[None]
    new_primal = jnp.maximum(jnp.where(is_design, mean, half), 0.0)
    primal_step = new_primal - primal
    image = again(image_kernel, spots, turned, primal_step.reshape(wide), square)
    step_image = to_owners(image.reshape(1, *by_spot), add)[0]
    new_dual = jnp.maximum(
        dual_own + sigma * row_own * row_own * (own_rhs - old_image - 2.0 * step_image), 0.0
    )
    dual_step = new_dual - dual_own
    (primal_total, dual_total, interaction), _ = total(
        (
            jnp.sum((primal_step / col_scale) ** 2),
            jnp.sum((dual_step / row_own) ** 2),
            jnp.sum(dual_step * step_image),
        ),
        (),
    )
    movement = omega * primal_total + dual_total / omega
    return (
        new_primal.reshape(scen_dev, cols_dev),
        new_dual.reshape(share * tile),
        movement,
        interaction,
    )


def solution(mesh):
    placed = (
        P(("scen", "arc"), None, None),
        P(("scen", "arc")),
        P(("scen", "arc")),
        P("arc"),
        P("scen", "arc"),
        P("scen"),
        P("scen", "arc"),
        P("scen"),
        P(),
    )
    return jax.shard_map(
        per_device,
        mesh=mesh,
        in_specs=placed,
        out_specs=(P("scen", "arc"), P(("scen", "arc")), P(), P()),
        check_vma=False,
    )
```

```python
import functools

import jax
import jax.numpy as jnp
from jax import lax
from jax.experimental import pallas as pl
from jax.experimental.pallas import tpu as pltpu
from jax.sharding import PartitionSpec as P

TILE = 128
PER_COPY = 4
CHUNK = 32
RING = 4
STEP = 4
F32 = jnp.float32
BF16 = jnp.bfloat16


def peak(block):
    parts = [jnp.abs(block[k : k + 16]) for k in range(0, block.shape[0], 16)]
    while len(parts) > 1:
        parts = [jnp.maximum(a, b) for a, b in zip(parts[::2], parts[1::2])]
    return jnp.max(parts[0].astype(F32), axis=0, keepdims=True)


def first_kernel(
    rows, copy_of, spot_of, tiles, dual, primal,
    turned, slot_rows, slot_spots, sums, col_peak, back, ring, sems, seen,
):
    count = tiles.shape[0]
    copies = col_peak.shape[0]
    chunks = count // CHUNK
    col_peak[...] = jnp.zeros_like(col_peak)
    back[...] = jnp.zeros_like(back)

    def fetch(chunk):
        slot = lax.rem(chunk, RING)
        return pltpu.make_async_copy(
            tiles.at[pl.ds(chunk * CHUNK, CHUNK)], ring.at[slot], sems.at[slot]
        )

    for chunk in range(RING - 1):
        fetch(chunk).start()

    @pl.loop(0, copies)
    def _(copy):
        seen[copy] = 0

    def one(k, block):
        r = rows[k]
        spot = spot_of[k]
        copy = copy_of[k]
        nth = seen[copy]
        seen[copy] = nth + 1
        slot_rows[copy * PER_COPY + nth] = r
        slot_spots[copy * PER_COPY + nth] = spot
        here = pl.ds(copy, 1)
        col_peak[here, :] = jnp.maximum(col_peak[here, :], peak(block))
        picked = jnp.broadcast_to(dual[pl.ds(r, 1), :], (16, TILE)).astype(BF16)
        back[here, :] += jnp.dot(picked, block, preferred_element_type=F32)[:1]
        block = jnp.transpose(block)
        turned[copy, :, pl.ds(pl.multiple_of(nth * TILE, TILE), TILE)] = block
        sums[0, pl.ds(spot, 1), :] = peak(block)
        values = jnp.broadcast_to(primal[here, :], (16, TILE)).astype(BF16)
        sums[1, pl.ds(spot, 1), :] = jnp.dot(values, block, preferred_element_type=F32)[:1]

    @pl.loop(0, chunks)
    def _(chunk):
        fetch(chunk).wait()

        @pl.when(chunk + RING - 1 < chunks)
        def _():
            fetch(chunk + RING - 1).start()

        slot = lax.rem(chunk, RING)

        for at in range(CHUNK):
            one(chunk * CHUNK + at, ring[slot, at])

def each_copy(copies, one):
    @pl.loop(0, copies // STEP)
    def _(step):
        for u in range(STEP):
            one(step * STEP + u)


def row_kernel(spots, turned, col_scale, row_peak):
    def one(copy):
        spread = jnp.transpose(jnp.broadcast_to(col_scale[pl.ds(copy, 1), :], (TILE, TILE)))
        for b in range(PER_COPY):
            block = jnp.abs(turned[copy, :, b * TILE : (b + 1) * TILE].astype(F32))
            here = pl.ds(spots[copy * PER_COPY + b], 1)
            row_peak[here, :] = jnp.max(block * spread, axis=0, keepdims=True)

    each_copy(turned.shape[0], one)


def col_kernel(spots, turned, row_scale, col_peak):
    def one(copy):
        best = None
        for b in range(PER_COPY):
            scale = row_scale[pl.ds(spots[copy * PER_COPY + b], 1), :]
            part = jnp.abs(turned[copy, :, b * TILE : (b + 1) * TILE].astype(F32)) * scale
            best = part if best is None else jnp.maximum(best, part)
        col_peak[pl.ds(copy, 1), :] = jnp.max(jnp.transpose(best), axis=0, keepdims=True)

    each_copy(turned.shape[0], one)


def image_kernel(spots, turned, step, image):
    def one(copy):
        values = jnp.broadcast_to(step[pl.ds(copy, 1), :], (16, TILE)).astype(BF16)
        out = jnp.dot(values, turned[copy], preferred_element_type=F32)
        for b in range(PER_COPY):
            here = pl.ds(spots[copy * PER_COPY + b], 1)
            image[here, :] = out[:1, b * TILE : (b + 1) * TILE]

    each_copy(turned.shape[0], one)


VMEM = pl.BlockSpec(memory_space=pltpu.VMEM)
SMEM = pl.BlockSpec(memory_space=pltpu.SMEM)


def start(rows, copy_of, spot_of, tiles, dual, primal):
    pair = jax.ShapeDtypeStruct((2, *dual.shape), F32)
    wide = jax.ShapeDtypeStruct(primal.shape, F32)
    copies = primal.shape[0]
    return pl.pallas_call(
        first_kernel,
        out_shape=[
            pltpu.VMEM((copies, TILE, PER_COPY * TILE), BF16),
            jax.ShapeDtypeStruct(rows.shape, jnp.int32),
            jax.ShapeDtypeStruct(rows.shape, jnp.int32),
            pair,
            wide,
            wide,
        ],
        in_specs=[SMEM, SMEM, SMEM, pl.BlockSpec(memory_space=pltpu.HBM), VMEM, VMEM],
        out_specs=[VMEM, SMEM, SMEM, VMEM, VMEM, VMEM],
        scratch_shapes=[
            pltpu.VMEM((RING, CHUNK, TILE, TILE), BF16),
            pltpu.SemaphoreType.DMA((RING,)),
            pltpu.SMEM((copies,), jnp.int32),
        ],
        compiler_params=pltpu.CompilerParams(vmem_limit_bytes=20 * 1024 * 1024),
    )(rows, copy_of, spot_of, pltpu.with_memory_space_constraint(tiles, pltpu.HBM), dual, primal)


def again(kernel, spots, turned, vector, out):
    return pl.pallas_call(
        kernel,
        out_shape=jax.ShapeDtypeStruct(out, F32),
        in_specs=[SMEM, VMEM, VMEM],
        out_specs=VMEM,
        compiler_params=pltpu.CompilerParams(vmem_limit_bytes=20 * 1024 * 1024),
        cost_estimate=pl.CostEstimate(flops=7 * 10**9, bytes_accessed=2**24, transcendentals=0),
    )(spots, pltpu.with_memory_space_constraint(turned, pltpu.VMEM), vector)


CORE = 2


def swap_core(values):
    n = lax.axis_size("arc")
    return lax.ppermute(values, "arc", [(i, i ^ 1) for i in range(n)])


def exchange(values):
    n = lax.axis_size("arc")
    groups = [[*range(c, n, CORE)] for c in range(CORE)]
    return lax.all_to_all(values, "arc", 0, 0, axis_index_groups=groups, tiled=True)


def swap_scen(values):
    n = lax.axis_size("scen")
    return [values] + [
        lax.ppermute(values, "scen", [(i, (i + k) % n) for i in range(n)]) for k in range(1, n)
    ]


def add(parts):
    return functools.reduce(jnp.add, parts)


def high(parts):
    return functools.reduce(jnp.maximum, parts)


def per_device(tiles, tile_rows, tile_cols, design, cost, rhs, primal, dual, step_size):
    tile = tiles.shape[1]
    scen_dev, cols_dev = primal.shape
    col_tiles = cols_dev // tile
    rows_here = dual.shape[0]
    row_tiles = rows_here // tile
    copies = scen_dev * col_tiles
    n_scen, n_arc = lax.axis_size("scen"), lax.axis_size("arc")
    scenarios = scen_dev * n_scen
    share = row_tiles // n_arc
    arc_pos = lax.axis_index("arc")
    dual = dual.reshape(row_tiles, tile)
    rhs = rhs.reshape(row_tiles, tile)
    is_design = (design == 1).reshape(1, col_tiles, tile)
    def own(values):
        return lax.dynamic_slice_in_dim(values, arc_pos * share, share)

    cost, primal, step_size, own_rhs, dual_own = lax.optimization_barrier(
        (
            cost.reshape(copies, tile),
            primal.reshape(copies, tile),
            jnp.full((1, tile), step_size),
            own(rhs),
            own(dual),
        )
    )
    cost = cost.reshape(scen_dev, col_tiles, tile)
    primal = primal.reshape(scen_dev, col_tiles, tile)

    def total(values, held):
        row = jnp.stack(values)
        spread = jnp.broadcast_to(
            jnp.pad(row, (0, tile - row.shape[0]))[None], (n_scen * n_arc, tile)
        )
        (spread, held) = lax.optimization_barrier((spread, held))
        got = lax.all_to_all(spread, ("scen", "arc"), 0, 0, tiled=True)
        (got, held) = lax.optimization_barrier((got, held))
        half = got.shape[0] // 2
        sums = jnp.sum(got[:half] + got[half:], axis=0)
        return [sums[i] for i in range(len(values))], held

    square = (row_tiles, tile)
    wide = (copies, tile)
    chips = n_arc // CORE
    by_spot = (CORE, chips, share, tile)
    owner = tile_rows // share
    spot_of = ((owner ^ arc_pos) % CORE * chips + owner // CORE) * share + tile_rows % share
    copy_of = tile_rows // (row_tiles // scen_dev) * col_tiles + tile_cols

    turned, slot_rows, slot_spots, sums, col_peak, back = start(
        tile_rows, copy_of, spot_of, tiles, dual, primal.reshape(wide)
    )
    sums = sums.reshape(2, *by_spot)
    near = swap_core(sums[:, 1])
    col_peak = col_peak.reshape(scen_dev, col_tiles, tile)
    gap = cost - back.reshape(scen_dev, col_tiles, tile)
    shared = swap_scen(
        jnp.stack(
            (
                high([*col_peak]),
                add([*(gap / scenarios)]),
                add([*(primal / scenarios)]),
            )
        )
    )
    shared_peak = high([s[0] for s in shared])
    mean_gap = add([s[1] for s in shared])
    mean_primal = add([s[2] for s in shared])
    col_scale = 1.0 / jnp.sqrt(jnp.where(is_design, shared_peak[None], col_peak))

    row_high = again(row_kernel, slot_spots, turned, col_scale.reshape(wide), square)
    row_high = row_high.reshape(by_spot)
    near_high = swap_core(row_high[1])
    got = exchange(
        jnp.stack(
            (
                jnp.maximum(sums[0, 0], near[0]),
                sums[1, 0] + near[1],
                jnp.maximum(row_high[0], near_high),
            ),
            axis=1,
        )
    )
    own_peak = high([*got[:, 0]])
    old_image = add([*got[:, 1]])
    own_high = high([*got[:, 2]])
    own_scale = 1.0 / jnp.sqrt(own_peak)
    row_scale = lax.all_to_all(
        jnp.broadcast_to(own_scale[None], (n_arc, share, tile)), "arc", 0, 0, tiled=True
    ).reshape(square)
    row_own = own_scale / jnp.sqrt(own_scale * own_high)
    rhs_part = jnp.sum((row_own * own_rhs) ** 2)

    col_high = again(col_kernel, slot_rows, turned, row_scale, wide)
    col_peak = col_scale * col_high.reshape(col_scale.shape)
    shared_peak = high(swap_scen(high([*col_peak])))
    col_scale = col_scale / jnp.sqrt(jnp.where(is_design, shared_peak[None], col_peak))
    cost_part = jnp.sum((col_scale * cost) ** 2)
    held = (turned, col_scale, gap, mean_gap, mean_primal, primal, step_size, old_image, row_own, own_rhs, dual_own)
    (cost_total, rhs_total), held = total((cost_part, rhs_part), held)
    turned, col_scale, gap, mean_gap, mean_primal, primal, step_size, old_image, row_own, own_rhs, dual_own = held
    omega = jnp.sqrt(cost_total + 1e-06) / jnp.sqrt(rhs_total + 1e-06)
    tau = step_size[None] / omega
    sigma = step_size * omega

    weight = tau * col_scale * col_scale
    half = primal - weight * gap
    mean = mean_primal[None] - weight * mean_gap[None]
    new_primal = jnp.maximum(jnp.where(is_design, mean, half), 0.0)
    primal_step = new_primal - primal
    image = again(image_kernel, slot_spots, turned, primal_step.reshape(wide), square)
    image = image.reshape(by_spot)
    step_image = add([*exchange(image[0] + swap_core(image[1]))])
    new_dual = jnp.maximum(
        dual_own + sigma * row_own * row_own * (own_rhs - old_image - 2.0 * step_image), 0.0
    )
    dual_step = new_dual - dual_own
    (primal_total, dual_total, interaction), _ = total(
        (
            jnp.sum((primal_step / col_scale) ** 2),
            jnp.sum((dual_step / row_own) ** 2),
            jnp.sum(dual_step * step_image),
        ),
        (),
    )
    movement = omega * primal_total + dual_total / omega
    return (
        new_primal.reshape(scen_dev, cols_dev),
        new_dual.reshape(share * tile),
        movement,
        interaction,
    )


def solution(mesh):
    placed = (
        P(("scen", "arc"), None, None),
        P(("scen", "arc")),
        P(("scen", "arc")),
        P("arc"),
        P("scen", "arc"),
        P("scen"),
        P("scen", "arc"),
        P("scen"),
        P(),
    )
    return jax.shard_map(
        per_device,
        mesh=mesh,
        in_specs=placed,
        out_specs=(P("scen", "arc"), P(("scen", "arc")), P(), P()),
        check_vma=False,
    )
```

```python
import functools

import jax
import jax.numpy as jnp
from jax import lax
from jax.experimental import pallas as pl
from jax.experimental.pallas import tpu as pltpu
from jax.sharding import PartitionSpec as P

TILE = 128
PER_COPY = 4
CHUNK = 32
RING = 4
STEP = 4
CORE = 2
F32 = jnp.float32
BF16 = jnp.bfloat16


def peak(block):
    parts = [jnp.abs(block[k : k + 16]) for k in range(0, block.shape[0], 16)]
    while len(parts) > 1:
        parts = [jnp.maximum(a, b) for a, b in zip(parts[::2], parts[1::2])]
    return jnp.max(parts[0].astype(F32), axis=0, keepdims=True)


def by_scen(ref, scen_dev):
    size = ref.shape[0] // scen_dev
    return [ref[k * size : (k + 1) * size, :] for k in range(scen_dev)]


def add(parts):
    return functools.reduce(jnp.add, parts)


def high(parts):
    return functools.reduce(jnp.maximum, parts)


def first_kernel(
    n_scen, n_arc, rows_hbm, cols_hbm, tiles, dual_hbm, rhs_hbm, cost_hbm, primal_hbm,
    turned, slot_rows, slot_spots, sums, col_peak, gap, cost, primal, send, own_dual, own_rhs,
    ring, sems, seen, dual, rows, cols, cost_flat, primal_flat, more,
):
    count = tiles.shape[0]
    copies = col_peak.shape[0]
    scen_dev = cost_flat.shape[0]
    col_tiles = copies // scen_dev
    row_tiles = dual.shape[0]
    per_scen = row_tiles // scen_dev
    share = row_tiles // n_arc
    chunks = count // CHUNK
    me = lax.axis_index("arc")

    def fetch(chunk):
        slot = lax.rem(chunk, RING)
        return pltpu.make_async_copy(
            tiles.at[pl.ds(chunk * CHUNK, CHUNK)], ring.at[slot], sems.at[slot]
        )

    mine = pl.ds(me * share, share)
    others = [
        pltpu.make_async_copy(dual_hbm, dual, more.at[0]),
        pltpu.make_async_copy(dual_hbm.at[mine], own_dual, more.at[1]),
        pltpu.make_async_copy(rhs_hbm.at[mine], own_rhs, more.at[2]),
        pltpu.make_async_copy(rows_hbm, rows, more.at[3]),
        pltpu.make_async_copy(cols_hbm, cols, more.at[4]),
        pltpu.make_async_copy(cost_hbm, cost_flat, more.at[5]),
        pltpu.make_async_copy(primal_hbm, primal_flat, more.at[6]),
    ]
    for copy in others:
        copy.start()
    for chunk in range(RING - 1):
        fetch(chunk).start()

    col_peak[...] = jnp.zeros_like(col_peak)
    gap[...] = jnp.zeros_like(gap)
    @pl.loop(0, copies)
    def _(copy):
        seen[copy] = 0

    for copy in others:
        copy.wait()
    for s in range(scen_dev):
        for c in range(col_tiles):
            at, to = slice(c * TILE, (c + 1) * TILE), s * col_tiles + c
            cost[to : to + 1, :] = cost_flat[s : s + 1, at]
            primal[to : to + 1, :] = primal_flat[s : s + 1, at]

    def one(k, block):
        r = rows[k]
        owner = r // share
        spot = ((owner ^ me) % CORE * (n_arc // CORE) + owner // CORE) * share + r % share
        copy = r // per_scen * col_tiles + cols[k]
        nth = seen[copy]
        seen[copy] = nth + 1
        slot_rows[copy * PER_COPY + nth] = r
        slot_spots[copy * PER_COPY + nth] = spot
        here = pl.ds(copy, 1)
        col_peak[here, :] = jnp.maximum(col_peak[here, :], peak(block))
        picked = jnp.broadcast_to(dual[pl.ds(r, 1), :], (16, TILE)).astype(BF16)
        gap[here, :] += jnp.dot(picked, block, preferred_element_type=F32)[:1]
        block = jnp.transpose(block)
        turned[copy, :, pl.ds(pl.multiple_of(nth * TILE, TILE), TILE)] = block
        sums[0, pl.ds(spot, 1), :] = peak(block)
        values = jnp.broadcast_to(primal[here, :], (16, TILE)).astype(BF16)
        sums[1, pl.ds(spot, 1), :] = jnp.dot(values, block, preferred_element_type=F32)[:1]

    @pl.loop(0, chunks)
    def _(chunk):
        fetch(chunk).wait()

        @pl.when(chunk + RING - 1 < chunks)
        def _():
            fetch(chunk + RING - 1).start()

        slot = lax.rem(chunk, RING)
        for at in range(CHUNK):
            one(chunk * CHUNK + at, ring[slot, at])

    gap[...] = cost[...] - gap[...]
    scenarios = scen_dev * n_scen
    send[:col_tiles, :] = high(by_scen(col_peak, scen_dev))
    send[col_tiles : 2 * col_tiles, :] = add([g / scenarios for g in by_scen(gap, scen_dev)])
    send[2 * col_tiles :, :] = add([p / scenarios for p in by_scen(primal, scen_dev)])


def each_copy(copies, one):
    @pl.loop(0, copies // STEP)
    def _(step):
        for u in range(STEP):
            one(step * STEP + u)


def row_kernel(spots, turned, col_peak, design, shared, row_high, col_scale):
    copies = col_peak.shape[0]
    col_tiles = design.shape[0]
    is_design = design[...] == 1
    for s in range(copies // col_tiles):
        at = slice(s * col_tiles, (s + 1) * col_tiles)
        high_here = jnp.where(is_design, shared[:col_tiles, :], col_peak[at, :])
        col_scale[at, :] = 1.0 / jnp.sqrt(high_here)

    def one(copy):
        spread = jnp.transpose(jnp.broadcast_to(col_scale[pl.ds(copy, 1), :], (TILE, TILE)))
        for b in range(PER_COPY):
            block = jnp.abs(turned[copy, :, b * TILE : (b + 1) * TILE]).astype(F32)
            here = pl.ds(spots[copy * PER_COPY + b], 1)
            row_high[here, :] = jnp.max(block * spread, axis=0, keepdims=True)

    each_copy(copies, one)


def col_kernel(rows, turned, row_scale, col_scale, cost, design, own_row, own_rhs, col_peak, send):
    def one(copy):
        best = None
        for b in range(PER_COPY):
            scale = row_scale[pl.ds(rows[copy * PER_COPY + b], 1), :]
            part = jnp.abs(turned[copy, :, b * TILE : (b + 1) * TILE]).astype(F32) * scale
            best = part if best is None else jnp.maximum(best, part)
        here = pl.ds(copy, 1)
        top = jnp.max(jnp.transpose(best), axis=0, keepdims=True)
        col_peak[here, :] = col_scale[here, :] * top

    each_copy(turned.shape[0], one)
    col_tiles = design.shape[0]
    is_design = design[...] == 1
    scen_dev = col_peak.shape[0] // col_tiles
    peaks = by_scen(col_peak, scen_dev)
    send[:col_tiles, :] = high(peaks)
    scaled = [
        (jnp.where(is_design, scale, scale / jnp.sqrt(p)) * c) ** 2
        for scale, p, c in zip(by_scen(col_scale, scen_dev), peaks, by_scen(cost, scen_dev))
    ]
    send[col_tiles : 2 * col_tiles, :] = add(scaled)
    right = (own_row[...] * own_rhs[...]) ** 2
    send[2 * col_tiles :, :] = add([right[k : k + 8] for k in range(0, right.shape[0], 8)])


def lanes(terms):
    lane = lax.broadcasted_iota(jnp.int32, (1, TILE), 1)
    row = jnp.zeros((1, TILE), F32)
    for k, term in enumerate(terms):
        row = jnp.where(lane == k, jnp.sum(term, axis=1, keepdims=True), row)
    return row


def norm_kernel(shared, design, send):
    col_tiles = design.shape[0]
    squares = shared[col_tiles : 2 * col_tiles, :]
    squares = jnp.where(design[...] == 1, squares / shared[:col_tiles, :], squares)
    rows = [jnp.sum(t, axis=0, keepdims=True) for t in (squares, shared[2 * col_tiles :, :])]
    send[...] = jnp.broadcast_to(lanes(rows), send.shape)


def image_kernel(
    spots, turned, step_size, totals, col_peak, shared, col_scale, gap, means, primal, design,
    image, new_primal, scalars, step,
):
    col_tiles = design.shape[0]
    copies = gap.shape[0]
    is_design = design[...] == 1
    total = jnp.sum(totals[...], axis=0, keepdims=True)
    cost_total, rhs_total = total[:, :1], total[:, 1:2]
    omega = jnp.sqrt(cost_total + 1e-06) / jnp.sqrt(rhs_total + 1e-06)
    tau = step_size[:, :1] / omega
    mean_gap = means[col_tiles : 2 * col_tiles, :]
    mean_primal = means[2 * col_tiles :, :]
    moved = None
    for s in range(copies // col_tiles):
        at = slice(s * col_tiles, (s + 1) * col_tiles)
        top = jnp.where(is_design, shared[:col_tiles, :], col_peak[at, :])
        scale = col_scale[at, :] / jnp.sqrt(top)
        weight = tau * scale * scale
        here = primal[at, :]
        half = jnp.where(is_design, mean_primal, here) - weight * jnp.where(
            is_design, mean_gap, gap[at, :]
        )
        new = jnp.maximum(half, 0.0)
        step[at, :] = new - here
        square = ((new - here) / scale) ** 2
        moved = square if moved is None else moved + square
        for c in range(col_tiles):
            new_primal[s : s + 1, c * TILE : (c + 1) * TILE] = new[c : c + 1, :]
    scalars[:1, :] = jnp.broadcast_to(omega, (1, TILE))
    scalars[1:2, :] = jnp.sum(moved, axis=0, keepdims=True)

    def one(copy):
        values = jnp.broadcast_to(step[pl.ds(copy, 1), :], (16, TILE)).astype(BF16)
        out = jnp.dot(values, turned[copy], preferred_element_type=F32)
        for b in range(PER_COPY):
            here = pl.ds(spots[copy * PER_COPY + b], 1)
            image[here, :] = out[:1, b * TILE : (b + 1) * TILE]

    each_copy(copies, one)


def dual_kernel(step_size, scalars, images, old, own_row, own_rhs, dual, new_dual, send):
    omega = scalars[:1, :]
    sigma = step_size[...] * omega
    step_image = add([images[k] for k in range(images.shape[0])])
    scale = own_row[...]
    new = jnp.maximum(
        dual[...] + sigma * scale * scale * (own_rhs[...] - old[...] - 2.0 * step_image), 0.0
    )
    step = new - dual[...]
    new_dual[...] = new
    terms = (
        scalars[1:2, :],
        jnp.sum((step / scale) ** 2, axis=0, keepdims=True),
        jnp.sum(step * step_image, axis=0, keepdims=True),
    )
    send[...] = jnp.broadcast_to(lanes(terms), send.shape)


VMEM = pl.BlockSpec(memory_space=pltpu.VMEM)
SMEM = pl.BlockSpec(memory_space=pltpu.SMEM)
HBM = pl.BlockSpec(memory_space=pltpu.HBM)
LIMIT = 20 * 1024 * 1024


def f32(*shape):
    return jax.ShapeDtypeStruct(shape, F32)


def start(n_scen, n_arc, rows, cols, tiles, dual, rhs, cost, primal):
    copies = cost.size // TILE
    col_tiles = copies // cost.shape[0]
    share = dual.shape[0] // n_arc
    slots = jax.ShapeDtypeStruct(rows.shape, jnp.int32)
    wide = f32(copies, TILE)
    own = f32(share, TILE)
    return pl.pallas_call(
        functools.partial(first_kernel, n_scen, n_arc),
        out_shape=[
            pltpu.VMEM((copies, TILE, PER_COPY * TILE), BF16),
            slots,
            slots,
            f32(2, *dual.shape),
            wide,
            wide,
            wide,
            wide,
            f32(3 * col_tiles, TILE),
            own,
            own,
        ],
        in_specs=[HBM] * 7,
        out_specs=[VMEM, SMEM, SMEM] + [VMEM] * 8,
        scratch_shapes=[
            pltpu.VMEM((RING, CHUNK, TILE, TILE), BF16),
            pltpu.SemaphoreType.DMA((RING,)),
            pltpu.SMEM((copies,), jnp.int32),
            pltpu.VMEM(dual.shape, F32),
            pltpu.SMEM(rows.shape, jnp.int32),
            pltpu.SMEM(cols.shape, jnp.int32),
            pltpu.VMEM(cost.shape, F32),
            pltpu.VMEM(primal.shape, F32),
            pltpu.SemaphoreType.DMA((7,)),
        ],
        compiler_params=pltpu.CompilerParams(vmem_limit_bytes=LIMIT),
    )(
        *[
            pltpu.with_memory_space_constraint(a, pltpu.HBM)
            for a in (rows, cols, tiles, dual, rhs, cost, primal)
        ]
    )


def again(kernel, outs, scalars, turned, *vectors, scratch=()):
    specs = [SMEM] * len(scalars)
    if turned is not None:
        vectors = (pltpu.with_memory_space_constraint(turned, pltpu.VMEM), *vectors)
    return pl.pallas_call(
        kernel,
        out_shape=outs,
        in_specs=specs + [VMEM] * len(vectors),
        out_specs=[VMEM] * len(outs),
        scratch_shapes=scratch,
        compiler_params=pltpu.CompilerParams(vmem_limit_bytes=LIMIT),
        cost_estimate=pl.CostEstimate(
            flops=7 * 10**9 if turned is not None else 10**6, bytes_accessed=2**20, transcendentals=0
        ),
    )(*scalars, *vectors)


def swap_core(values):
    n = lax.axis_size("arc")
    return lax.ppermute(values, "arc", [(i, i ^ 1) for i in range(n)])


def exchange(values):
    n = lax.axis_size("arc")
    groups = [[*range(c, n, CORE)] for c in range(CORE)]
    return lax.all_to_all(values, "arc", 0, 0, axis_index_groups=groups, tiled=True)


def join_scen(values, tops):
    for pairs in ((1, 0, 3, 2), (3, 2, 1, 0)):
        other = lax.ppermute(values, "scen", [*enumerate(pairs)])
        values = jnp.concatenate(
            [jnp.maximum(values[:tops], other[:tops]), values[tops:] + other[tops:]]
        )
    return values


def per_device(tiles, tile_rows, tile_cols, design, cost, rhs, primal, dual, step_size):
    tile = tiles.shape[1]
    scen_dev, cols_dev = primal.shape
    col_tiles = cols_dev // tile
    row_tiles = dual.shape[0] // tile
    copies = scen_dev * col_tiles
    n_scen, n_arc = lax.axis_size("scen"), lax.axis_size("arc")
    share = row_tiles // n_arc
    chips = n_arc // CORE
    by_spot = (CORE, chips, share, tile)
    wide = f32(copies, tile)
    tall = f32(row_tiles, tile)
    own = f32(share, tile)
    design = design.reshape(col_tiles, tile)
    step_size, cost = lax.optimization_barrier((jnp.full((1, tile), step_size), cost))

    (
        turned, slot_rows, slot_spots, sums, col_peak, gap, cost, primal, send, own_dual, own_rhs
    ) = start(
        n_scen, n_arc, tile_rows, tile_cols, tiles,
        dual.reshape(row_tiles, tile), rhs.reshape(row_tiles, tile), cost, primal,
    )
    sums = sums.reshape(2, *by_spot)
    near = swap_core(sums[:, 1])
    means = join_scen(send, col_tiles)
    means, near = lax.optimization_barrier((means, near))

    row_high, col_scale = again(
        row_kernel, [tall, wide], [slot_spots], turned, col_peak, design, means
    )
    row_high = row_high.reshape(by_spot)
    near_high = swap_core(row_high[1])
    got = exchange(
        jnp.stack(
            (
                jnp.maximum(sums[0, 0], near[0]),
                sums[1, 0] + near[1],
                jnp.maximum(row_high[0], near_high),
            ),
            axis=1,
        )
    )
    own_scale = 1.0 / jnp.sqrt(high([*got[:, 0]]))
    old_image = add([*got[:, 1]])
    own_row = own_scale / jnp.sqrt(own_scale * high([*got[:, 2]]))
    own_scale, own_row, old_image = lax.optimization_barrier((own_scale, own_row, old_image))
    row_scale = lax.all_to_all(
        jnp.broadcast_to(own_scale[None], (n_arc, share, tile)), "arc", 0, 0, tiled=True
    ).reshape(row_tiles, tile)

    col_peak, send = again(
        col_kernel, [wide, f32(2 * col_tiles + 8, tile)], [slot_rows],
        turned, row_scale, col_scale, cost, design, own_row, own_rhs,
    )
    shared = join_scen(send, col_tiles)
    (send,) = again(norm_kernel, [f32(n_arc, tile)], [], None, shared, design)
    totals = lax.all_to_all(send, "arc", 0, 0, tiled=True)

    image, new_primal, scalars = again(
        image_kernel, [tall, f32(scen_dev, cols_dev), f32(8, tile)], [slot_spots],
        turned, step_size, totals, col_peak, shared, col_scale, gap, means, primal, design,
        scratch=[pltpu.VMEM((copies, tile), F32)],
    )
    image = image.reshape(by_spot)
    images = exchange(image[0] + swap_core(image[1]))
    new_dual, send = again(
        dual_kernel, [own, f32(n_scen * n_arc, tile)], [], None,
        step_size, scalars, images, old_image, own_row, own_rhs, own_dual,
    )
    sums = jnp.sum(lax.all_to_all(send, ("scen", "arc"), 0, 0, tiled=True), axis=0)
    omega = scalars[0, 0]
    movement = omega * sums[0] + sums[1] / omega
    return (new_primal, new_dual.reshape(share * tile), movement, sums[2])


def solution(mesh):
    placed = (
        P(("scen", "arc"), None, None),
        P(("scen", "arc")),
        P(("scen", "arc")),
        P("arc"),
        P("scen", "arc"),
        P("scen"),
        P("scen", "arc"),
        P("scen"),
        P(),
    )
    return jax.shard_map(
        per_device,
        mesh=mesh,
        in_specs=placed,
        out_specs=(P("scen", "arc"), P(("scen", "arc")), P(), P()),
        check_vma=False,
    )
```

```python
import functools

import jax
import jax.numpy as jnp
from jax import lax
from jax.experimental import pallas as pl
from jax.experimental.pallas import tpu as pltpu
from jax.sharding import PartitionSpec as P

TILE = 128
PER_COPY = 4
CHUNK = 64
RING = 3
STEP = 32
CORE = 2
F32 = jnp.float32
BF16 = jnp.bfloat16


def peak(block):
    parts = [jnp.abs(block[k : k + 16]) for k in range(0, block.shape[0], 16)]
    while len(parts) > 1:
        parts = [jnp.maximum(a, b) for a, b in zip(parts[::2], parts[1::2])]
    return jnp.max(parts[0].astype(F32), axis=0, keepdims=True)


def bits(size):
    assert size & (size - 1) == 0
    return size.bit_length() - 1


def by_scen(ref, scen_dev):
    size = ref.shape[0] // scen_dev
    return [ref[k * size : (k + 1) * size, :] for k in range(scen_dev)]


def add(parts):
    return functools.reduce(jnp.add, parts)


def high(parts):
    return functools.reduce(jnp.maximum, parts)


def first_kernel(
    n_scen, n_arc, rows_hbm, cols_hbm, tiles, dual_hbm, rhs_hbm, cost_hbm, primal_hbm,
    turned, slot_rows, slot_spots, sums, col_peak, gap, cost, primal, send, own_dual, own_rhs,
    ring, sems, seen, dual, rows, cols, cost_flat, primal_flat, more,
):
    count = tiles.shape[0]
    copies = col_peak.shape[0]
    scen_dev = cost_flat.shape[0]
    col_tiles = copies // scen_dev
    row_tiles = dual.shape[0]
    per_scen = row_tiles // scen_dev
    share = row_tiles // n_arc
    chunks = count // CHUNK
    me = lax.axis_index("arc")

    def fetch(chunk):
        slot = lax.rem(chunk, RING)
        return pltpu.make_async_copy(
            tiles.at[pl.ds(chunk * CHUNK, CHUNK)], ring.at[slot], sems.at[slot]
        )

    mine = pl.ds(me * share, share)
    others = [
        pltpu.make_async_copy(dual_hbm, dual, more.at[0]),
        pltpu.make_async_copy(dual_hbm.at[mine], own_dual, more.at[1]),
        pltpu.make_async_copy(rhs_hbm.at[mine], own_rhs, more.at[2]),
        pltpu.make_async_copy(rows_hbm, rows, more.at[3]),
        pltpu.make_async_copy(cols_hbm, cols, more.at[4]),
        pltpu.make_async_copy(cost_hbm, cost_flat, more.at[5]),
        pltpu.make_async_copy(primal_hbm, primal_flat, more.at[6]),
    ]
    for copy in others:
        copy.start()
    for chunk in range(RING - 1):
        fetch(chunk).start()

    col_peak[...] = jnp.zeros_like(col_peak)
    gap[...] = jnp.zeros_like(gap)
    @pl.loop(0, copies)
    def _(copy):
        seen[copy] = 0

    for copy in others:
        copy.wait()
    for s in range(scen_dev):
        for c in range(col_tiles):
            at, to = slice(c * TILE, (c + 1) * TILE), s * col_tiles + c
            cost[to : to + 1, :] = cost_flat[s : s + 1, at]
            primal[to : to + 1, :] = primal_flat[s : s + 1, at]

    def one(k, block):
        r = rows[k]
        owner = r >> bits(share)
        spot = ((owner ^ me) & 1) * (row_tiles // CORE)
        spot = spot + ((owner >> 1) << bits(share)) + (r & (share - 1))
        copy = ((r >> bits(per_scen)) << bits(col_tiles)) + cols[k]
        nth = seen[copy]
        seen[copy] = nth + 1
        slot_rows[copy * PER_COPY + nth] = r
        slot_spots[copy * PER_COPY + nth] = spot
        here = pl.ds(copy, 1)
        col_peak[here, :] = jnp.maximum(col_peak[here, :], peak(block))
        picked = jnp.broadcast_to(dual[pl.ds(r, 1), :], (16, TILE)).astype(BF16)
        gap[here, :] += jnp.dot(picked, block, preferred_element_type=F32)[:1]
        block = jnp.transpose(block)
        turned[copy, :, pl.ds(pl.multiple_of(nth * TILE, TILE), TILE)] = block
        sums[0, pl.ds(spot, 1), :] = peak(block)
        values = jnp.broadcast_to(primal[here, :], (16, TILE)).astype(BF16)
        sums[1, pl.ds(spot, 1), :] = jnp.dot(values, block, preferred_element_type=F32)[:1]

    @pl.loop(0, chunks)
    def _(chunk):
        fetch(chunk).wait()

        @pl.when(chunk + RING - 1 < chunks)
        def _():
            fetch(chunk + RING - 1).start()

        slot = lax.rem(chunk, RING)
        for at in range(CHUNK):
            one(chunk * CHUNK + at, ring[slot, at])

    gap[...] = cost[...] - gap[...]
    scenarios = scen_dev * n_scen
    send[:col_tiles, :] = high(by_scen(col_peak, scen_dev))
    send[col_tiles : 2 * col_tiles, :] = add([g / scenarios for g in by_scen(gap, scen_dev)])
    send[2 * col_tiles :, :] = add([p / scenarios for p in by_scen(primal, scen_dev)])


def each_copy(copies, one):
    @pl.loop(0, copies // STEP)
    def _(step):
        for u in range(STEP):
            one(step * STEP + u)


def joined(parts, rows, tops):
    join = lambda f: f(f(parts[0][rows, :], parts[2][rows, :]), f(parts[1][rows, :], parts[3][rows, :]))
    return join(jnp.maximum if rows.stop <= tops else jnp.add)


def row_kernel(
    rows, turned, reduced, col_peak, design, own, first, second, third,
    send, own_scale, old, col_scale, means,
):
    copies = col_peak.shape[0]
    col_tiles = design.shape[0]
    share = own_scale.shape[0]
    chips = reduced.shape[0] // (2 * share)
    pieces = [reduced[k * share : (k + 1) * share, :] for k in range(2 * chips)]
    scale = 1.0 / jnp.sqrt(high(pieces[::2]))
    own_scale[...] = scale
    old[...] = add(pieces[1::2])
    for k in range(send.shape[0] // (2 * share)):
        send[2 * k * share : (2 * k + 1) * share, :] = scale
    parts = (own, first, second, third)
    shared = joined(parts, slice(0, col_tiles), col_tiles)
    for k in range(2):
        at = slice((k + 1) * col_tiles, (k + 2) * col_tiles)
        means[k * col_tiles : (k + 1) * col_tiles, :] = joined(parts, at, col_tiles)
    is_design = design[...] == 1
    for s in range(copies // col_tiles):
        at = slice(s * col_tiles, (s + 1) * col_tiles)
        col_scale[at, :] = 1.0 / jnp.sqrt(jnp.where(is_design, shared, col_peak[at, :]))

    def one(copy):
        spread = jnp.transpose(jnp.broadcast_to(col_scale[pl.ds(copy, 1), :], (TILE, TILE)))
        for b in range(PER_COPY):
            block = jnp.abs(turned[copy, :, b * TILE : (b + 1) * TILE].astype(F32))
            r = rows[copy * PER_COPY + b]
            at = ((r >> bits(share)) << bits(2 * share)) + share + (r & (share - 1))
            send[pl.ds(at, 1), :] = jnp.max(block * spread, axis=0, keepdims=True)

    each_copy(copies, one)


def col_kernel(
    rows, turned, gathered, own_scale, own_rhs, col_scale, cost, design, col_peak, send, own_row
):
    share = own_scale.shape[0]

    def one(copy):
        best = None
        for b in range(PER_COPY):
            r = rows[copy * PER_COPY + b]
            at = ((r >> bits(share)) << bits(2 * share)) + (r & (share - 1))
            scale = gathered[pl.ds(at, 1), :]
            part = jnp.abs(turned[copy, :, b * TILE : (b + 1) * TILE].astype(F32)) * scale
            best = part if best is None else jnp.maximum(best, part)
        here = pl.ds(copy, 1)
        top = jnp.max(jnp.transpose(best), axis=0, keepdims=True)
        col_peak[here, :] = col_scale[here, :] * top

    each_copy(turned.shape[0], one)
    devices = gathered.shape[0] // (2 * share)
    highs = [gathered[(2 * k + 1) * share : (2 * k + 2) * share, :] for k in range(devices)]
    scale = own_scale[...]
    scale = scale / jnp.sqrt(scale * high(highs))
    own_row[...] = scale
    col_tiles = design.shape[0]
    is_design = design[...] == 1
    scen_dev = col_peak.shape[0] // col_tiles
    peaks = by_scen(col_peak, scen_dev)
    send[:col_tiles, :] = high(peaks)
    scaled = [
        (jnp.where(is_design, scale, scale / jnp.sqrt(p)) * c) ** 2
        for scale, p, c in zip(by_scen(col_scale, scen_dev), peaks, by_scen(cost, scen_dev))
    ]
    send[col_tiles : 2 * col_tiles, :] = add(scaled)
    right = (scale * own_rhs[...]) ** 2
    send[2 * col_tiles :, :] = add([right[k : k + 8] for k in range(0, share, 8)])


def lanes(terms):
    lane = lax.broadcasted_iota(jnp.int32, (1, TILE), 1)
    row = jnp.zeros((1, TILE), F32)
    for k, term in enumerate(terms):
        row = jnp.where(lane == k, jnp.sum(term, axis=1, keepdims=True), row)
    return row


def norm_kernel(design, own, first, second, third, shared, send):
    col_tiles = design.shape[0]
    parts = (own, first, second, third)
    tops = joined(parts, slice(0, col_tiles), col_tiles)
    shared[...] = tops
    squares = joined(parts, slice(col_tiles, 2 * col_tiles), col_tiles)
    squares = jnp.where(design[...] == 1, squares / tops, squares)
    right = joined(parts, slice(2 * col_tiles, 2 * col_tiles + 8), col_tiles)
    rows = [jnp.sum(t, axis=0, keepdims=True) for t in (squares, right)]
    send[...] = jnp.broadcast_to(lanes(rows), send.shape)


def image_kernel(
    spots, turned, step_size, totals, col_peak, shared, col_scale, gap, means, primal, design,
    image, new_primal, scalars, step,
):
    col_tiles = design.shape[0]
    copies = gap.shape[0]
    is_design = design[...] == 1
    total = jnp.sum(totals[...], axis=0, keepdims=True)
    cost_total, rhs_total = total[:, :1], total[:, 1:2]
    omega = jnp.sqrt(cost_total + 1e-06) / jnp.sqrt(rhs_total + 1e-06)
    tau = step_size[:, :1] / omega
    mean_gap = means[:col_tiles, :]
    mean_primal = means[col_tiles:, :]
    moved = None
    for s in range(copies // col_tiles):
        at = slice(s * col_tiles, (s + 1) * col_tiles)
        top = jnp.where(is_design, shared[...], col_peak[at, :])
        scale = col_scale[at, :] / jnp.sqrt(top)
        weight = tau * scale * scale
        here = primal[at, :]
        half = jnp.where(is_design, mean_primal, here) - weight * jnp.where(
            is_design, mean_gap, gap[at, :]
        )
        new = jnp.maximum(half, 0.0)
        step[at, :] = new - here
        square = ((new - here) / scale) ** 2
        moved = square if moved is None else moved + square
        for c in range(col_tiles):
            new_primal[s : s + 1, c * TILE : (c + 1) * TILE] = new[c : c + 1, :]
    scalars[:1, :] = jnp.broadcast_to(omega, (1, TILE))
    scalars[1:2, :] = jnp.sum(moved, axis=0, keepdims=True)

    def one(copy):
        values = jnp.broadcast_to(step[pl.ds(copy, 1), :], (16, TILE)).astype(BF16)
        out = jnp.dot(values, turned[copy], preferred_element_type=F32)
        for b in range(PER_COPY):
            here = pl.ds(spots[copy * PER_COPY + b], 1)
            image[here, :] = out[:1, b * TILE : (b + 1) * TILE]

    each_copy(copies, one)


def dual_kernel(step_size, scalars, images, old, own_row, own_rhs, dual, new_dual, send):
    omega = scalars[:1, :]
    sigma = step_size[...] * omega
    step_image = add([images[k] for k in range(images.shape[0])])
    scale = own_row[...]
    new = jnp.maximum(
        dual[...] + sigma * scale * scale * (own_rhs[...] - old[...] - 2.0 * step_image), 0.0
    )
    step = new - dual[...]
    new_dual[...] = new
    terms = (
        scalars[1:2, :],
        jnp.sum((step / scale) ** 2, axis=0, keepdims=True),
        jnp.sum(step * step_image, axis=0, keepdims=True),
    )
    send[...] = jnp.broadcast_to(lanes(terms), send.shape)


VMEM = pl.BlockSpec(memory_space=pltpu.VMEM)
SMEM = pl.BlockSpec(memory_space=pltpu.SMEM)
HBM = pl.BlockSpec(memory_space=pltpu.HBM)
LIMIT = 20 * 1024 * 1024


def f32(*shape):
    return jax.ShapeDtypeStruct(shape, F32)


def start(n_scen, n_arc, rows, cols, tiles, dual, rhs, cost, primal):
    copies = cost.size // TILE
    col_tiles = copies // cost.shape[0]
    share = dual.shape[0] // n_arc
    slots = jax.ShapeDtypeStruct(rows.shape, jnp.int32)
    wide = f32(copies, TILE)
    own = f32(share, TILE)
    return pl.pallas_call(
        functools.partial(first_kernel, n_scen, n_arc),
        out_shape=[
            pltpu.VMEM((copies, TILE, PER_COPY * TILE), BF16),
            slots,
            slots,
            f32(2, *dual.shape),
            wide,
            wide,
            wide,
            wide,
            f32(3 * col_tiles, TILE),
            own,
            own,
        ],
        in_specs=[HBM] * 7,
        out_specs=[VMEM, SMEM, SMEM] + [VMEM] * 8,
        scratch_shapes=[
            pltpu.VMEM((RING, CHUNK, TILE, TILE), BF16),
            pltpu.SemaphoreType.DMA((RING,)),
            pltpu.SMEM((copies,), jnp.int32),
            pltpu.VMEM(dual.shape, F32),
            pltpu.SMEM(rows.shape, jnp.int32),
            pltpu.SMEM(cols.shape, jnp.int32),
            pltpu.VMEM(cost.shape, F32),
            pltpu.VMEM(primal.shape, F32),
            pltpu.SemaphoreType.DMA((7,)),
        ],
        compiler_params=pltpu.CompilerParams(vmem_limit_bytes=LIMIT),
    )(
        *[
            pltpu.with_memory_space_constraint(a, pltpu.HBM)
            for a in (rows, cols, tiles, dual, rhs, cost, primal)
        ]
    )


def again(kernel, outs, scalars, turned, *vectors, scratch=()):
    specs = [SMEM] * len(scalars)
    if turned is not None:
        vectors = (pltpu.with_memory_space_constraint(turned, pltpu.VMEM), *vectors)
    return pl.pallas_call(
        kernel,
        out_shape=outs,
        in_specs=specs + [VMEM] * len(vectors),
        out_specs=[VMEM] * len(outs),
        scratch_shapes=scratch,
        compiler_params=pltpu.CompilerParams(vmem_limit_bytes=LIMIT),
        cost_estimate=pl.CostEstimate(
            flops=7 * 10**9 if turned is not None else 10**6, bytes_accessed=2**20, transcendentals=0
        ),
    )(*scalars, *vectors)


def swap_core(values):
    n = lax.axis_size("arc")
    return lax.ppermute(values, "arc", [(i, i ^ 1) for i in range(n)])


def exchange(values):
    n = lax.axis_size("arc")
    groups = [[*range(c, n, CORE)] for c in range(CORE)]
    return lax.all_to_all(values, "arc", 0, 0, axis_index_groups=groups, tiled=True)


def with_scen(values):
    n = lax.axis_size("scen")
    shifts = [[(i, (i - k) % n) for i in range(n)] for k in range(1, n)]
    return [values] + [lax.ppermute(values, "scen", pairs) for pairs in shifts]


def per_device(tiles, tile_rows, tile_cols, design, cost, rhs, primal, dual, step_size):
    tile = tiles.shape[1]
    scen_dev, cols_dev = primal.shape
    col_tiles = cols_dev // tile
    row_tiles = dual.shape[0] // tile
    copies = scen_dev * col_tiles
    n_scen, n_arc = lax.axis_size("scen"), lax.axis_size("arc")
    share = row_tiles // n_arc
    chips = n_arc // CORE
    by_spot = (CORE, chips, share, tile)
    wide = f32(copies, tile)
    tall = f32(row_tiles, tile)
    own = f32(share, tile)
    design = design.reshape(col_tiles, tile)
    step_size, cost = lax.optimization_barrier((jnp.full((1, tile), step_size), cost))

    (
        turned, slot_rows, slot_spots, sums, col_peak, gap, cost, primal, send, own_dual, own_rhs
    ) = start(
        n_scen, n_arc, tile_rows, tile_cols, tiles,
        dual.reshape(row_tiles, tile), rhs.reshape(row_tiles, tile), cost, primal,
    )
    sends = with_scen(send)
    sums = sums.reshape(2, *by_spot)
    near, sends = lax.optimization_barrier((swap_core(sums[:, 1]), sends))
    reduced = exchange(
        jnp.stack((jnp.maximum(sums[0, 0], near[0]), sums[1, 0] + near[1]), axis=1)
    )
    send, own_scale, old_image, col_scale, means = again(
        row_kernel, [f32(2 * row_tiles, tile), own, own, wide, f32(2 * col_tiles, tile)],
        [slot_rows], turned, reduced.reshape(row_tiles, tile), col_peak, design, *sends,
    )
    gathered = lax.all_to_all(
        send.reshape(n_arc, 2, share, tile), "arc", 0, 0, tiled=True
    ).reshape(2 * row_tiles, tile)
    col_peak, send, own_row = again(
        col_kernel, [wide, f32(2 * col_tiles + 8, tile), own], [slot_rows],
        turned, gathered, own_scale, own_rhs, col_scale, cost, design,
    )
    shared, send = again(
        norm_kernel, [f32(col_tiles, tile), f32(n_arc, tile)], [], None, design, *with_scen(send)
    )
    totals = lax.all_to_all(send, "arc", 0, 0, tiled=True)

    image, new_primal, scalars = again(
        image_kernel, [tall, f32(scen_dev, cols_dev), f32(8, tile)], [slot_spots],
        turned, step_size, totals, col_peak, shared, col_scale, gap, means, primal, design,
        scratch=[pltpu.VMEM((copies, tile), F32)],
    )
    image = image.reshape(by_spot)
    images = exchange(image[0] + swap_core(image[1]))
    new_dual, send = again(
        dual_kernel, [own, f32(n_scen * n_arc, tile)], [], None,
        step_size, scalars, images, old_image, own_row, own_rhs, own_dual,
    )
    sums = jnp.sum(lax.all_to_all(send, ("scen", "arc"), 0, 0, tiled=True), axis=0)
    omega = scalars[0, 0]
    movement = omega * sums[0] + sums[1] / omega
    return (new_primal, new_dual.reshape(share * tile), movement, sums[2])


def solution(mesh):
    placed = (
        P(("scen", "arc"), None, None),
        P(("scen", "arc")),
        P(("scen", "arc")),
        P("arc"),
        P("scen", "arc"),
        P("scen"),
        P("scen", "arc"),
        P("scen"),
        P(),
    )
    return jax.shard_map(
        per_device,
        mesh=mesh,
        in_specs=placed,
        out_specs=(P("scen", "arc"), P(("scen", "arc")), P(), P()),
        check_vma=False,
    )
```

```python
import functools

import jax
import jax.numpy as jnp
from jax import lax
from jax.experimental import pallas as pl
from jax.experimental.pallas import tpu as pltpu
from jax.sharding import PartitionSpec as P

TILE = 128
PER_COPY = 4
CHUNK = 64
RING = 3
STEP = 32
CORE = 2
F32 = jnp.float32
BF16 = jnp.bfloat16


def peak(block):
    parts = [jnp.abs(block[k : k + 16]) for k in range(0, block.shape[0], 16)]
    while len(parts) > 1:
        parts = [jnp.maximum(a, b) for a, b in zip(parts[::2], parts[1::2])]
    return jnp.max(parts[0].astype(F32), axis=0, keepdims=True)


def bits(size):
    assert size & (size - 1) == 0
    return size.bit_length() - 1


def pieces_of(ref, share):
    return [ref[k : k + share, :] for k in range(0, ref.shape[0], share)]


def by_scen(ref, scen_dev):
    size = ref.shape[0] // scen_dev
    return [ref[k * size : (k + 1) * size, :] for k in range(scen_dev)]


def add(parts):
    return functools.reduce(jnp.add, parts)


def high(parts):
    return functools.reduce(jnp.maximum, parts)


def split_cores(rows, keep, give, share, me, part=0, parts=1):
    for chip in range(rows.shape[0] // (CORE * share)):
        to = (chip * parts + part) * share
        for ref, core in ((keep, me & 1), (give, 1 - (me & 1))):
            start = pl.multiple_of((chip * CORE + core) * share, share)
            ref[to : to + share, :] = rows[pl.ds(start, share), :]


def first_kernel(
    n_scen, n_arc, rows_hbm, cols_hbm, tiles, dual_hbm, rhs_hbm, cost_hbm, primal_hbm,
    turned, slot_rows, keep, give, col_peak, gap, cost, primal, send, own_dual, own_rhs,
    ring, sems, seen, row_peak, dual, rows, cols, cost_flat, primal_flat, more,
):
    count = tiles.shape[0]
    copies = col_peak.shape[0]
    scen_dev = cost_flat.shape[0]
    col_tiles = copies // scen_dev
    row_tiles = dual.shape[0]
    per_scen = row_tiles // scen_dev
    share = row_tiles // n_arc
    chunks = count // CHUNK
    me = lax.axis_index("arc")

    def fetch(chunk):
        slot = lax.rem(chunk, RING)
        return pltpu.make_async_copy(
            tiles.at[pl.ds(chunk * CHUNK, CHUNK)], ring.at[slot], sems.at[slot]
        )

    mine = pl.ds(me * share, share)
    others = [
        pltpu.make_async_copy(dual_hbm, dual, more.at[0]),
        pltpu.make_async_copy(dual_hbm.at[mine], own_dual, more.at[1]),
        pltpu.make_async_copy(rhs_hbm.at[mine], own_rhs, more.at[2]),
        pltpu.make_async_copy(rows_hbm, rows, more.at[3]),
        pltpu.make_async_copy(cols_hbm, cols, more.at[4]),
        pltpu.make_async_copy(cost_hbm, cost_flat, more.at[5]),
        pltpu.make_async_copy(primal_hbm, primal_flat, more.at[6]),
    ]
    for copy in others:
        copy.start()
    for chunk in range(RING - 1):
        fetch(chunk).start()

    col_peak[...] = jnp.zeros_like(col_peak)
    gap[...] = jnp.zeros_like(gap)
    @pl.loop(0, copies)
    def _(copy):
        seen[copy] = 0

    for copy in others:
        copy.wait()
    for s in range(scen_dev):
        for c in range(col_tiles):
            at, to = slice(c * TILE, (c + 1) * TILE), s * col_tiles + c
            cost[to : to + 1, :] = cost_flat[s : s + 1, at]
            primal[to : to + 1, :] = primal_flat[s : s + 1, at]

    def one(k, block):
        r = rows[k]
        copy = ((r >> bits(per_scen)) << bits(col_tiles)) + cols[k]
        nth = seen[copy]
        seen[copy] = nth + 1
        slot_rows[copy * PER_COPY + nth] = r
        here = pl.ds(copy, 1)
        col_peak[here, :] = jnp.maximum(col_peak[here, :], peak(block))
        picked = jnp.broadcast_to(dual[pl.ds(r, 1), :], (16, TILE)).astype(BF16)
        gap[here, :] += jnp.dot(picked, block, preferred_element_type=F32)[:1]
        block = jnp.transpose(block)
        turned[copy, :, pl.ds(pl.multiple_of(nth * TILE, TILE), TILE)] = block
        row_peak[pl.ds(r, 1), :] = peak(block)

    @pl.loop(0, chunks)
    def _(chunk):
        fetch(chunk).wait()

        @pl.when(chunk + RING - 1 < chunks)
        def _():
            fetch(chunk + RING - 1).start()

        slot = lax.rem(chunk, RING)
        for at in range(CHUNK):
            one(chunk * CHUNK + at, ring[slot, at])

    split_cores(row_peak, keep, give, share, me)
    gap[...] = cost[...] - gap[...]
    scenarios = scen_dev * n_scen
    send[:col_tiles, :] = high(by_scen(col_peak, scen_dev))
    send[col_tiles : 2 * col_tiles, :] = add([g / scenarios for g in by_scen(gap, scen_dev)])
    send[2 * col_tiles :, :] = add([p / scenarios for p in by_scen(primal, scen_dev)])


def each_copy(copies, one):
    @pl.loop(0, copies // STEP)
    def _(step):
        for u in range(STEP):
            one(step * STEP + u)


def joined(parts, rows, tops):
    join = lambda f: f(f(parts[0][rows, :], parts[2][rows, :]), f(parts[1][rows, :], parts[3][rows, :]))
    return join(jnp.maximum if rows.stop <= tops else jnp.add)


def row_kernel(
    rows, turned, reduced, col_peak, design, own, first, second, third,
    send, own_scale, col_scale, means,
):
    copies = col_peak.shape[0]
    col_tiles = design.shape[0]
    share = own_scale.shape[0]
    scale = 1.0 / jnp.sqrt(high(pieces_of(reduced, share)))
    own_scale[...] = scale
    for k in range(send.shape[0] // (2 * share)):
        send[2 * k * share : (2 * k + 1) * share, :] = scale
    parts = (own, first, second, third)
    shared = joined(parts, slice(0, col_tiles), col_tiles)
    for k in range(2):
        at = slice((k + 1) * col_tiles, (k + 2) * col_tiles)
        means[k * col_tiles : (k + 1) * col_tiles, :] = joined(parts, at, col_tiles)
    is_design = design[...] == 1
    for s in range(copies // col_tiles):
        at = slice(s * col_tiles, (s + 1) * col_tiles)
        col_scale[at, :] = 1.0 / jnp.sqrt(jnp.where(is_design, shared, col_peak[at, :]))

    def one(copy):
        spread = jnp.transpose(jnp.broadcast_to(col_scale[pl.ds(copy, 1), :], (TILE, TILE)))
        for b in range(PER_COPY):
            block = jnp.abs(turned[copy, :, b * TILE : (b + 1) * TILE].astype(F32))
            r = rows[copy * PER_COPY + b]
            at = ((r >> bits(share)) << bits(2 * share)) + share + (r & (share - 1))
            send[pl.ds(at, 1), :] = jnp.max(block * spread, axis=0, keepdims=True)

    each_copy(copies, one)


def col_kernel(
    rows, turned, gathered, own_scale, own_rhs, col_scale, cost, design, col_peak, send, own_row
):
    share = own_scale.shape[0]

    def one(copy):
        best = None
        for b in range(PER_COPY):
            r = rows[copy * PER_COPY + b]
            at = ((r >> bits(share)) << bits(2 * share)) + (r & (share - 1))
            scale = gathered[pl.ds(at, 1), :]
            part = jnp.abs(turned[copy, :, b * TILE : (b + 1) * TILE].astype(F32)) * scale
            best = part if best is None else jnp.maximum(best, part)
        here = pl.ds(copy, 1)
        top = jnp.max(jnp.transpose(best), axis=0, keepdims=True)
        col_peak[here, :] = col_scale[here, :] * top

    each_copy(turned.shape[0], one)
    scale = own_scale[...]
    scale = scale / jnp.sqrt(scale * high(pieces_of(gathered, share)[1::2]))
    own_row[...] = scale
    col_tiles = design.shape[0]
    is_design = design[...] == 1
    scen_dev = col_peak.shape[0] // col_tiles
    peaks = by_scen(col_peak, scen_dev)
    send[:col_tiles, :] = high(peaks)
    scaled = [
        (jnp.where(is_design, scale, scale / jnp.sqrt(p)) * c) ** 2
        for scale, p, c in zip(by_scen(col_scale, scen_dev), peaks, by_scen(cost, scen_dev))
    ]
    send[col_tiles : 2 * col_tiles, :] = add(scaled)
    right = (scale * own_rhs[...]) ** 2
    send[2 * col_tiles :, :] = add([right[k : k + 8] for k in range(0, share, 8)])


def lanes(terms):
    lane = lax.broadcasted_iota(jnp.int32, (1, TILE), 1)
    row = jnp.zeros((1, TILE), F32)
    for k, term in enumerate(terms):
        row = jnp.where(lane == k, jnp.sum(term, axis=1, keepdims=True), row)
    return row


def norm_kernel(design, own, first, second, third, shared, send):
    col_tiles = design.shape[0]
    parts = (own, first, second, third)
    tops = joined(parts, slice(0, col_tiles), col_tiles)
    shared[...] = tops
    squares = joined(parts, slice(col_tiles, 2 * col_tiles), col_tiles)
    squares = jnp.where(design[...] == 1, squares / tops, squares)
    right = joined(parts, slice(2 * col_tiles, 2 * col_tiles + 8), col_tiles)
    rows = [jnp.sum(t, axis=0, keepdims=True) for t in (squares, right)]
    send[...] = jnp.broadcast_to(lanes(rows), send.shape)


def image_kernel(
    share, rows, turned, step_size, totals, col_peak, shared, col_scale, gap, means, primal, design,
    keep, give, new_primal, scalars, step, image, old,
):
    col_tiles = design.shape[0]
    copies = gap.shape[0]
    is_design = design[...] == 1
    total = jnp.sum(totals[...], axis=0, keepdims=True)
    cost_total, rhs_total = total[:, :1], total[:, 1:2]
    omega = jnp.sqrt(cost_total + 1e-06) / jnp.sqrt(rhs_total + 1e-06)
    tau = step_size[:, :1] / omega
    mean_gap = means[:col_tiles, :]
    mean_primal = means[col_tiles:, :]
    moved = None
    for s in range(copies // col_tiles):
        at = slice(s * col_tiles, (s + 1) * col_tiles)
        top = jnp.where(is_design, shared[...], col_peak[at, :])
        scale = col_scale[at, :] / jnp.sqrt(top)
        weight = tau * scale * scale
        here = primal[at, :]
        half = jnp.where(is_design, mean_primal, here) - weight * jnp.where(
            is_design, mean_gap, gap[at, :]
        )
        new = jnp.maximum(half, 0.0)
        step[at, :] = new - here
        square = ((new - here) / scale) ** 2
        moved = square if moved is None else moved + square
        for c in range(col_tiles):
            new_primal[s : s + 1, c * TILE : (c + 1) * TILE] = new[c : c + 1, :]
    scalars[:1, :] = jnp.broadcast_to(omega, (1, TILE))
    scalars[1:2, :] = jnp.sum(moved, axis=0, keepdims=True)

    def one(copy):
        here = pl.ds(copy, 1)
        values = [jnp.broadcast_to(v[here, :], (8, TILE)) for v in (step, primal)]
        values = jnp.concatenate(values, axis=0).astype(BF16)
        out = jnp.dot(values, turned[copy], preferred_element_type=F32)
        for b in range(PER_COPY):
            here, at = pl.ds(rows[copy * PER_COPY + b], 1), slice(b * TILE, (b + 1) * TILE)
            image[here, :] = out[:1, at]
            old[here, :] = out[8:9, at]

    each_copy(copies, one)
    me = lax.axis_index("arc")
    split_cores(image, keep, give, share, me, 0, 2)
    split_cores(old, keep, give, share, me, 1, 2)


def dual_kernel(step_size, scalars, images, own_row, own_rhs, dual, new_dual, send):
    omega = scalars[:1, :]
    sigma = step_size[...] * omega
    scale = own_row[...]
    pieces = pieces_of(images, scale.shape[0])
    step_image, old = add(pieces[::2]), add(pieces[1::2])
    new = jnp.maximum(
        dual[...] + sigma * scale * scale * (own_rhs[...] - old - 2.0 * step_image), 0.0
    )
    step = new - dual[...]
    new_dual[...] = new
    terms = (
        scalars[1:2, :],
        jnp.sum((step / scale) ** 2, axis=0, keepdims=True),
        jnp.sum(step * step_image, axis=0, keepdims=True),
    )
    send[...] = jnp.broadcast_to(lanes(terms), send.shape)


VMEM = pl.BlockSpec(memory_space=pltpu.VMEM)
SMEM = pl.BlockSpec(memory_space=pltpu.SMEM)
HBM = pl.BlockSpec(memory_space=pltpu.HBM)
LIMIT = 20 * 1024 * 1024


def f32(*shape):
    return jax.ShapeDtypeStruct(shape, F32)


def start(n_scen, n_arc, rows, cols, tiles, dual, rhs, cost, primal):
    copies = cost.size // TILE
    col_tiles = copies // cost.shape[0]
    share = dual.shape[0] // n_arc
    slots = jax.ShapeDtypeStruct(rows.shape, jnp.int32)
    wide = f32(copies, TILE)
    own = f32(share, TILE)
    half = f32(dual.shape[0] // CORE, TILE)
    return pl.pallas_call(
        functools.partial(first_kernel, n_scen, n_arc),
        out_shape=[
            pltpu.VMEM((copies, TILE, PER_COPY * TILE), BF16),
            slots,
            half,
            half,
            wide,
            wide,
            wide,
            wide,
            f32(3 * col_tiles, TILE),
            own,
            own,
        ],
        in_specs=[HBM] * 7,
        out_specs=[VMEM, SMEM] + [VMEM] * 9,
        scratch_shapes=[
            pltpu.VMEM((RING, CHUNK, TILE, TILE), BF16),
            pltpu.SemaphoreType.DMA((RING,)),
            pltpu.SMEM((copies,), jnp.int32),
            pltpu.VMEM(dual.shape, F32),
            pltpu.VMEM(dual.shape, F32),
            pltpu.SMEM(rows.shape, jnp.int32),
            pltpu.SMEM(cols.shape, jnp.int32),
            pltpu.VMEM(cost.shape, F32),
            pltpu.VMEM(primal.shape, F32),
            pltpu.SemaphoreType.DMA((7,)),
        ],
        compiler_params=pltpu.CompilerParams(vmem_limit_bytes=LIMIT),
    )(
        *[
            pltpu.with_memory_space_constraint(a, pltpu.HBM)
            for a in (rows, cols, tiles, dual, rhs, cost, primal)
        ]
    )


def again(kernel, outs, scalars, turned, *vectors, scratch=()):
    specs = [SMEM] * len(scalars)
    if turned is not None:
        vectors = (pltpu.with_memory_space_constraint(turned, pltpu.VMEM), *vectors)
    return pl.pallas_call(
        kernel,
        out_shape=outs,
        in_specs=specs + [VMEM] * len(vectors),
        out_specs=[VMEM] * len(outs),
        scratch_shapes=scratch,
        compiler_params=pltpu.CompilerParams(vmem_limit_bytes=LIMIT),
        cost_estimate=pl.CostEstimate(
            flops=7 * 10**9 if turned is not None else 10**6, bytes_accessed=2**20, transcendentals=0
        ),
    )(*scalars, *vectors)


def swap_core(values):
    n = lax.axis_size("arc")
    return lax.ppermute(values, "arc", [(i, i ^ 1) for i in range(n)])


def exchange(values):
    n = lax.axis_size("arc")
    groups = [[*range(c, n, CORE)] for c in range(CORE)]
    return lax.all_to_all(values, "arc", 0, 0, axis_index_groups=groups, tiled=True)


def with_scen(values):
    n = lax.axis_size("scen")
    shifts = [[(i, (i - k) % n) for i in range(n)] for k in range(1, n)]
    return [values] + [lax.ppermute(values, "scen", pairs) for pairs in shifts]


def per_device(tiles, tile_rows, tile_cols, design, cost, rhs, primal, dual, step_size):
    tile = tiles.shape[1]
    scen_dev, cols_dev = primal.shape
    col_tiles = cols_dev // tile
    row_tiles = dual.shape[0] // tile
    copies = scen_dev * col_tiles
    n_scen, n_arc = lax.axis_size("scen"), lax.axis_size("arc")
    share = row_tiles // n_arc
    chips = n_arc // CORE
    wide = f32(copies, tile)
    tall = f32(row_tiles, tile)
    own = f32(share, tile)
    design = design.reshape(col_tiles, tile)
    step_size, cost = lax.optimization_barrier((jnp.full((1, tile), step_size), cost))

    (
        turned, slot_rows, keep, give, col_peak, gap, cost, primal, send, own_dual, own_rhs
    ) = start(
        n_scen, n_arc, tile_rows, tile_cols, tiles,
        dual.reshape(row_tiles, tile), rhs.reshape(row_tiles, tile), cost, primal,
    )
    sends = with_scen(send)
    near, sends = lax.optimization_barrier((swap_core(give), sends))
    reduced = exchange(jnp.maximum(keep, near).reshape(chips, share, tile))
    send, own_scale, col_scale, means = again(
        row_kernel, [f32(2 * row_tiles, tile), own, wide, f32(2 * col_tiles, tile)],
        [slot_rows], turned, reduced.reshape(chips * share, tile), col_peak, design, *sends,
    )
    gathered = lax.all_to_all(
        send.reshape(n_arc, 2, share, tile), "arc", 0, 0, tiled=True
    ).reshape(2 * row_tiles, tile)
    col_peak, send, own_row = again(
        col_kernel, [wide, f32(2 * col_tiles + 8, tile), own], [slot_rows],
        turned, gathered, own_scale, own_rhs, col_scale, cost, design,
    )
    shared, send = again(
        norm_kernel, [f32(col_tiles, tile), f32(n_arc, tile)], [], None, design, *with_scen(send)
    )
    totals = lax.all_to_all(send, "arc", 0, 0, tiled=True)

    keep, give, new_primal, scalars = again(
        functools.partial(image_kernel, share),
        [tall, tall, f32(scen_dev, cols_dev), f32(8, tile)], [slot_rows],
        turned, step_size, totals, col_peak, shared, col_scale, gap, means, primal, design,
        scratch=[pltpu.VMEM(a.shape, F32) for a in (wide, tall, tall)],
    )
    images = exchange((keep + swap_core(give)).reshape(chips, 2 * share, tile))
    new_dual, send = again(
        dual_kernel, [own, f32(n_scen * n_arc, tile)], [], None,
        step_size, scalars, images.reshape(row_tiles, tile), own_row, own_rhs, own_dual,
    )
    sums = jnp.sum(lax.all_to_all(send, ("scen", "arc"), 0, 0, tiled=True), axis=0)
    omega = scalars[0, 0]
    movement = omega * sums[0] + sums[1] / omega
    return (new_primal, new_dual.reshape(share * tile), movement, sums[2])


def solution(mesh):
    placed = (
        P(("scen", "arc"), None, None),
        P(("scen", "arc")),
        P(("scen", "arc")),
        P("arc"),
        P("scen", "arc"),
        P("scen"),
        P("scen", "arc"),
        P("scen"),
        P(),
    )
    return jax.shard_map(
        per_device,
        mesh=mesh,
        in_specs=placed,
        out_specs=(P("scen", "arc"), P(("scen", "arc")), P(), P()),
        check_vma=False,
    )
```

```python
import functools

import jax
import jax.numpy as jnp
from jax import lax
from jax.experimental import pallas as pl
from jax.experimental.pallas import tpu as pltpu
from jax.sharding import PartitionSpec as P

TILE = 128
PER_COPY = 4
CHUNK = 64
RING = 3
STEP = 32
CORE = 2
F32 = jnp.float32
BF16 = jnp.bfloat16


def peak(block):
    parts = [jnp.abs(block[k : k + 16]) for k in range(0, block.shape[0], 16)]
    while len(parts) > 1:
        parts = [jnp.maximum(a, b) for a, b in zip(parts[::2], parts[1::2])]
    return jnp.max(parts[0].astype(F32), axis=0, keepdims=True)


def bits(size):
    assert size & (size - 1) == 0
    return size.bit_length() - 1


def pieces_of(ref, share):
    return [ref[k : k + share, :] for k in range(0, ref.shape[0], share)]


def by_scen(ref, scen_dev):
    size = ref.shape[0] // scen_dev
    return [ref[k * size : (k + 1) * size, :] for k in range(scen_dev)]


def add(parts):
    return functools.reduce(jnp.add, parts)


def high(parts):
    return functools.reduce(jnp.maximum, parts)


def split_cores(rows, keep, give, share, me, part=0, parts=1):
    for chip in range(rows.shape[0] // (CORE * share)):
        to = (chip * parts + part) * share
        for ref, core in ((keep, me & 1), (give, 1 - (me & 1))):
            start = pl.multiple_of((chip * CORE + core) * share, share)
            ref[to : to + share, :] = rows[pl.ds(start, share), :]


def first_kernel(
    n_scen, n_arc, rows_hbm, cols_hbm, tiles, dual_hbm, rhs_hbm, cost_hbm, primal_hbm,
    turned, slot_rows, keep, give, col_peak, gap, cost, primal, send, own_dual, own_rhs,
    ring, sems, seen, row_peak, dual, rows, cols, cost_flat, primal_flat, more,
):
    count = tiles.shape[0]
    copies = col_peak.shape[0]
    scen_dev = cost_flat.shape[0]
    col_tiles = copies // scen_dev
    row_tiles = dual.shape[0]
    per_scen = row_tiles // scen_dev
    share = row_tiles // n_arc
    chunks = count // CHUNK
    me = lax.axis_index("arc")

    def fetch(chunk):
        slot = lax.rem(chunk, RING)
        return pltpu.make_async_copy(
            tiles.at[pl.ds(chunk * CHUNK, CHUNK)], ring.at[slot], sems.at[slot]
        )

    mine = pl.ds(me * share, share)
    others = [
        pltpu.make_async_copy(dual_hbm, dual, more.at[0]),
        pltpu.make_async_copy(dual_hbm.at[mine], own_dual, more.at[1]),
        pltpu.make_async_copy(rhs_hbm.at[mine], own_rhs, more.at[2]),
        pltpu.make_async_copy(rows_hbm, rows, more.at[3]),
        pltpu.make_async_copy(cols_hbm, cols, more.at[4]),
        pltpu.make_async_copy(cost_hbm, cost_flat, more.at[5]),
        pltpu.make_async_copy(primal_hbm, primal_flat, more.at[6]),
    ]
    for copy in others:
        copy.start()
    for chunk in range(RING - 1):
        fetch(chunk).start()

    col_peak[...] = jnp.zeros_like(col_peak)
    gap[...] = jnp.zeros_like(gap)
    @pl.loop(0, copies)
    def _(copy):
        seen[copy] = 0

    for copy in others:
        copy.wait()
    for s in range(scen_dev):
        for c in range(col_tiles):
            at, to = slice(c * TILE, (c + 1) * TILE), s * col_tiles + c
            cost[to : to + 1, :] = cost_flat[s : s + 1, at]
            primal[to : to + 1, :] = primal_flat[s : s + 1, at]

    def one(k, block):
        r = rows[k]
        copy = ((r >> bits(per_scen)) << bits(col_tiles)) + cols[k]
        nth = seen[copy]
        seen[copy] = nth + 1
        slot_rows[copy * PER_COPY + nth] = r
        here = pl.ds(copy, 1)
        col_peak[here, :] = jnp.maximum(col_peak[here, :], peak(block))
        picked = jnp.broadcast_to(dual[pl.ds(r, 1), :], (16, TILE)).astype(BF16)
        gap[here, :] += jnp.dot(picked, block, preferred_element_type=F32)[:1]
        block = jnp.transpose(block)
        turned[copy, :, pl.ds(pl.multiple_of(nth * TILE, TILE), TILE)] = block
        row_peak[pl.ds(r, 1), :] = peak(block)

    @pl.loop(0, chunks)
    def _(chunk):
        fetch(chunk).wait()

        @pl.when(chunk + RING - 1 < chunks)
        def _():
            fetch(chunk + RING - 1).start()

        slot = lax.rem(chunk, RING)
        for at in range(CHUNK):
            one(chunk * CHUNK + at, ring[slot, at])

    split_cores(row_peak, keep, give, share, me)
    gap[...] = cost[...] - gap[...]
    scenarios = scen_dev * n_scen
    send[:col_tiles, :] = high(by_scen(col_peak, scen_dev))
    send[col_tiles : 2 * col_tiles, :] = add([g / scenarios for g in by_scen(gap, scen_dev)])
    send[2 * col_tiles :, :] = add([p / scenarios for p in by_scen(primal, scen_dev)])


def each_copy(copies, one):
    @pl.loop(0, copies // STEP)
    def _(step):
        for u in range(STEP):
            one(step * STEP + u)


def joined(parts, rows, tops):
    join = lambda f: f(f(parts[0][rows, :], parts[2][rows, :]), f(parts[1][rows, :], parts[3][rows, :]))
    return join(jnp.maximum if rows.stop <= tops else jnp.add)


def row_kernel(
    share, rows, turned, col_peak, design, own, first, second, third,
    keep, give, col_scale, means, row_high,
):
    copies = col_peak.shape[0]
    col_tiles = design.shape[0]
    parts = (own, first, second, third)
    shared = joined(parts, slice(0, col_tiles), col_tiles)
    for k in range(2):
        at = slice((k + 1) * col_tiles, (k + 2) * col_tiles)
        means[k * col_tiles : (k + 1) * col_tiles, :] = joined(parts, at, col_tiles)
    is_design = design[...] == 1
    for s in range(copies // col_tiles):
        at = slice(s * col_tiles, (s + 1) * col_tiles)
        col_scale[at, :] = 1.0 / jnp.sqrt(jnp.where(is_design, shared, col_peak[at, :]))

    def one(copy):
        spread = jnp.transpose(jnp.broadcast_to(col_scale[pl.ds(copy, 1), :], (TILE, TILE)))
        for b in range(PER_COPY):
            block = jnp.abs(turned[copy, :, b * TILE : (b + 1) * TILE].astype(F32))
            here = pl.ds(rows[copy * PER_COPY + b], 1)
            row_high[here, :] = jnp.max(block * spread, axis=0, keepdims=True)

    each_copy(copies, one)
    split_cores(row_high, keep, give, share, lax.axis_index("arc"))


def col_kernel(
    share, rows, turned, same, other, own_row, own_rhs, col_scale, cost, design,
    col_peak, send, row_scale,
):
    me = lax.axis_index("arc")
    for k in range(same.shape[0] // share):
        at = slice(k * share, (k + 1) * share)
        for ref, core in ((same, me & 1), (other, 1 - (me & 1))):
            first = pl.multiple_of((k * CORE + core) * share, share)
            row_scale[pl.ds(first, share), :] = ref[at, :]

    def one(copy):
        best = None
        for b in range(PER_COPY):
            scale = row_scale[pl.ds(rows[copy * PER_COPY + b], 1), :]
            part = jnp.abs(turned[copy, :, b * TILE : (b + 1) * TILE].astype(F32)) * scale
            best = part if best is None else jnp.maximum(best, part)
        here = pl.ds(copy, 1)
        top = jnp.max(jnp.transpose(best), axis=0, keepdims=True)
        col_peak[here, :] = col_scale[here, :] * top

    each_copy(turned.shape[0], one)
    col_tiles = design.shape[0]
    is_design = design[...] == 1
    scen_dev = col_peak.shape[0] // col_tiles
    peaks = by_scen(col_peak, scen_dev)
    send[:col_tiles, :] = high(peaks)
    scaled = [
        (jnp.where(is_design, scale, scale / jnp.sqrt(p)) * c) ** 2
        for scale, p, c in zip(by_scen(col_scale, scen_dev), peaks, by_scen(cost, scen_dev))
    ]
    send[col_tiles : 2 * col_tiles, :] = add(scaled)
    right = (own_row[...] * own_rhs[...]) ** 2
    send[2 * col_tiles :, :] = add([right[k : k + 8] for k in range(0, share, 8)])


def lanes(terms):
    lane = lax.broadcasted_iota(jnp.int32, (1, TILE), 1)
    row = jnp.zeros((1, TILE), F32)
    for k, term in enumerate(terms):
        row = jnp.where(lane == k, jnp.sum(term, axis=1, keepdims=True), row)
    return row


def norm_kernel(design, own, first, second, third, shared, send):
    col_tiles = design.shape[0]
    parts = (own, first, second, third)
    tops = joined(parts, slice(0, col_tiles), col_tiles)
    shared[...] = tops
    squares = joined(parts, slice(col_tiles, 2 * col_tiles), col_tiles)
    squares = jnp.where(design[...] == 1, squares / tops, squares)
    right = joined(parts, slice(2 * col_tiles, 2 * col_tiles + 8), col_tiles)
    rows = [jnp.sum(t, axis=0, keepdims=True) for t in (squares, right)]
    send[...] = jnp.broadcast_to(lanes(rows), send.shape)


def image_kernel(
    share, rows, turned, step_size, totals, col_peak, shared, col_scale, gap, means, primal, design,
    keep, give, new_primal, scalars, step, image, old,
):
    col_tiles = design.shape[0]
    copies = gap.shape[0]
    is_design = design[...] == 1
    total = jnp.sum(totals[...], axis=0, keepdims=True)
    cost_total, rhs_total = total[:, :1], total[:, 1:2]
    omega = jnp.sqrt(cost_total + 1e-06) / jnp.sqrt(rhs_total + 1e-06)
    tau = step_size[...] / omega
    mean_gap = means[:col_tiles, :]
    mean_primal = means[col_tiles:, :]
    moved = None
    for s in range(copies // col_tiles):
        at = slice(s * col_tiles, (s + 1) * col_tiles)
        top = jnp.where(is_design, shared[...], col_peak[at, :])
        scale = col_scale[at, :] / jnp.sqrt(top)
        weight = tau * scale * scale
        here = primal[at, :]
        half = jnp.where(is_design, mean_primal, here) - weight * jnp.where(
            is_design, mean_gap, gap[at, :]
        )
        new = jnp.maximum(half, 0.0)
        step[at, :] = new - here
        square = ((new - here) / scale) ** 2
        moved = square if moved is None else moved + square
        for c in range(col_tiles):
            new_primal[s : s + 1, c * TILE : (c + 1) * TILE] = new[c : c + 1, :]
    scalars[:1, :] = jnp.broadcast_to(omega, (1, TILE))
    scalars[1:2, :] = jnp.sum(moved, axis=0, keepdims=True)

    def one(copy):
        here = pl.ds(copy, 1)
        values = [jnp.broadcast_to(v[here, :], (8, TILE)) for v in (step, primal)]
        values = jnp.concatenate(values, axis=0).astype(BF16)
        out = jnp.dot(values, turned[copy], preferred_element_type=F32)
        for b in range(PER_COPY):
            here, at = pl.ds(rows[copy * PER_COPY + b], 1), slice(b * TILE, (b + 1) * TILE)
            image[here, :] = out[:1, at]
            old[here, :] = out[8:9, at]

    each_copy(copies, one)
    me = lax.axis_index("arc")
    split_cores(image, keep, give, share, me, 0, 2)
    split_cores(old, keep, give, share, me, 1, 2)


def dual_kernel(step_size, scalars, images, own_row, own_rhs, dual, new_dual, send):
    omega = scalars[:1, :]
    sigma = step_size[...] * omega
    scale = own_row[...]
    pieces = pieces_of(images, scale.shape[0])
    step_image, old = add(pieces[::2]), add(pieces[1::2])
    new = jnp.maximum(
        dual[...] + sigma * scale * scale * (own_rhs[...] - old - 2.0 * step_image), 0.0
    )
    step = new - dual[...]
    new_dual[...] = new
    terms = (
        scalars[1:2, :],
        jnp.sum((step / scale) ** 2, axis=0, keepdims=True),
        jnp.sum(step * step_image, axis=0, keepdims=True),
    )
    send[...] = jnp.broadcast_to(lanes(terms), send.shape)


VMEM = pl.BlockSpec(memory_space=pltpu.VMEM)
SMEM = pl.BlockSpec(memory_space=pltpu.SMEM)
HBM = pl.BlockSpec(memory_space=pltpu.HBM)
LIMIT = 20 * 1024 * 1024


def f32(*shape):
    return jax.ShapeDtypeStruct(shape, F32)


def start(n_scen, n_arc, rows, cols, tiles, dual, rhs, cost, primal):
    copies = cost.size // TILE
    col_tiles = copies // cost.shape[0]
    share = dual.shape[0] // n_arc
    slots = jax.ShapeDtypeStruct(rows.shape, jnp.int32)
    wide = f32(copies, TILE)
    own = f32(share, TILE)
    half = f32(dual.shape[0] // CORE, TILE)
    return pl.pallas_call(
        functools.partial(first_kernel, n_scen, n_arc),
        out_shape=[
            pltpu.VMEM((copies, TILE, PER_COPY * TILE), BF16),
            slots,
            half,
            half,
            wide,
            wide,
            wide,
            wide,
            f32(3 * col_tiles, TILE),
            own,
            own,
        ],
        in_specs=[HBM] * 7,
        out_specs=[VMEM, SMEM] + [VMEM] * 9,
        scratch_shapes=[
            pltpu.VMEM((RING, CHUNK, TILE, TILE), BF16),
            pltpu.SemaphoreType.DMA((RING,)),
            pltpu.SMEM((copies,), jnp.int32),
            pltpu.VMEM(dual.shape, F32),
            pltpu.VMEM(dual.shape, F32),
            pltpu.SMEM(rows.shape, jnp.int32),
            pltpu.SMEM(cols.shape, jnp.int32),
            pltpu.VMEM(cost.shape, F32),
            pltpu.VMEM(primal.shape, F32),
            pltpu.SemaphoreType.DMA((7,)),
        ],
        compiler_params=pltpu.CompilerParams(vmem_limit_bytes=LIMIT),
    )(
        *[
            pltpu.with_memory_space_constraint(a, pltpu.HBM)
            for a in (rows, cols, tiles, dual, rhs, cost, primal)
        ]
    )


def again(kernel, outs, scalars, turned, *vectors, scratch=()):
    specs = [SMEM] * len(scalars)
    if turned is not None:
        vectors = (pltpu.with_memory_space_constraint(turned, pltpu.VMEM), *vectors)
    return pl.pallas_call(
        kernel,
        out_shape=outs,
        in_specs=specs + [VMEM] * len(vectors),
        out_specs=[VMEM] * len(outs),
        scratch_shapes=scratch,
        compiler_params=pltpu.CompilerParams(vmem_limit_bytes=LIMIT),
        cost_estimate=pl.CostEstimate(
            flops=7 * 10**9 if turned is not None else 10**6, bytes_accessed=2**20, transcendentals=0
        ),
    )(*scalars, *vectors)


def swap_core(values):
    n = lax.axis_size("arc")
    return lax.ppermute(values, "arc", [(i, i ^ 1) for i in range(n)])


def exchange(values):
    n = lax.axis_size("arc")
    groups = [[*range(c, n, CORE)] for c in range(CORE)]
    return lax.all_to_all(values, "arc", 0, 0, axis_index_groups=groups, tiled=True)


def with_scen(values):
    n = lax.axis_size("scen")
    shifts = [[(i, (i - k) % n) for i in range(n)] for k in range(1, n)]
    return [values] + [lax.ppermute(values, "scen", pairs) for pairs in shifts]


def per_device(tiles, tile_rows, tile_cols, design, cost, rhs, primal, dual, step_size):
    tile = tiles.shape[1]
    scen_dev, cols_dev = primal.shape
    col_tiles = cols_dev // tile
    row_tiles = dual.shape[0] // tile
    copies = scen_dev * col_tiles
    n_scen, n_arc = lax.axis_size("scen"), lax.axis_size("arc")
    share = row_tiles // n_arc
    chips = n_arc // CORE
    wide = f32(copies, tile)
    tall = f32(row_tiles, tile)
    own = f32(share, tile)
    design = design.reshape(col_tiles, tile)
    step_size, cost = lax.optimization_barrier((jnp.full((1, 1), step_size), cost))

    (
        turned, slot_rows, keep, give, col_peak, gap, cost, primal, send, own_dual, own_rhs
    ) = start(
        n_scen, n_arc, tile_rows, tile_cols, tiles,
        dual.reshape(row_tiles, tile), rhs.reshape(row_tiles, tile), cost, primal,
    )
    sends = with_scen(send)
    near, sends = lax.optimization_barrier((swap_core(give), sends))
    half = f32(row_tiles // CORE, tile)
    keep_high, give, col_scale, means = again(
        functools.partial(row_kernel, share), [half, half, wide, f32(2 * col_tiles, tile)],
        [slot_rows], turned, col_peak, design, *sends, scratch=[pltpu.VMEM(tall.shape, F32)],
    )
    tops = [jnp.maximum(keep, near), jnp.maximum(keep_high, swap_core(give))]
    got = exchange(jnp.stack([t.reshape(chips, share, tile) for t in tops], axis=1))
    own_scale = 1.0 / jnp.sqrt(high([*got[:, 0]]))
    own_row = own_scale / jnp.sqrt(own_scale * high([*got[:, 1]]))
    own_scale, own_row = lax.optimization_barrier((own_scale, own_row))
    same = exchange(jnp.broadcast_to(own_scale[None], (chips, share, tile)))
    same = same.reshape(half.shape)
    col_peak, send = again(
        functools.partial(col_kernel, share),
        [wide, f32(2 * col_tiles + 8, tile)], [slot_rows],
        turned, same, swap_core(same), own_row, own_rhs, col_scale, cost, design,
        scratch=[pltpu.VMEM(tall.shape, F32)],
    )
    shared, send = again(
        norm_kernel, [f32(col_tiles, tile), f32(n_arc, tile)], [], None, design, *with_scen(send)
    )
    totals = lax.all_to_all(send, "arc", 0, 0, tiled=True)

    keep, give, new_primal, scalars = again(
        functools.partial(image_kernel, share),
        [tall, tall, f32(scen_dev, cols_dev), f32(8, tile)], [slot_rows],
        turned, step_size, totals, col_peak, shared, col_scale, gap, means, primal, design,
        scratch=[pltpu.VMEM(a.shape, F32) for a in (wide, tall, tall)],
    )
    images = exchange((keep + swap_core(give)).reshape(chips, 2 * share, tile))
    new_dual, send = again(
        dual_kernel, [own, f32(n_scen * n_arc, tile)], [], None,
        step_size, scalars, images.reshape(row_tiles, tile), own_row, own_rhs, own_dual,
    )
    sums = jnp.sum(lax.all_to_all(send, ("scen", "arc"), 0, 0, tiled=True), axis=0)
    omega = scalars[0, 0]
    movement = omega * sums[0] + sums[1] / omega
    return (new_primal, new_dual.reshape(share * tile), movement, sums[2])


def solution(mesh):
    placed = (
        P(("scen", "arc"), None, None),
        P(("scen", "arc")),
        P(("scen", "arc")),
        P("arc"),
        P("scen", "arc"),
        P("scen"),
        P("scen", "arc"),
        P("scen"),
        P(),
    )
    return jax.shard_map(
        per_device,
        mesh=mesh,
        in_specs=placed,
        out_specs=(P("scen", "arc"), P(("scen", "arc")), P(), P()),
        check_vma=False,
    )
```

```python
import functools

import jax
import jax.numpy as jnp
from jax import lax
from jax.experimental import pallas as pl
from jax.experimental.pallas import tpu as pltpu
from jax.sharding import PartitionSpec as P

TILE = 128
PER_COPY = 4
CHUNK = 64
RING = 3
STEP = 32
CORE = 2
F32 = jnp.float32
BF16 = jnp.bfloat16


def peak(block):
    parts = [jnp.abs(block[k : k + 16]) for k in range(0, block.shape[0], 16)]
    while len(parts) > 1:
        parts = [jnp.maximum(a, b) for a, b in zip(parts[::2], parts[1::2])]
    return jnp.max(parts[0].astype(F32), axis=0, keepdims=True)


def bits(size):
    assert size & (size - 1) == 0
    return size.bit_length() - 1


def pieces_of(ref, share):
    return [ref[k : k + share, :] for k in range(0, ref.shape[0], share)]


def by_scen(ref, scen_dev):
    size = ref.shape[0] // scen_dev
    return [ref[k * size : (k + 1) * size, :] for k in range(scen_dev)]


def add(parts):
    return functools.reduce(jnp.add, parts)


def high(parts):
    return functools.reduce(jnp.maximum, parts)


def split_cores(rows, keep, give, share, me, part=0, parts=1):
    for chip in range(rows.shape[0] // (CORE * share)):
        to = (chip * parts + part) * share
        for ref, core in ((keep, me & 1), (give, 1 - (me & 1))):
            start = pl.multiple_of((chip * CORE + core) * share, share)
            ref[to : to + share, :] = rows[pl.ds(start, share), :]


def first_kernel(
    n_scen, n_arc, rows_hbm, cols_hbm, tiles, dual_hbm, rhs_hbm, cost_hbm, primal_hbm,
    turned, slot_rows, keep, give, col_peak, gap, cost, primal, send, own_dual, own_rhs,
    ring, sems, seen, row_peak, dual, rows, cols, cost_flat, primal_flat, more,
):
    count = tiles.shape[0]
    copies = col_peak.shape[0]
    scen_dev = cost_flat.shape[0]
    col_tiles = copies // scen_dev
    row_tiles = dual.shape[0]
    per_scen = row_tiles // scen_dev
    share = row_tiles // n_arc
    chunks = count // CHUNK
    me = lax.axis_index("arc")

    def fetch(chunk):
        slot = lax.rem(chunk, RING)
        return pltpu.make_async_copy(
            tiles.at[pl.ds(chunk * CHUNK, CHUNK)], ring.at[slot], sems.at[slot]
        )

    mine = pl.ds(me * share, share)
    others = [
        pltpu.make_async_copy(dual_hbm, dual, more.at[0]),
        pltpu.make_async_copy(dual_hbm.at[mine], own_dual, more.at[1]),
        pltpu.make_async_copy(rhs_hbm.at[mine], own_rhs, more.at[2]),
        pltpu.make_async_copy(rows_hbm, rows, more.at[3]),
        pltpu.make_async_copy(cols_hbm, cols, more.at[4]),
        pltpu.make_async_copy(cost_hbm, cost_flat, more.at[5]),
        pltpu.make_async_copy(primal_hbm, primal_flat, more.at[6]),
    ]
    for copy in others:
        copy.start()
    for chunk in range(RING - 1):
        fetch(chunk).start()

    col_peak[...] = jnp.zeros_like(col_peak)
    gap[...] = jnp.zeros_like(gap)
    @pl.loop(0, copies)
    def _(copy):
        seen[copy] = 0

    for copy in others:
        copy.wait()
    for s in range(scen_dev):
        for c in range(col_tiles):
            at, to = slice(c * TILE, (c + 1) * TILE), s * col_tiles + c
            cost[to : to + 1, :] = cost_flat[s : s + 1, at]
            primal[to : to + 1, :] = primal_flat[s : s + 1, at]

    def one(k, block):
        r = rows[k]
        copy = ((r >> bits(per_scen)) << bits(col_tiles)) + cols[k]
        nth = seen[copy]
        seen[copy] = nth + 1
        slot_rows[copy * PER_COPY + nth] = r
        here = pl.ds(copy, 1)
        col_peak[here, :] = jnp.maximum(col_peak[here, :], peak(block))
        picked = jnp.broadcast_to(dual[pl.ds(r, 1), :], (16, TILE)).astype(BF16)
        gap[here, :] += jnp.dot(picked, block, preferred_element_type=F32)[:1]
        block = jnp.transpose(block)
        turned[copy, :, pl.ds(pl.multiple_of(nth * TILE, TILE), TILE)] = block
        row_peak[pl.ds(r, 1), :] = peak(block)

    @pl.loop(0, chunks)
    def _(chunk):
        fetch(chunk).wait()

        @pl.when(chunk + RING - 1 < chunks)
        def _():
            fetch(chunk + RING - 1).start()

        slot = lax.rem(chunk, RING)
        for at in range(CHUNK):
            one(chunk * CHUNK + at, ring[slot, at])

    split_cores(row_peak, keep, give, share, me)
    gap[...] = cost[...] - gap[...]
    scenarios = scen_dev * n_scen
    send[:col_tiles, :] = high(by_scen(col_peak, scen_dev))
    send[col_tiles : 2 * col_tiles, :] = add([g / scenarios for g in by_scen(gap, scen_dev)])
    send[2 * col_tiles :, :] = add([p / scenarios for p in by_scen(primal, scen_dev)])


def each_copy(copies, one):
    @pl.loop(0, copies // STEP)
    def _(step):
        for u in range(STEP):
            one(step * STEP + u)


def joined(parts, rows, tops):
    join = lambda f: f(f(parts[0][rows, :], parts[2][rows, :]), f(parts[1][rows, :], parts[3][rows, :]))
    return join(jnp.maximum if rows.stop <= tops else jnp.add)


def row_kernel(
    share, rows, turned, col_peak, design, own, first, second, third,
    keep, give, col_scale, means, row_high,
):
    copies = col_peak.shape[0]
    col_tiles = design.shape[0]
    parts = (own, first, second, third)
    shared = joined(parts, slice(0, col_tiles), col_tiles)
    for k in range(2):
        at = slice((k + 1) * col_tiles, (k + 2) * col_tiles)
        means[k * col_tiles : (k + 1) * col_tiles, :] = joined(parts, at, col_tiles)
    is_design = design[...] == 1
    for s in range(copies // col_tiles):
        at = slice(s * col_tiles, (s + 1) * col_tiles)
        col_scale[at, :] = 1.0 / jnp.sqrt(jnp.where(is_design, shared, col_peak[at, :]))

    def one(copy):
        spread = jnp.transpose(jnp.broadcast_to(col_scale[pl.ds(copy, 1), :], (TILE, TILE)))
        for b in range(PER_COPY):
            block = jnp.abs(turned[copy, :, b * TILE : (b + 1) * TILE].astype(F32))
            here = pl.ds(rows[copy * PER_COPY + b], 1)
            row_high[here, :] = jnp.max(block * spread, axis=0, keepdims=True)

    each_copy(copies, one)
    split_cores(row_high, keep, give, share, lax.axis_index("arc"))


def col_kernel(
    share, rows, turned, same, other, own_row, own_rhs, col_scale, cost, design,
    col_peak, send, row_scale,
):
    me = lax.axis_index("arc")
    for k in range(same.shape[0] // share):
        at = slice(k * share, (k + 1) * share)
        for ref, core in ((same, me & 1), (other, 1 - (me & 1))):
            first = pl.multiple_of((k * CORE + core) * share, share)
            row_scale[pl.ds(first, share), :] = ref[at, :]

    def one(copy):
        best = None
        for b in range(PER_COPY):
            scale = row_scale[pl.ds(rows[copy * PER_COPY + b], 1), :]
            part = jnp.abs(turned[copy, :, b * TILE : (b + 1) * TILE].astype(F32)) * scale
            best = part if best is None else jnp.maximum(best, part)
        here = pl.ds(copy, 1)
        top = jnp.max(jnp.transpose(best), axis=0, keepdims=True)
        col_peak[here, :] = col_scale[here, :] * top

    each_copy(turned.shape[0], one)
    col_tiles = design.shape[0]
    is_design = design[...] == 1
    scen_dev = col_peak.shape[0] // col_tiles
    peaks = by_scen(col_peak, scen_dev)
    send[:col_tiles, :] = high(peaks)
    scaled = [
        (jnp.where(is_design, scale, scale / jnp.sqrt(p)) * c) ** 2
        for scale, p, c in zip(by_scen(col_scale, scen_dev), peaks, by_scen(cost, scen_dev))
    ]
    send[col_tiles : 2 * col_tiles, :] = add(scaled)
    right = (own_row[...] * own_rhs[...]) ** 2
    send[2 * col_tiles :, :] = add([right[k : k + 8] for k in range(0, share, 8)])


def lanes(terms):
    lane = lax.broadcasted_iota(jnp.int32, (1, TILE), 1)
    row = jnp.zeros((1, TILE), F32)
    for k, term in enumerate(terms):
        row = jnp.where(lane == k, jnp.sum(term, axis=1, keepdims=True), row)
    return row


def norm_kernel(design, own, first, second, third, shared, send):
    col_tiles = design.shape[0]
    parts = (own, first, second, third)
    tops = joined(parts, slice(0, col_tiles), col_tiles)
    shared[...] = tops
    squares = joined(parts, slice(col_tiles, 2 * col_tiles), col_tiles)
    squares = jnp.where(design[...] == 1, squares / tops, squares)
    right = joined(parts, slice(2 * col_tiles, 2 * col_tiles + 8), col_tiles)
    rows = [jnp.sum(t, axis=0, keepdims=True) for t in (squares, right)]
    send[...] = jnp.broadcast_to(lanes(rows), send.shape)


def image_kernel(
    share, rows, turned, step_size, totals, col_peak, shared, col_scale, gap, means, primal, design,
    keep, give, new_primal, scalars, step, image, old,
):
    col_tiles = design.shape[0]
    copies = gap.shape[0]
    is_design = design[...] == 1
    total = jnp.sum(totals[...], axis=0, keepdims=True)
    cost_total, rhs_total = total[:, :1], total[:, 1:2]
    omega = jnp.sqrt(cost_total + 1e-06) / jnp.sqrt(rhs_total + 1e-06)
    tau = step_size[:, :1] / omega
    mean_gap = means[:col_tiles, :]
    mean_primal = means[col_tiles:, :]
    moved = None
    for s in range(copies // col_tiles):
        at = slice(s * col_tiles, (s + 1) * col_tiles)
        top = jnp.where(is_design, shared[...], col_peak[at, :])
        scale = col_scale[at, :] / jnp.sqrt(top)
        weight = tau * scale * scale
        here = primal[at, :]
        half = jnp.where(is_design, mean_primal, here) - weight * jnp.where(
            is_design, mean_gap, gap[at, :]
        )
        new = jnp.maximum(half, 0.0)
        step[at, :] = new - here
        square = ((new - here) / scale) ** 2
        moved = square if moved is None else moved + square
        for c in range(col_tiles):
            new_primal[s : s + 1, c * TILE : (c + 1) * TILE] = new[c : c + 1, :]
    scalars[:1, :] = jnp.broadcast_to(omega, (1, TILE))
    scalars[1:2, :] = jnp.sum(moved, axis=0, keepdims=True)

    def one(copy):
        here = pl.ds(copy, 1)
        values = [jnp.broadcast_to(v[here, :], (8, TILE)) for v in (step, primal)]
        values = jnp.concatenate(values, axis=0).astype(BF16)
        out = jnp.dot(values, turned[copy], preferred_element_type=F32)
        for b in range(PER_COPY):
            here, at = pl.ds(rows[copy * PER_COPY + b], 1), slice(b * TILE, (b + 1) * TILE)
            image[here, :] = out[:1, at]
            old[here, :] = out[8:9, at]

    each_copy(copies, one)
    me = lax.axis_index("arc")
    split_cores(image, keep, give, share, me, 0, 2)
    split_cores(old, keep, give, share, me, 1, 2)


def dual_kernel(step_size, scalars, images, own_row, own_rhs, dual, new_dual, send):
    omega = scalars[:1, :]
    sigma = step_size[...] * omega
    scale = own_row[...]
    pieces = pieces_of(images, scale.shape[0])
    step_image, old = add(pieces[::2]), add(pieces[1::2])
    new = jnp.maximum(
        dual[...] + sigma * scale * scale * (own_rhs[...] - old - 2.0 * step_image), 0.0
    )
    step = new - dual[...]
    new_dual[...] = new
    terms = (
        scalars[1:2, :],
        jnp.sum((step / scale) ** 2, axis=0, keepdims=True),
        jnp.sum(step * step_image, axis=0, keepdims=True),
    )
    send[...] = jnp.broadcast_to(lanes(terms), send.shape)


VMEM = pl.BlockSpec(memory_space=pltpu.VMEM)
SMEM = pl.BlockSpec(memory_space=pltpu.SMEM)
HBM = pl.BlockSpec(memory_space=pltpu.HBM)
LIMIT = 20 * 1024 * 1024


def f32(*shape):
    return jax.ShapeDtypeStruct(shape, F32)


def start(n_scen, n_arc, rows, cols, tiles, dual, rhs, cost, primal):
    copies = cost.size // TILE
    col_tiles = copies // cost.shape[0]
    share = dual.shape[0] // n_arc
    slots = jax.ShapeDtypeStruct(rows.shape, jnp.int32)
    wide = f32(copies, TILE)
    own = f32(share, TILE)
    half = f32(dual.shape[0] // CORE, TILE)
    return pl.pallas_call(
        functools.partial(first_kernel, n_scen, n_arc),
        out_shape=[
            pltpu.VMEM((copies, TILE, PER_COPY * TILE), BF16),
            slots,
            half,
            half,
            wide,
            wide,
            wide,
            wide,
            f32(3 * col_tiles, TILE),
            own,
            own,
        ],
        in_specs=[HBM] * 7,
        out_specs=[VMEM, SMEM] + [VMEM] * 9,
        scratch_shapes=[
            pltpu.VMEM((RING, CHUNK, TILE, TILE), BF16),
            pltpu.SemaphoreType.DMA((RING,)),
            pltpu.SMEM((copies,), jnp.int32),
            pltpu.VMEM(dual.shape, F32),
            pltpu.VMEM(dual.shape, F32),
            pltpu.SMEM(rows.shape, jnp.int32),
            pltpu.SMEM(cols.shape, jnp.int32),
            pltpu.VMEM(cost.shape, F32),
            pltpu.VMEM(primal.shape, F32),
            pltpu.SemaphoreType.DMA((7,)),
        ],
        compiler_params=pltpu.CompilerParams(vmem_limit_bytes=LIMIT),
    )(
        *[
            pltpu.with_memory_space_constraint(a, pltpu.HBM)
            for a in (rows, cols, tiles, dual, rhs, cost, primal)
        ]
    )


def again(kernel, outs, scalars, turned, *vectors, scratch=()):
    specs = [SMEM] * len(scalars)
    if turned is not None:
        vectors = (pltpu.with_memory_space_constraint(turned, pltpu.VMEM), *vectors)
    return pl.pallas_call(
        kernel,
        out_shape=outs,
        in_specs=specs + [VMEM] * len(vectors),
        out_specs=[VMEM] * len(outs),
        scratch_shapes=scratch,
        compiler_params=pltpu.CompilerParams(vmem_limit_bytes=LIMIT),
        cost_estimate=pl.CostEstimate(
            flops=7 * 10**9 if turned is not None else 10**6, bytes_accessed=2**20, transcendentals=0
        ),
    )(*scalars, *vectors)


def swap_core(values):
    n = lax.axis_size("arc")
    return lax.ppermute(values, "arc", [(i, i ^ 1) for i in range(n)])


def exchange(values):
    n = lax.axis_size("arc")
    groups = [[*range(c, n, CORE)] for c in range(CORE)]
    return lax.all_to_all(values, "arc", 0, 0, axis_index_groups=groups, tiled=True)


def with_scen(values):
    n = lax.axis_size("scen")
    shifts = [[(i, (i - k) % n) for i in range(n)] for k in range(1, n)]
    return [values] + [lax.ppermute(values, "scen", pairs) for pairs in shifts]


def per_device(tiles, tile_rows, tile_cols, design, cost, rhs, primal, dual, step_size):
    tile = tiles.shape[1]
    scen_dev, cols_dev = primal.shape
    col_tiles = cols_dev // tile
    row_tiles = dual.shape[0] // tile
    copies = scen_dev * col_tiles
    n_scen, n_arc = lax.axis_size("scen"), lax.axis_size("arc")
    share = row_tiles // n_arc
    chips = n_arc // CORE
    wide = f32(copies, tile)
    tall = f32(row_tiles, tile)
    own = f32(share, tile)
    design = design.reshape(col_tiles, tile)
    step_size, cost = lax.optimization_barrier((jnp.full((1, tile), step_size), cost))

    (
        turned, slot_rows, keep, give, col_peak, gap, cost, primal, send, own_dual, own_rhs
    ) = start(
        n_scen, n_arc, tile_rows, tile_cols, tiles,
        dual.reshape(row_tiles, tile), rhs.reshape(row_tiles, tile), cost, primal,
    )
    sends = with_scen(send)
    near, sends = lax.optimization_barrier((swap_core(give), sends))
    half = f32(row_tiles // CORE, tile)
    keep_high, give, col_scale, means = again(
        functools.partial(row_kernel, share), [half, half, wide, f32(2 * col_tiles, tile)],
        [slot_rows], turned, col_peak, design, *sends, scratch=[pltpu.VMEM(tall.shape, F32)],
    )
    tops = [jnp.maximum(keep, near), jnp.maximum(keep_high, swap_core(give))]
    got = exchange(jnp.stack([t.reshape(chips, share, tile) for t in tops], axis=1))
    own_scale = 1.0 / jnp.sqrt(high([*got[:, 0]]))
    own_row = own_scale / jnp.sqrt(own_scale * high([*got[:, 1]]))
    own_scale, own_row = lax.optimization_barrier((own_scale, own_row))
    same = exchange(jnp.broadcast_to(own_scale[None], (chips, share, tile)))
    same = same.reshape(half.shape)
    col_peak, send = again(
        functools.partial(col_kernel, share),
        [wide, f32(2 * col_tiles + 8, tile)], [slot_rows],
        turned, same, swap_core(same), own_row, own_rhs, col_scale, cost, design,
        scratch=[pltpu.VMEM(tall.shape, F32)],
    )
    shared, send = again(
        norm_kernel, [f32(col_tiles, tile), f32(n_arc, tile)], [], None, design, *with_scen(send)
    )
    totals = lax.all_to_all(send, "arc", 0, 0, tiled=True)

    keep, give, new_primal, scalars = again(
        functools.partial(image_kernel, share),
        [tall, tall, f32(scen_dev, cols_dev), f32(8, tile)], [slot_rows],
        turned, step_size, totals, col_peak, shared, col_scale, gap, means, primal, design,
        scratch=[pltpu.VMEM(a.shape, F32) for a in (wide, tall, tall)],
    )
    images = exchange((keep + swap_core(give)).reshape(chips, 2 * share, tile))
    new_dual, send = again(
        dual_kernel, [own, f32(n_scen * n_arc, tile)], [], None,
        step_size, scalars, images.reshape(row_tiles, tile), own_row, own_rhs, own_dual,
    )
    sums = jnp.sum(lax.all_to_all(send, ("scen", "arc"), 0, 0, tiled=True), axis=0)
    omega = scalars[0, 0]
    movement = omega * sums[0] + sums[1] / omega
    return (new_primal, new_dual.reshape(share * tile), movement, sums[2])


def solution(mesh):
    placed = (
        P(("scen", "arc"), None, None),
        P(("scen", "arc")),
        P(("scen", "arc")),
        P("arc"),
        P("scen", "arc"),
        P("scen"),
        P("scen", "arc"),
        P("scen"),
        P(),
    )
    return jax.shard_map(
        per_device,
        mesh=mesh,
        in_specs=placed,
        out_specs=(P("scen", "arc"), P(("scen", "arc")), P(), P()),
        check_vma=False,
    )
```

```python
import functools

import jax
import jax.numpy as jnp
from jax import lax
from jax.experimental import pallas as pl
from jax.experimental.pallas import tpu as pltpu
from jax.sharding import PartitionSpec as P

TILE = 128
PER_COPY = 4
CHUNK = 64
RING = 3
STEP = 32
CORE = 2
F32 = jnp.float32
BF16 = jnp.bfloat16


def peak(block):
    parts = [jnp.abs(block[k : k + 16]) for k in range(0, block.shape[0], 16)]
    while len(parts) > 1:
        parts = [jnp.maximum(a, b) for a, b in zip(parts[::2], parts[1::2])]
    return jnp.max(parts[0].astype(F32), axis=0, keepdims=True)


def bits(size):
    assert size & (size - 1) == 0
    return size.bit_length() - 1


def pieces_of(ref, share):
    return [ref[k : k + share, :] for k in range(0, ref.shape[0], share)]


def by_scen(ref, scen_dev):
    size = ref.shape[0] // scen_dev
    return [ref[k * size : (k + 1) * size, :] for k in range(scen_dev)]


def add(parts):
    return functools.reduce(jnp.add, parts)


def high(parts):
    return functools.reduce(jnp.maximum, parts)


def split_cores(rows, keep, give, share, me, part=0, parts=1):
    for chip in range(rows.shape[0] // (CORE * share)):
        to = (chip * parts + part) * share
        for ref, core in ((keep, me & 1), (give, 1 - (me & 1))):
            start = pl.multiple_of((chip * CORE + core) * share, share)
            ref[to : to + share, :] = rows[pl.ds(start, share), :]


def first_kernel(
    n_scen, n_arc, rows_hbm, cols_hbm, tiles, dual_hbm, rhs_hbm, cost_hbm, primal_hbm,
    turned, slot_rows, keep, give, col_peak, gap, cost, primal, send, own_dual, own_rhs,
    ring, sems, seen, row_peak, dual, rows, cols, cost_flat, primal_flat, more,
):
    count = tiles.shape[0]
    copies = col_peak.shape[0]
    scen_dev = cost_flat.shape[0]
    col_tiles = copies // scen_dev
    row_tiles = dual.shape[0]
    per_scen = row_tiles // scen_dev
    share = row_tiles // n_arc
    chunks = count // CHUNK
    me = lax.axis_index("arc")

    def fetch(chunk):
        slot = lax.rem(chunk, RING)
        return pltpu.make_async_copy(
            tiles.at[pl.ds(chunk * CHUNK, CHUNK)], ring.at[slot], sems.at[slot]
        )

    mine = pl.ds(me * share, share)
    others = [
        pltpu.make_async_copy(dual_hbm, dual, more.at[0]),
        pltpu.make_async_copy(dual_hbm.at[mine], own_dual, more.at[1]),
        pltpu.make_async_copy(rhs_hbm.at[mine], own_rhs, more.at[2]),
        pltpu.make_async_copy(rows_hbm, rows, more.at[3]),
        pltpu.make_async_copy(cols_hbm, cols, more.at[4]),
        pltpu.make_async_copy(cost_hbm, cost_flat, more.at[5]),
        pltpu.make_async_copy(primal_hbm, primal_flat, more.at[6]),
    ]
    for copy in others:
        copy.start()
    for chunk in range(RING - 1):
        fetch(chunk).start()

    col_peak[...] = jnp.zeros_like(col_peak)
    gap[...] = jnp.zeros_like(gap)
    @pl.loop(0, copies)
    def _(copy):
        seen[copy] = 0

    for copy in others:
        copy.wait()
    for s in range(scen_dev):
        for c in range(col_tiles):
            at, to = slice(c * TILE, (c + 1) * TILE), s * col_tiles + c
            cost[to : to + 1, :] = cost_flat[s : s + 1, at]
            primal[to : to + 1, :] = primal_flat[s : s + 1, at]

    def one(k, block):
        r = rows[k]
        copy = ((r >> bits(per_scen)) << bits(col_tiles)) + cols[k]
        nth = seen[copy]
        seen[copy] = nth + 1
        slot_rows[copy * PER_COPY + nth] = r
        here = pl.ds(copy, 1)
        col_peak[here, :] = jnp.maximum(col_peak[here, :], peak(block))
        picked = jnp.broadcast_to(dual[pl.ds(r, 1), :], (16, TILE)).astype(BF16)
        gap[here, :] += jnp.dot(picked, block, preferred_element_type=F32)[:1]
        block = jnp.transpose(block)
        turned[copy, :, pl.ds(pl.multiple_of(nth * TILE, TILE), TILE)] = block
        row_peak[pl.ds(r, 1), :] = peak(block)

    @pl.loop(0, chunks)
    def _(chunk):
        fetch(chunk).wait()

        @pl.when(chunk + RING - 1 < chunks)
        def _():
            fetch(chunk + RING - 1).start()

        slot = lax.rem(chunk, RING)
        for at in range(CHUNK):
            one(chunk * CHUNK + at, ring[slot, at])

    split_cores(row_peak, keep, give, share, me)
    gap[...] = cost[...] - gap[...]
    scenarios = scen_dev * n_scen
    send[:col_tiles, :] = high(by_scen(col_peak, scen_dev))
    send[col_tiles : 2 * col_tiles, :] = add([g / scenarios for g in by_scen(gap, scen_dev)])
    send[2 * col_tiles :, :] = add([p / scenarios for p in by_scen(primal, scen_dev)])


def each_copy(copies, one):
    @pl.loop(0, copies // STEP)
    def _(step):
        for u in range(STEP):
            one(step * STEP + u)


def joined(parts, rows, tops):
    join = lambda f: f(f(parts[0][rows, :], parts[2][rows, :]), f(parts[1][rows, :], parts[3][rows, :]))
    return join(jnp.maximum if rows.stop <= tops else jnp.add)


def row_kernel(
    share, rows, turned, col_peak, design, own, first, second, third,
    keep, give, col_scale, means, row_high,
):
    copies = col_peak.shape[0]
    col_tiles = design.shape[0]
    parts = (own, first, second, third)
    shared = joined(parts, slice(0, col_tiles), col_tiles)
    for k in range(2):
        at = slice((k + 1) * col_tiles, (k + 2) * col_tiles)
        means[k * col_tiles : (k + 1) * col_tiles, :] = joined(parts, at, col_tiles)
    is_design = design[...] == 1
    for s in range(copies // col_tiles):
        at = slice(s * col_tiles, (s + 1) * col_tiles)
        col_scale[at, :] = 1.0 / jnp.sqrt(jnp.where(is_design, shared, col_peak[at, :]))

    def one(copy):
        spread = jnp.transpose(jnp.broadcast_to(col_scale[pl.ds(copy, 1), :], (TILE, TILE)))
        for b in range(PER_COPY):
            block = jnp.abs(turned[copy, :, b * TILE : (b + 1) * TILE].astype(F32))
            here = pl.ds(rows[copy * PER_COPY + b], 1)
            row_high[here, :] = jnp.max(block * spread, axis=0, keepdims=True)

    each_copy(copies, one)
    split_cores(row_high, keep, give, share, lax.axis_index("arc"))


def col_kernel(
    rows, turned, gathered, own_scale, own_rhs, col_scale, cost, design,
    col_peak, send, own_row, row_scale,
):
    share = own_scale.shape[0]
    me = lax.axis_index("arc")
    pieces = pieces_of(gathered, share)
    for chip in range(len(pieces) // (CORE + 1)):
        for piece, core in zip(pieces[chip * (CORE + 1) :], (me & 1, 1 - (me & 1))):
            first = pl.multiple_of((chip * CORE + core) * share, share)
            row_scale[pl.ds(first, share), :] = piece
    own = own_scale[...]
    own = own / jnp.sqrt(own * high(pieces[CORE :: CORE + 1]))
    own_row[...] = own

    def one(copy):
        best = None
        for b in range(PER_COPY):
            scale = row_scale[pl.ds(rows[copy * PER_COPY + b], 1), :]
            part = jnp.abs(turned[copy, :, b * TILE : (b + 1) * TILE].astype(F32)) * scale
            best = part if best is None else jnp.maximum(best, part)
        here = pl.ds(copy, 1)
        top = jnp.max(jnp.transpose(best), axis=0, keepdims=True)
        col_peak[here, :] = col_scale[here, :] * top

    each_copy(turned.shape[0], one)
    col_tiles = design.shape[0]
    is_design = design[...] == 1
    scen_dev = col_peak.shape[0] // col_tiles
    peaks = by_scen(col_peak, scen_dev)
    send[:col_tiles, :] = high(peaks)
    scaled = [
        (jnp.where(is_design, scale, scale / jnp.sqrt(p)) * c) ** 2
        for scale, p, c in zip(by_scen(col_scale, scen_dev), peaks, by_scen(cost, scen_dev))
    ]
    send[col_tiles : 2 * col_tiles, :] = add(scaled)
    right = (own * own_rhs[...]) ** 2
    send[2 * col_tiles :, :] = add([right[k : k + 8] for k in range(0, share, 8)])


def lanes(terms):
    lane = lax.broadcasted_iota(jnp.int32, (1, TILE), 1)
    row = jnp.zeros((1, TILE), F32)
    for k, term in enumerate(terms):
        row = jnp.where(lane == k, jnp.sum(term, axis=1, keepdims=True), row)
    return row


def norm_kernel(design, own, first, second, third, shared, send):
    col_tiles = design.shape[0]
    parts = (own, first, second, third)
    tops = joined(parts, slice(0, col_tiles), col_tiles)
    shared[...] = tops
    squares = joined(parts, slice(col_tiles, 2 * col_tiles), col_tiles)
    squares = jnp.where(design[...] == 1, squares / tops, squares)
    right = joined(parts, slice(2 * col_tiles, 2 * col_tiles + 8), col_tiles)
    rows = [jnp.sum(t, axis=0, keepdims=True) for t in (squares, right)]
    send[...] = jnp.broadcast_to(lanes(rows), send.shape)


def image_kernel(
    share, rows, turned, step_size, totals, col_peak, shared, col_scale, gap, means, primal, design,
    keep, give, new_primal, scalars, step, image, old,
):
    col_tiles = design.shape[0]
    copies = gap.shape[0]
    is_design = design[...] == 1
    total = jnp.sum(totals[...], axis=0, keepdims=True)
    cost_total, rhs_total = total[:, :1], total[:, 1:2]
    omega = jnp.sqrt(cost_total + 1e-06) / jnp.sqrt(rhs_total + 1e-06)
    tau = step_size[:, :1] / omega
    mean_gap = means[:col_tiles, :]
    mean_primal = means[col_tiles:, :]
    moved = None
    for s in range(copies // col_tiles):
        at = slice(s * col_tiles, (s + 1) * col_tiles)
        top = jnp.where(is_design, shared[...], col_peak[at, :])
        scale = col_scale[at, :] / jnp.sqrt(top)
        weight = tau * scale * scale
        here = primal[at, :]
        half = jnp.where(is_design, mean_primal, here) - weight * jnp.where(
            is_design, mean_gap, gap[at, :]
        )
        new = jnp.maximum(half, 0.0)
        step[at, :] = new - here
        square = ((new - here) / scale) ** 2
        moved = square if moved is None else moved + square
        for c in range(col_tiles):
            new_primal[s : s + 1, c * TILE : (c + 1) * TILE] = new[c : c + 1, :]
    scalars[:1, :] = jnp.broadcast_to(omega, (1, TILE))
    scalars[1:2, :] = jnp.sum(moved, axis=0, keepdims=True)

    def one(copy):
        here = pl.ds(copy, 1)
        values = [jnp.broadcast_to(v[here, :], (8, TILE)) for v in (step, primal)]
        values = jnp.concatenate(values, axis=0).astype(BF16)
        out = jnp.dot(values, turned[copy], preferred_element_type=F32)
        for b in range(PER_COPY):
            here, at = pl.ds(rows[copy * PER_COPY + b], 1), slice(b * TILE, (b + 1) * TILE)
            image[here, :] = out[:1, at]
            old[here, :] = out[8:9, at]

    each_copy(copies, one)
    me = lax.axis_index("arc")
    split_cores(image, keep, give, share, me, 0, 2)
    split_cores(old, keep, give, share, me, 1, 2)


def dual_kernel(step_size, scalars, images, own_row, own_rhs, dual, new_dual, send):
    omega = scalars[:1, :]
    sigma = step_size[...] * omega
    scale = own_row[...]
    pieces = pieces_of(images, scale.shape[0])
    step_image, old = add(pieces[::2]), add(pieces[1::2])
    new = jnp.maximum(
        dual[...] + sigma * scale * scale * (own_rhs[...] - old - 2.0 * step_image), 0.0
    )
    step = new - dual[...]
    new_dual[...] = new
    moved = jnp.sum((step / scale) ** 2, axis=0, keepdims=True)
    terms = (
        omega * scalars[1:2, :] + moved / omega,
        jnp.sum(step * step_image, axis=0, keepdims=True),
    )
    send[...] = jnp.broadcast_to(lanes(terms), send.shape)


VMEM = pl.BlockSpec(memory_space=pltpu.VMEM)
SMEM = pl.BlockSpec(memory_space=pltpu.SMEM)
HBM = pl.BlockSpec(memory_space=pltpu.HBM)
LIMIT = 20 * 1024 * 1024


def f32(*shape):
    return jax.ShapeDtypeStruct(shape, F32)


def start(n_scen, n_arc, rows, cols, tiles, dual, rhs, cost, primal):
    copies = cost.size // TILE
    col_tiles = copies // cost.shape[0]
    share = dual.shape[0] // n_arc
    slots = jax.ShapeDtypeStruct(rows.shape, jnp.int32)
    wide = f32(copies, TILE)
    own = f32(share, TILE)
    half = f32(dual.shape[0] // CORE, TILE)
    return pl.pallas_call(
        functools.partial(first_kernel, n_scen, n_arc),
        out_shape=[
            pltpu.VMEM((copies, TILE, PER_COPY * TILE), BF16),
            slots,
            half,
            half,
            wide,
            wide,
            wide,
            wide,
            f32(3 * col_tiles, TILE),
            own,
            own,
        ],
        in_specs=[HBM] * 7,
        out_specs=[VMEM, SMEM] + [VMEM] * 9,
        scratch_shapes=[
            pltpu.VMEM((RING, CHUNK, TILE, TILE), BF16),
            pltpu.SemaphoreType.DMA((RING,)),
            pltpu.SMEM((copies,), jnp.int32),
            pltpu.VMEM(dual.shape, F32),
            pltpu.VMEM(dual.shape, F32),
            pltpu.SMEM(rows.shape, jnp.int32),
            pltpu.SMEM(cols.shape, jnp.int32),
            pltpu.VMEM(cost.shape, F32),
            pltpu.VMEM(primal.shape, F32),
            pltpu.SemaphoreType.DMA((7,)),
        ],
        compiler_params=pltpu.CompilerParams(vmem_limit_bytes=LIMIT),
    )(
        *[
            pltpu.with_memory_space_constraint(a, pltpu.HBM)
            for a in (rows, cols, tiles, dual, rhs, cost, primal)
        ]
    )


def again(kernel, outs, scalars, turned, *vectors, scratch=()):
    specs = [SMEM] * len(scalars)
    if turned is not None:
        vectors = (pltpu.with_memory_space_constraint(turned, pltpu.VMEM), *vectors)
    return pl.pallas_call(
        kernel,
        out_shape=outs,
        in_specs=specs + [VMEM] * len(vectors),
        out_specs=[VMEM] * len(outs),
        scratch_shapes=scratch,
        compiler_params=pltpu.CompilerParams(vmem_limit_bytes=LIMIT),
        cost_estimate=pl.CostEstimate(
            flops=7 * 10**9 if turned is not None else 10**6, bytes_accessed=2**20, transcendentals=0
        ),
    )(*scalars, *vectors)


def swap_core(values):
    n = lax.axis_size("arc")
    return lax.ppermute(values, "arc", [(i, i ^ 1) for i in range(n)])


def exchange(values):
    n = lax.axis_size("arc")
    groups = [[*range(c, n, CORE)] for c in range(CORE)]
    return lax.all_to_all(values, "arc", 0, 0, axis_index_groups=groups, tiled=True)


def with_scen(values):
    n = lax.axis_size("scen")
    shifts = [[(i, (i - k) % n) for i in range(n)] for k in range(1, n)]
    return [values] + [lax.ppermute(values, "scen", pairs) for pairs in shifts]


def per_device(tiles, tile_rows, tile_cols, design, cost, rhs, primal, dual, step_size):
    tile = tiles.shape[1]
    scen_dev, cols_dev = primal.shape
    col_tiles = cols_dev // tile
    row_tiles = dual.shape[0] // tile
    copies = scen_dev * col_tiles
    n_scen, n_arc = lax.axis_size("scen"), lax.axis_size("arc")
    share = row_tiles // n_arc
    chips = n_arc // CORE
    wide = f32(copies, tile)
    tall = f32(row_tiles, tile)
    own = f32(share, tile)
    design = design.reshape(col_tiles, tile)
    step_size, cost = lax.optimization_barrier((jnp.full((1, tile), step_size), cost))

    (
        turned, slot_rows, keep, give, col_peak, gap, cost, primal, send, own_dual, own_rhs
    ) = start(
        n_scen, n_arc, tile_rows, tile_cols, tiles,
        dual.reshape(row_tiles, tile), rhs.reshape(row_tiles, tile), cost, primal,
    )
    sends = with_scen(send)
    near, sends = lax.optimization_barrier((swap_core(give), sends))
    reduced = exchange(jnp.maximum(keep, near).reshape(chips, share, tile))
    own_scale = 1.0 / jnp.sqrt(high([*reduced]))
    own_scale, col_peak = lax.optimization_barrier((own_scale, col_peak))
    other_scale = swap_core(own_scale)
    half = f32(row_tiles // CORE, tile)
    keep, give, col_scale, means = again(
        functools.partial(row_kernel, share), [half, half, wide, f32(2 * col_tiles, tile)],
        [slot_rows], turned, col_peak, design, *sends, scratch=[pltpu.VMEM(tall.shape, F32)],
    )
    row_high = jnp.maximum(keep, swap_core(give)).reshape(chips, share, tile)
    scales = [jnp.broadcast_to(v[None], row_high.shape) for v in (own_scale, other_scale)]
    gathered = exchange(jnp.stack((*scales, row_high), axis=1))
    col_peak, send, own_row = again(
        col_kernel, [wide, f32(2 * col_tiles + 8, tile), own], [slot_rows],
        turned, gathered.reshape(-1, tile), own_scale, own_rhs, col_scale, cost, design,
        scratch=[pltpu.VMEM(tall.shape, F32)],
    )
    shared, send = again(
        norm_kernel, [f32(col_tiles, tile), f32(n_arc, tile)], [], None, design, *with_scen(send)
    )
    totals = lax.all_to_all(send, "arc", 0, 0, tiled=True)

    keep, give, new_primal, scalars = again(
        functools.partial(image_kernel, share),
        [tall, tall, f32(scen_dev, cols_dev), f32(8, tile)], [slot_rows],
        turned, step_size, totals, col_peak, shared, col_scale, gap, means, primal, design,
        scratch=[pltpu.VMEM(a.shape, F32) for a in (wide, tall, tall)],
    )
    images = exchange((keep + swap_core(give)).reshape(chips, 2 * share, tile))
    new_dual, send = again(
        dual_kernel, [own, f32(n_scen * n_arc, tile)], [], None,
        step_size, scalars, images.reshape(row_tiles, tile), own_row, own_rhs, own_dual,
    )
    sums = jnp.sum(lax.all_to_all(send, ("scen", "arc"), 0, 0, tiled=True), axis=0)
    return (new_primal, new_dual.reshape(share * tile), sums[0], sums[1])


def solution(mesh):
    placed = (
        P(("scen", "arc"), None, None),
        P(("scen", "arc")),
        P(("scen", "arc")),
        P("arc"),
        P("scen", "arc"),
        P("scen"),
        P("scen", "arc"),
        P("scen"),
        P(),
    )
    return jax.shard_map(
        per_device,
        mesh=mesh,
        in_specs=placed,
        out_specs=(P("scen", "arc"), P(("scen", "arc")), P(), P()),
        check_vma=False,
    )
```

```python
import functools

import jax
import jax.numpy as jnp
from jax import lax
from jax.experimental import pallas as pl
from jax.experimental.pallas import tpu as pltpu
from jax.sharding import PartitionSpec as P

TILE = 128
PER_COPY = 4
CHUNK = 64
RING = 3
STEP = 32
CORE = 2
F32 = jnp.float32
BF16 = jnp.bfloat16


def peak(block):
    parts = [jnp.abs(block[k : k + 16]) for k in range(0, block.shape[0], 16)]
    while len(parts) > 1:
        parts = [jnp.maximum(a, b) for a, b in zip(parts[::2], parts[1::2])]
    return jnp.max(parts[0].astype(F32), axis=0, keepdims=True)


def bits(size):
    assert size & (size - 1) == 0
    return size.bit_length() - 1


def pieces_of(ref, share):
    return [ref[k : k + share, :] for k in range(0, ref.shape[0], share)]


def by_scen(ref, scen_dev):
    size = ref.shape[0] // scen_dev
    return [ref[k * size : (k + 1) * size, :] for k in range(scen_dev)]


def add(parts):
    return functools.reduce(jnp.add, parts)


def high(parts):
    return functools.reduce(jnp.maximum, parts)


def split_cores(rows, keep, give, share, me, part=0, parts=1):
    for chip in range(rows.shape[0] // (CORE * share)):
        to = (chip * parts + part) * share
        for ref, core in ((keep, me & 1), (give, 1 - (me & 1))):
            start = pl.multiple_of((chip * CORE + core) * share, share)
            ref[to : to + share, :] = rows[pl.ds(start, share), :]


def first_kernel(
    n_scen, n_arc, rows_hbm, cols_hbm, tiles, dual_hbm, rhs_hbm, cost_hbm, primal_hbm,
    turned, slot_rows, keep, give, col_peak, gap, cost, primal, send, own_dual, own_rhs,
    ring, sems, seen, row_peak, dual, rows, cols, cost_flat, primal_flat, more,
):
    count = tiles.shape[0]
    copies = col_peak.shape[0]
    scen_dev = cost_flat.shape[0]
    col_tiles = copies // scen_dev
    row_tiles = dual.shape[0]
    per_scen = row_tiles // scen_dev
    share = row_tiles // n_arc
    chunks = count // CHUNK
    me = lax.axis_index("arc")

    def fetch(chunk):
        slot = lax.rem(chunk, RING)
        return pltpu.make_async_copy(
            tiles.at[pl.ds(chunk * CHUNK, CHUNK)], ring.at[slot], sems.at[slot]
        )

    mine = pl.ds(me * share, share)
    others = [
        pltpu.make_async_copy(dual_hbm, dual, more.at[0]),
        pltpu.make_async_copy(dual_hbm.at[mine], own_dual, more.at[1]),
        pltpu.make_async_copy(rhs_hbm.at[mine], own_rhs, more.at[2]),
        pltpu.make_async_copy(rows_hbm, rows, more.at[3]),
        pltpu.make_async_copy(cols_hbm, cols, more.at[4]),
        pltpu.make_async_copy(cost_hbm, cost_flat, more.at[5]),
        pltpu.make_async_copy(primal_hbm, primal_flat, more.at[6]),
    ]
    for copy in others:
        copy.start()
    for chunk in range(RING - 1):
        fetch(chunk).start()

    col_peak[...] = jnp.zeros_like(col_peak)
    gap[...] = jnp.zeros_like(gap)
    @pl.loop(0, copies)
    def _(copy):
        seen[copy] = 0

    for copy in others:
        copy.wait()
    for s in range(scen_dev):
        for c in range(col_tiles):
            at, to = slice(c * TILE, (c + 1) * TILE), s * col_tiles + c
            cost[to : to + 1, :] = cost_flat[s : s + 1, at]
            primal[to : to + 1, :] = primal_flat[s : s + 1, at]

    def one(k, block):
        r = rows[k]
        copy = ((r >> bits(per_scen)) << bits(col_tiles)) + cols[k]
        nth = seen[copy]
        seen[copy] = nth + 1
        slot_rows[copy * PER_COPY + nth] = r
        here = pl.ds(copy, 1)
        col_peak[here, :] = jnp.maximum(col_peak[here, :], peak(block))
        picked = jnp.broadcast_to(dual[pl.ds(r, 1), :], (16, TILE)).astype(BF16)
        gap[here, :] += jnp.dot(picked, block, preferred_element_type=F32)[:1]
        block = jnp.transpose(block)
        turned[copy, :, pl.ds(pl.multiple_of(nth * TILE, TILE), TILE)] = block
        row_peak[pl.ds(r, 1), :] = peak(block)

    @pl.loop(0, chunks)
    def _(chunk):
        fetch(chunk).wait()

        @pl.when(chunk + RING - 1 < chunks)
        def _():
            fetch(chunk + RING - 1).start()

        slot = lax.rem(chunk, RING)
        for at in range(CHUNK):
            one(chunk * CHUNK + at, ring[slot, at])

    split_cores(row_peak, keep, give, share, me)
    gap[...] = cost[...] - gap[...]
    scenarios = scen_dev * n_scen
    send[:col_tiles, :] = high(by_scen(col_peak, scen_dev))
    send[col_tiles : 2 * col_tiles, :] = add([g / scenarios for g in by_scen(gap, scen_dev)])
    send[2 * col_tiles :, :] = add([p / scenarios for p in by_scen(primal, scen_dev)])


def each_copy(copies, one):
    @pl.loop(0, copies // STEP)
    def _(step):
        for u in range(STEP):
            one(step * STEP + u)


def joined(parts, rows, tops):
    join = lambda f: f(f(parts[0][rows, :], parts[2][rows, :]), f(parts[1][rows, :], parts[3][rows, :]))
    return join(jnp.maximum if rows.stop <= tops else jnp.add)


def row_kernel(
    rows, turned, own_scale, col_peak, design, own, first, third, second,
    keep, give, col_scale, means, row_high,
):
    copies = col_peak.shape[0]
    col_tiles = design.shape[0]
    parts = (own, first, second, third)
    shared = joined(parts, slice(0, col_tiles), col_tiles)
    for k in range(2):
        at = slice((k + 1) * col_tiles, (k + 2) * col_tiles)
        means[k * col_tiles : (k + 1) * col_tiles, :] = joined(parts, at, col_tiles)
    is_design = design[...] == 1
    for s in range(copies // col_tiles):
        at = slice(s * col_tiles, (s + 1) * col_tiles)
        col_scale[at, :] = 1.0 / jnp.sqrt(jnp.where(is_design, shared, col_peak[at, :]))

    def one(copy):
        spread = jnp.transpose(jnp.broadcast_to(col_scale[pl.ds(copy, 1), :], (TILE, TILE)))
        for b in range(PER_COPY):
            block = jnp.abs(turned[copy, :, b * TILE : (b + 1) * TILE].astype(F32))
            here = pl.ds(rows[copy * PER_COPY + b], 1)
            row_high[here, :] = jnp.max(block * spread, axis=0, keepdims=True)

    each_copy(copies, one)
    share = own_scale.shape[0]
    split_cores(row_high, keep, give, share, lax.axis_index("arc"))
    give[keep.shape[0] :, :] = own_scale[...]


def col_kernel(
    rows, turned, gathered, own_scale, own_rhs, col_scale, cost, design,
    col_peak, send, own_row, row_scale,
):
    share = own_scale.shape[0]
    me = lax.axis_index("arc")
    pieces = pieces_of(gathered, share)
    for chip in range(len(pieces) // (CORE + 1)):
        for piece, core in zip(pieces[chip * (CORE + 1) :], (me & 1, 1 - (me & 1))):
            first = pl.multiple_of((chip * CORE + core) * share, share)
            row_scale[pl.ds(first, share), :] = piece
    own = own_scale[...]
    own = own / jnp.sqrt(own * high(pieces[CORE :: CORE + 1]))
    own_row[...] = own

    def one(copy):
        best = None
        for b in range(PER_COPY):
            scale = row_scale[pl.ds(rows[copy * PER_COPY + b], 1), :]
            part = jnp.abs(turned[copy, :, b * TILE : (b + 1) * TILE].astype(F32)) * scale
            best = part if best is None else jnp.maximum(best, part)
        here = pl.ds(copy, 1)
        top = jnp.max(jnp.transpose(best), axis=0, keepdims=True)
        col_peak[here, :] = col_scale[here, :] * top

    each_copy(turned.shape[0], one)
    col_tiles = design.shape[0]
    is_design = design[...] == 1
    scen_dev = col_peak.shape[0] // col_tiles
    peaks = by_scen(col_peak, scen_dev)
    send[:col_tiles, :] = high(peaks)
    scaled = [
        (jnp.where(is_design, scale, scale / jnp.sqrt(p)) * c) ** 2
        for scale, p, c in zip(by_scen(col_scale, scen_dev), peaks, by_scen(cost, scen_dev))
    ]
    send[col_tiles : 2 * col_tiles, :] = add(scaled)
    right = (own * own_rhs[...]) ** 2
    send[2 * col_tiles :, :] = add([right[k : k + 8] for k in range(0, share, 8)])


def lanes(terms):
    lane = lax.broadcasted_iota(jnp.int32, (1, TILE), 1)
    row = jnp.zeros((1, TILE), F32)
    for k, term in enumerate(terms):
        row = jnp.where(lane == k, jnp.sum(term, axis=1, keepdims=True), row)
    return row


def norm_kernel(design, own, first, third, second, shared, send):
    col_tiles = design.shape[0]
    parts = (own, first, second, third)
    tops = joined(parts, slice(0, col_tiles), col_tiles)
    shared[...] = tops
    squares = joined(parts, slice(col_tiles, 2 * col_tiles), col_tiles)
    squares = jnp.where(design[...] == 1, squares / tops, squares)
    right = joined(parts, slice(2 * col_tiles, 2 * col_tiles + 8), col_tiles)
    rows = [jnp.sum(t, axis=0, keepdims=True) for t in (squares, right)]
    send[...] = jnp.broadcast_to(lanes(rows), send.shape)


def image_kernel(
    share, rows, turned, step_size, totals, col_peak, shared, col_scale, gap, means, primal, design,
    keep, give, new_primal, scalars, step, image, old,
):
    col_tiles = design.shape[0]
    copies = gap.shape[0]
    is_design = design[...] == 1
    total = jnp.sum(totals[...], axis=0, keepdims=True)
    cost_total, rhs_total = total[:, :1], total[:, 1:2]
    omega = jnp.sqrt(cost_total + 1e-06) / jnp.sqrt(rhs_total + 1e-06)
    tau = step_size[:, :1] / omega
    mean_gap = means[:col_tiles, :]
    mean_primal = means[col_tiles:, :]
    moved = None
    for s in range(copies // col_tiles):
        at = slice(s * col_tiles, (s + 1) * col_tiles)
        top = jnp.where(is_design, shared[...], col_peak[at, :])
        scale = col_scale[at, :] / jnp.sqrt(top)
        weight = tau * scale * scale
        here = primal[at, :]
        half = jnp.where(is_design, mean_primal, here) - weight * jnp.where(
            is_design, mean_gap, gap[at, :]
        )
        new = jnp.maximum(half, 0.0)
        step[at, :] = new - here
        square = ((new - here) / scale) ** 2
        moved = square if moved is None else moved + square
        for c in range(col_tiles):
            new_primal[s : s + 1, c * TILE : (c + 1) * TILE] = new[c : c + 1, :]
    scalars[:1, :] = jnp.broadcast_to(omega, (1, TILE))
    scalars[1:2, :] = jnp.sum(moved, axis=0, keepdims=True)

    def one(copy):
        here = pl.ds(copy, 1)
        values = [jnp.broadcast_to(v[here, :], (8, TILE)) for v in (step, primal)]
        values = jnp.concatenate(values, axis=0).astype(BF16)
        out = jnp.dot(values, turned[copy], preferred_element_type=F32)
        for b in range(PER_COPY):
            here, at = pl.ds(rows[copy * PER_COPY + b], 1), slice(b * TILE, (b + 1) * TILE)
            image[here, :] = out[:1, at]
            old[here, :] = out[8:9, at]

    each_copy(copies, one)
    me = lax.axis_index("arc")
    split_cores(image, keep, give, share, me, 0, 2)
    split_cores(old, keep, give, share, me, 1, 2)


def dual_kernel(step_size, scalars, images, own_row, own_rhs, dual, new_dual, send):
    omega = scalars[:1, :]
    sigma = step_size[...] * omega
    scale = own_row[...]
    pieces = pieces_of(images, scale.shape[0])
    step_image, old = add(pieces[::2]), add(pieces[1::2])
    new = jnp.maximum(
        dual[...] + sigma * scale * scale * (own_rhs[...] - old - 2.0 * step_image), 0.0
    )
    step = new - dual[...]
    new_dual[...] = new
    moved = jnp.sum((step / scale) ** 2, axis=0, keepdims=True)
    terms = (
        omega * scalars[1:2, :] + moved / omega,
        jnp.sum(step * step_image, axis=0, keepdims=True),
    )
    send[...] = jnp.broadcast_to(lanes(terms), send.shape)


VMEM = pl.BlockSpec(memory_space=pltpu.VMEM)
SMEM = pl.BlockSpec(memory_space=pltpu.SMEM)
HBM = pl.BlockSpec(memory_space=pltpu.HBM)
LIMIT = 20 * 1024 * 1024


def f32(*shape):
    return jax.ShapeDtypeStruct(shape, F32)


def start(n_scen, n_arc, rows, cols, tiles, dual, rhs, cost, primal):
    copies = cost.size // TILE
    col_tiles = copies // cost.shape[0]
    share = dual.shape[0] // n_arc
    slots = jax.ShapeDtypeStruct(rows.shape, jnp.int32)
    wide = f32(copies, TILE)
    own = f32(share, TILE)
    half = f32(dual.shape[0] // CORE, TILE)
    return pl.pallas_call(
        functools.partial(first_kernel, n_scen, n_arc),
        out_shape=[
            pltpu.VMEM((copies, TILE, PER_COPY * TILE), BF16),
            slots,
            half,
            half,
            wide,
            wide,
            wide,
            wide,
            f32(3 * col_tiles, TILE),
            own,
            own,
        ],
        in_specs=[HBM] * 7,
        out_specs=[VMEM, SMEM] + [VMEM] * 9,
        scratch_shapes=[
            pltpu.VMEM((RING, CHUNK, TILE, TILE), BF16),
            pltpu.SemaphoreType.DMA((RING,)),
            pltpu.SMEM((copies,), jnp.int32),
            pltpu.VMEM(dual.shape, F32),
            pltpu.VMEM(dual.shape, F32),
            pltpu.SMEM(rows.shape, jnp.int32),
            pltpu.SMEM(cols.shape, jnp.int32),
            pltpu.VMEM(cost.shape, F32),
            pltpu.VMEM(primal.shape, F32),
            pltpu.SemaphoreType.DMA((7,)),
        ],
        compiler_params=pltpu.CompilerParams(vmem_limit_bytes=LIMIT),
    )(
        *[
            pltpu.with_memory_space_constraint(a, pltpu.HBM)
            for a in (rows, cols, tiles, dual, rhs, cost, primal)
        ]
    )


def again(kernel, outs, scalars, turned, *vectors, scratch=()):
    specs = [SMEM] * len(scalars)
    if turned is not None:
        vectors = (pltpu.with_memory_space_constraint(turned, pltpu.VMEM), *vectors)
    return pl.pallas_call(
        kernel,
        out_shape=outs,
        in_specs=specs + [VMEM] * len(vectors),
        out_specs=[VMEM] * len(outs),
        scratch_shapes=scratch,
        compiler_params=pltpu.CompilerParams(vmem_limit_bytes=LIMIT),
        cost_estimate=pl.CostEstimate(
            flops=7 * 10**9 if turned is not None else 10**6, bytes_accessed=2**20, transcendentals=0
        ),
    )(*scalars, *vectors)


def swap_core(values):
    n = lax.axis_size("arc")
    return lax.ppermute(values, "arc", [(i, i ^ 1) for i in range(n)])


def exchange(values):
    n = lax.axis_size("arc")
    groups = [[*range(c, n, CORE)] for c in range(CORE)]
    return lax.all_to_all(values, "arc", 0, 0, axis_index_groups=groups, tiled=True)


def with_scen(values):
    n = lax.axis_size("scen")
    shifts = [[(i, (i - k) % n) for i in range(n)] for k in (1, 3, 2)]
    return [values] + [lax.ppermute(values, "scen", pairs) for pairs in shifts]


def per_device(tiles, tile_rows, tile_cols, design, cost, rhs, primal, dual, step_size):
    tile = tiles.shape[1]
    scen_dev, cols_dev = primal.shape
    col_tiles = cols_dev // tile
    row_tiles = dual.shape[0] // tile
    copies = scen_dev * col_tiles
    n_scen, n_arc = lax.axis_size("scen"), lax.axis_size("arc")
    share = row_tiles // n_arc
    chips = n_arc // CORE
    wide = f32(copies, tile)
    tall = f32(row_tiles, tile)
    own = f32(share, tile)
    design = design.reshape(col_tiles, tile)
    step_size, cost = lax.optimization_barrier((jnp.full((1, tile), step_size), cost))

    (
        turned, slot_rows, keep, give, col_peak, gap, cost, primal, send, own_dual, own_rhs
    ) = start(
        n_scen, n_arc, tile_rows, tile_cols, tiles,
        dual.reshape(row_tiles, tile), rhs.reshape(row_tiles, tile), cost, primal,
    )
    sends = with_scen(send)
    near, sends = lax.optimization_barrier((swap_core(give), sends))
    reduced = exchange(jnp.maximum(keep, near).reshape(chips, share, tile))
    own_scale = 1.0 / jnp.sqrt(high([*reduced]))
    own_scale, col_peak = lax.optimization_barrier((own_scale, col_peak))
    half = f32(row_tiles // CORE, tile)
    keep, give, col_scale, means = again(
        row_kernel, [half, f32(half.shape[0] + share, tile), wide, f32(2 * col_tiles, tile)],
        [slot_rows], turned, own_scale, col_peak, design, *sends,
        scratch=[pltpu.VMEM(tall.shape, F32)],
    )
    near = swap_core(give)
    row_high = jnp.maximum(keep, near[: half.shape[0]]).reshape(chips, share, tile)
    scales = [
        jnp.broadcast_to(v[None], row_high.shape) for v in (own_scale, near[half.shape[0] :])
    ]
    gathered = exchange(jnp.stack((*scales, row_high), axis=1))
    col_peak, send, own_row = again(
        col_kernel, [wide, f32(2 * col_tiles + 8, tile), own], [slot_rows],
        turned, gathered.reshape(-1, tile), own_scale, own_rhs, col_scale, cost, design,
        scratch=[pltpu.VMEM(tall.shape, F32)],
    )
    shared, send = again(
        norm_kernel, [f32(col_tiles, tile), f32(n_arc, tile)], [], None, design, *with_scen(send)
    )
    totals = lax.all_to_all(send, "arc", 0, 0, tiled=True)

    keep, give, new_primal, scalars = again(
        functools.partial(image_kernel, share),
        [tall, tall, f32(scen_dev, cols_dev), f32(8, tile)], [slot_rows],
        turned, step_size, totals, col_peak, shared, col_scale, gap, means, primal, design,
        scratch=[pltpu.VMEM(a.shape, F32) for a in (wide, tall, tall)],
    )
    images = exchange((keep + swap_core(give)).reshape(chips, 2 * share, tile))
    new_dual, send = again(
        dual_kernel, [own, f32(n_scen * n_arc, tile)], [], None,
        step_size, scalars, images.reshape(row_tiles, tile), own_row, own_rhs, own_dual,
    )
    sums = jnp.sum(lax.all_to_all(send, ("scen", "arc"), 0, 0, tiled=True), axis=0)
    return (new_primal, new_dual.reshape(share * tile), sums[0], sums[1])


def solution(mesh):
    placed = (
        P(("scen", "arc"), None, None),
        P(("scen", "arc")),
        P(("scen", "arc")),
        P("arc"),
        P("scen", "arc"),
        P("scen"),
        P("scen", "arc"),
        P("scen"),
        P(),
    )
    return jax.shard_map(
        per_device,
        mesh=mesh,
        in_specs=placed,
        out_specs=(P("scen", "arc"), P(("scen", "arc")), P(), P()),
        check_vma=False,
    )
```

```python
import functools

import jax
import jax.numpy as jnp
from jax import lax
from jax.experimental import pallas as pl
from jax.experimental.pallas import tpu as pltpu
from jax.sharding import PartitionSpec as P

TILE = 128
PER_COPY = 4
CHUNK = 64
RING = 3
STEP = 32
CORE = 2
F32 = jnp.float32
BF16 = jnp.bfloat16


def peak(block):
    parts = [jnp.abs(block[k : k + 16]) for k in range(0, block.shape[0], 16)]
    while len(parts) > 1:
        parts = [jnp.maximum(a, b) for a, b in zip(parts[::2], parts[1::2])]
    return jnp.max(parts[0].astype(F32), axis=0, keepdims=True)


def bits(size):
    assert size & (size - 1) == 0
    return size.bit_length() - 1


def pieces_of(ref, share):
    return [ref[k : k + share, :] for k in range(0, ref.shape[0], share)]


def by_scen(ref, scen_dev):
    size = ref.shape[0] // scen_dev
    return [ref[k * size : (k + 1) * size, :] for k in range(scen_dev)]


def add(parts):
    return functools.reduce(jnp.add, parts)


def high(parts):
    return functools.reduce(jnp.maximum, parts)


def split_cores(rows, keep, give, share, me, part=0, parts=1):
    for chip in range(rows.shape[0] // (CORE * share)):
        to = (chip * parts + part) * share
        for ref, core in ((keep, me & 1), (give, 1 - (me & 1))):
            start = pl.multiple_of((chip * CORE + core) * share, share)
            ref[to : to + share, :] = rows[pl.ds(start, share), :]


def first_kernel(
    n_scen, n_arc, rows_hbm, cols_hbm, tiles, dual_hbm, rhs_hbm, cost_hbm, primal_hbm,
    turned, slot_rows, keep, give, col_peak, gap, cost, primal, send, own_dual, own_rhs,
    ring, sems, seen, row_peak, dual, rows, cols, cost_flat, primal_flat, more,
):
    count = tiles.shape[0]
    copies = col_peak.shape[0]
    scen_dev = cost_flat.shape[0]
    col_tiles = copies // scen_dev
    row_tiles = dual.shape[0]
    per_scen = row_tiles // scen_dev
    share = row_tiles // n_arc
    chunks = count // CHUNK
    me = lax.axis_index("arc")

    def fetch(chunk):
        slot = lax.rem(chunk, RING)
        return pltpu.make_async_copy(
            tiles.at[pl.ds(chunk * CHUNK, CHUNK)], ring.at[slot], sems.at[slot]
        )

    mine = pl.ds(me * share, share)
    others = [
        pltpu.make_async_copy(dual_hbm, dual, more.at[0]),
        pltpu.make_async_copy(dual_hbm.at[mine], own_dual, more.at[1]),
        pltpu.make_async_copy(rhs_hbm.at[mine], own_rhs, more.at[2]),
        pltpu.make_async_copy(rows_hbm, rows, more.at[3]),
        pltpu.make_async_copy(cols_hbm, cols, more.at[4]),
        pltpu.make_async_copy(cost_hbm, cost_flat, more.at[5]),
        pltpu.make_async_copy(primal_hbm, primal_flat, more.at[6]),
    ]
    for copy in others:
        copy.start()
    for chunk in range(RING - 1):
        fetch(chunk).start()

    col_peak[...] = jnp.zeros_like(col_peak)
    gap[...] = jnp.zeros_like(gap)
    @pl.loop(0, copies)
    def _(copy):
        seen[copy] = 0

    for copy in others:
        copy.wait()
    for s in range(scen_dev):
        for c in range(col_tiles):
            at, to = slice(c * TILE, (c + 1) * TILE), s * col_tiles + c
            cost[to : to + 1, :] = cost_flat[s : s + 1, at]
            primal[to : to + 1, :] = primal_flat[s : s + 1, at]

    def one(k, block):
        r = rows[k]
        copy = ((r >> bits(per_scen)) << bits(col_tiles)) + cols[k]
        nth = seen[copy]
        seen[copy] = nth + 1
        slot_rows[copy * PER_COPY + nth] = r
        here = pl.ds(copy, 1)
        col_peak[here, :] = jnp.maximum(col_peak[here, :], peak(block))
        picked = jnp.broadcast_to(dual[pl.ds(r, 1), :], (16, TILE)).astype(BF16)
        gap[here, :] += jnp.dot(picked, block, preferred_element_type=F32)[:1]
        block = jnp.transpose(block)
        turned[copy, :, pl.ds(pl.multiple_of(nth * TILE, TILE), TILE)] = block
        row_peak[pl.ds(r, 1), :] = peak(block)

    @pl.loop(0, chunks)
    def _(chunk):
        fetch(chunk).wait()

        @pl.when(chunk + RING - 1 < chunks)
        def _():
            fetch(chunk + RING - 1).start()

        slot = lax.rem(chunk, RING)
        for at in range(CHUNK):
            one(chunk * CHUNK + at, ring[slot, at])

    split_cores(row_peak, keep, give, share, me)
    gap[...] = cost[...] - gap[...]
    scenarios = scen_dev * n_scen
    send[:col_tiles, :] = high(by_scen(col_peak, scen_dev))
    send[col_tiles : 2 * col_tiles, :] = add([g / scenarios for g in by_scen(gap, scen_dev)])
    send[2 * col_tiles :, :] = add([p / scenarios for p in by_scen(primal, scen_dev)])


def each_copy(copies, one):
    @pl.loop(0, copies // STEP)
    def _(step):
        for u in range(STEP):
            one(step * STEP + u)


def joined(parts, rows, tops):
    join = lambda f: f(f(parts[0][rows, :], parts[2][rows, :]), f(parts[1][rows, :], parts[3][rows, :]))
    return join(jnp.maximum if rows.stop <= tops else jnp.add)


def row_kernel(
    rows, turned, own_scale, col_peak, design, own, first, third, second,
    keep, give, col_scale, means, row_high,
):
    copies = col_peak.shape[0]
    col_tiles = design.shape[0]
    parts = (own, first, second, third)
    shared = joined(parts, slice(0, col_tiles), col_tiles)
    for k in range(2):
        at = slice((k + 1) * col_tiles, (k + 2) * col_tiles)
        means[k * col_tiles : (k + 1) * col_tiles, :] = joined(parts, at, col_tiles)
    is_design = design[...] == 1
    for s in range(copies // col_tiles):
        at = slice(s * col_tiles, (s + 1) * col_tiles)
        col_scale[at, :] = 1.0 / jnp.sqrt(jnp.where(is_design, shared, col_peak[at, :]))

    def one(copy):
        spread = jnp.transpose(jnp.broadcast_to(col_scale[pl.ds(copy, 1), :], (TILE, TILE)))
        for b in range(PER_COPY):
            block = jnp.abs(turned[copy, :, b * TILE : (b + 1) * TILE].astype(F32))
            here = pl.ds(rows[copy * PER_COPY + b], 1)
            row_high[here, :] = jnp.max(block * spread, axis=0, keepdims=True)

    each_copy(copies, one)
    share = own_scale.shape[0]
    split_cores(row_high, keep, give, share, lax.axis_index("arc"))
    give[keep.shape[0] :, :] = own_scale[...]


def col_kernel(
    rows, turned, gathered, own_scale, own_rhs, col_scale, cost, design,
    col_peak, send, own_row, row_scale,
):
    share = own_scale.shape[0]
    me = lax.axis_index("arc")
    pieces = pieces_of(gathered, share)
    for chip in range(len(pieces) // (CORE + 1)):
        for piece, core in zip(pieces[chip * (CORE + 1) :], (me & 1, 1 - (me & 1))):
            first = pl.multiple_of((chip * CORE + core) * share, share)
            row_scale[pl.ds(first, share), :] = piece
    own = own_scale[...]
    own = own / jnp.sqrt(own * high(pieces[CORE :: CORE + 1]))
    own_row[...] = own

    def one(copy):
        best = None
        for b in range(PER_COPY):
            scale = row_scale[pl.ds(rows[copy * PER_COPY + b], 1), :]
            part = jnp.abs(turned[copy, :, b * TILE : (b + 1) * TILE].astype(F32)) * scale
            best = part if best is None else jnp.maximum(best, part)
        here = pl.ds(copy, 1)
        top = jnp.max(jnp.transpose(best), axis=0, keepdims=True)
        col_peak[here, :] = col_scale[here, :] * top

    each_copy(turned.shape[0], one)
    col_tiles = design.shape[0]
    is_design = design[...] == 1
    scen_dev = col_peak.shape[0] // col_tiles
    peaks = by_scen(col_peak, scen_dev)
    send[:col_tiles, :] = high(peaks)
    scaled = [
        (jnp.where(is_design, scale, scale / jnp.sqrt(p)) * c) ** 2
        for scale, p, c in zip(by_scen(col_scale, scen_dev), peaks, by_scen(cost, scen_dev))
    ]
    send[col_tiles : 2 * col_tiles, :] = add(scaled)
    right = (own * own_rhs[...]) ** 2
    send[2 * col_tiles :, :] = add([right[k : k + 8] for k in range(0, share, 8)])


def lanes(terms):
    lane = lax.broadcasted_iota(jnp.int32, (1, TILE), 1)
    row = jnp.zeros((1, TILE), F32)
    for k, term in enumerate(terms):
        row = jnp.where(lane == k, jnp.sum(term, axis=1, keepdims=True), row)
    return row


def norm_kernel(design, gathered, shared, send):
    col_tiles = design.shape[0]
    parts = pieces_of(gathered, 2 * col_tiles + 8)
    tops = joined(parts, slice(0, col_tiles), col_tiles)
    shared[...] = tops
    squares = joined(parts, slice(col_tiles, 2 * col_tiles), col_tiles)
    squares = jnp.where(design[...] == 1, squares / tops, squares)
    right = joined(parts, slice(2 * col_tiles, 2 * col_tiles + 8), col_tiles)
    rows = [jnp.sum(t, axis=0, keepdims=True) for t in (squares, right)]
    send[...] = jnp.broadcast_to(lanes(rows), send.shape)


def image_kernel(
    share, rows, turned, step_size, totals, col_peak, shared, col_scale, gap, means, primal, design,
    keep, give, new_primal, scalars, step, image, old,
):
    col_tiles = design.shape[0]
    copies = gap.shape[0]
    is_design = design[...] == 1
    total = jnp.sum(totals[...], axis=0, keepdims=True)
    cost_total, rhs_total = total[:, :1], total[:, 1:2]
    omega = jnp.sqrt(cost_total + 1e-06) / jnp.sqrt(rhs_total + 1e-06)
    tau = step_size[:, :1] / omega
    mean_gap = means[:col_tiles, :]
    mean_primal = means[col_tiles:, :]
    moved = None
    for s in range(copies // col_tiles):
        at = slice(s * col_tiles, (s + 1) * col_tiles)
        top = jnp.where(is_design, shared[...], col_peak[at, :])
        scale = col_scale[at, :] / jnp.sqrt(top)
        weight = tau * scale * scale
        here = primal[at, :]
        half = jnp.where(is_design, mean_primal, here) - weight * jnp.where(
            is_design, mean_gap, gap[at, :]
        )
        new = jnp.maximum(half, 0.0)
        step[at, :] = new - here
        square = ((new - here) / scale) ** 2
        moved = square if moved is None else moved + square
        for c in range(col_tiles):
            new_primal[s : s + 1, c * TILE : (c + 1) * TILE] = new[c : c + 1, :]
    scalars[:1, :] = jnp.broadcast_to(omega, (1, TILE))
    scalars[1:2, :] = jnp.sum(moved, axis=0, keepdims=True)

    def one(copy):
        here = pl.ds(copy, 1)
        values = [jnp.broadcast_to(v[here, :], (8, TILE)) for v in (step, primal)]
        values = jnp.concatenate(values, axis=0).astype(BF16)
        out = jnp.dot(values, turned[copy], preferred_element_type=F32)
        for b in range(PER_COPY):
            here, at = pl.ds(rows[copy * PER_COPY + b], 1), slice(b * TILE, (b + 1) * TILE)
            image[here, :] = out[:1, at]
            old[here, :] = out[8:9, at]

    each_copy(copies, one)
    me = lax.axis_index("arc")
    split_cores(image, keep, give, share, me, 0, 2)
    split_cores(old, keep, give, share, me, 1, 2)


def dual_kernel(step_size, scalars, images, own_row, own_rhs, dual, new_dual, send):
    omega = scalars[:1, :]
    sigma = step_size[...] * omega
    scale = own_row[...]
    pieces = pieces_of(images, scale.shape[0])
    step_image, old = add(pieces[::2]), add(pieces[1::2])
    new = jnp.maximum(
        dual[...] + sigma * scale * scale * (own_rhs[...] - old - 2.0 * step_image), 0.0
    )
    step = new - dual[...]
    new_dual[...] = new
    moved = jnp.sum((step / scale) ** 2, axis=0, keepdims=True)
    terms = (
        omega * scalars[1:2, :] + moved / omega,
        jnp.sum(step * step_image, axis=0, keepdims=True),
    )
    send[...] = jnp.broadcast_to(lanes(terms), send.shape)


VMEM = pl.BlockSpec(memory_space=pltpu.VMEM)
SMEM = pl.BlockSpec(memory_space=pltpu.SMEM)
HBM = pl.BlockSpec(memory_space=pltpu.HBM)
LIMIT = 20 * 1024 * 1024


def f32(*shape):
    return jax.ShapeDtypeStruct(shape, F32)


def start(n_scen, n_arc, rows, cols, tiles, dual, rhs, cost, primal):
    copies = cost.size // TILE
    col_tiles = copies // cost.shape[0]
    share = dual.shape[0] // n_arc
    slots = jax.ShapeDtypeStruct(rows.shape, jnp.int32)
    wide = f32(copies, TILE)
    own = f32(share, TILE)
    half = f32(dual.shape[0] // CORE, TILE)
    return pl.pallas_call(
        functools.partial(first_kernel, n_scen, n_arc),
        out_shape=[
            pltpu.VMEM((copies, TILE, PER_COPY * TILE), BF16),
            slots,
            half,
            half,
            wide,
            wide,
            wide,
            wide,
            f32(3 * col_tiles, TILE),
            own,
            own,
        ],
        in_specs=[HBM] * 7,
        out_specs=[VMEM, SMEM] + [VMEM] * 9,
        scratch_shapes=[
            pltpu.VMEM((RING, CHUNK, TILE, TILE), BF16),
            pltpu.SemaphoreType.DMA((RING,)),
            pltpu.SMEM((copies,), jnp.int32),
            pltpu.VMEM(dual.shape, F32),
            pltpu.VMEM(dual.shape, F32),
            pltpu.SMEM(rows.shape, jnp.int32),
            pltpu.SMEM(cols.shape, jnp.int32),
            pltpu.VMEM(cost.shape, F32),
            pltpu.VMEM(primal.shape, F32),
            pltpu.SemaphoreType.DMA((7,)),
        ],
        compiler_params=pltpu.CompilerParams(vmem_limit_bytes=LIMIT),
    )(
        *[
            pltpu.with_memory_space_constraint(a, pltpu.HBM)
            for a in (rows, cols, tiles, dual, rhs, cost, primal)
        ]
    )


def again(kernel, outs, scalars, turned, *vectors, scratch=()):
    specs = [SMEM] * len(scalars)
    if turned is not None:
        vectors = (pltpu.with_memory_space_constraint(turned, pltpu.VMEM), *vectors)
    return pl.pallas_call(
        kernel,
        out_shape=outs,
        in_specs=specs + [VMEM] * len(vectors),
        out_specs=[VMEM] * len(outs),
        scratch_shapes=scratch,
        compiler_params=pltpu.CompilerParams(vmem_limit_bytes=LIMIT),
        cost_estimate=pl.CostEstimate(
            flops=7 * 10**9 if turned is not None else 10**6, bytes_accessed=2**20, transcendentals=0
        ),
    )(*scalars, *vectors)


def swap_core(values):
    n = lax.axis_size("arc")
    return lax.ppermute(values, "arc", [(i, i ^ 1) for i in range(n)])


def exchange(values):
    n = lax.axis_size("arc")
    groups = [[*range(c, n, CORE)] for c in range(CORE)]
    return lax.all_to_all(values, "arc", 0, 0, axis_index_groups=groups, tiled=True)


def with_scen(values):
    n = lax.axis_size("scen")
    shifts = [[(i, (i - k) % n) for i in range(n)] for k in (1, 3, 2)]
    return [values] + [lax.ppermute(values, "scen", pairs) for pairs in shifts]


def all_scen(values):
    n = lax.axis_size("scen")
    spread = jnp.broadcast_to(values[None], (n, *values.shape))
    return lax.all_to_all(spread, "scen", 0, 0, tiled=True).reshape(-1, values.shape[1])


def per_device(tiles, tile_rows, tile_cols, design, cost, rhs, primal, dual, step_size):
    tile = tiles.shape[1]
    scen_dev, cols_dev = primal.shape
    col_tiles = cols_dev // tile
    row_tiles = dual.shape[0] // tile
    copies = scen_dev * col_tiles
    n_scen, n_arc = lax.axis_size("scen"), lax.axis_size("arc")
    share = row_tiles // n_arc
    chips = n_arc // CORE
    wide = f32(copies, tile)
    tall = f32(row_tiles, tile)
    own = f32(share, tile)
    design = design.reshape(col_tiles, tile)
    step_size, cost = lax.optimization_barrier((jnp.full((1, tile), step_size), cost))

    (
        turned, slot_rows, keep, give, col_peak, gap, cost, primal, send, own_dual, own_rhs
    ) = start(
        n_scen, n_arc, tile_rows, tile_cols, tiles,
        dual.reshape(row_tiles, tile), rhs.reshape(row_tiles, tile), cost, primal,
    )
    sends = with_scen(send)
    near, sends = lax.optimization_barrier((swap_core(give), sends))
    reduced = exchange(jnp.maximum(keep, near).reshape(chips, share, tile))
    own_scale = 1.0 / jnp.sqrt(high([*reduced]))
    own_scale, col_peak = lax.optimization_barrier((own_scale, col_peak))
    half = f32(row_tiles // CORE, tile)
    keep, give, col_scale, means = again(
        row_kernel, [half, f32(half.shape[0] + share, tile), wide, f32(2 * col_tiles, tile)],
        [slot_rows], turned, own_scale, col_peak, design, *sends,
        scratch=[pltpu.VMEM(tall.shape, F32)],
    )
    near = swap_core(give)
    row_high = jnp.maximum(keep, near[: half.shape[0]]).reshape(chips, share, tile)
    scales = [
        jnp.broadcast_to(v[None], row_high.shape) for v in (own_scale, near[half.shape[0] :])
    ]
    gathered = exchange(jnp.stack((*scales, row_high), axis=1))
    col_peak, send, own_row = again(
        col_kernel, [wide, f32(2 * col_tiles + 8, tile), own], [slot_rows],
        turned, gathered.reshape(-1, tile), own_scale, own_rhs, col_scale, cost, design,
        scratch=[pltpu.VMEM(tall.shape, F32)],
    )
    shared, send = again(
        norm_kernel, [f32(col_tiles, tile), f32(n_arc, tile)], [], None, design, all_scen(send)
    )
    totals = lax.all_to_all(send, "arc", 0, 0, tiled=True)

    keep, give, new_primal, scalars = again(
        functools.partial(image_kernel, share),
        [tall, tall, f32(scen_dev, cols_dev), f32(8, tile)], [slot_rows],
        turned, step_size, totals, col_peak, shared, col_scale, gap, means, primal, design,
        scratch=[pltpu.VMEM(a.shape, F32) for a in (wide, tall, tall)],
    )
    images = exchange((keep + swap_core(give)).reshape(chips, 2 * share, tile))
    new_dual, send = again(
        dual_kernel, [own, f32(n_scen * n_arc, tile)], [], None,
        step_size, scalars, images.reshape(row_tiles, tile), own_row, own_rhs, own_dual,
    )
    sums = jnp.sum(lax.all_to_all(send, ("scen", "arc"), 0, 0, tiled=True), axis=0)
    return (new_primal, new_dual.reshape(share * tile), sums[0], sums[1])


def solution(mesh):
    placed = (
        P(("scen", "arc"), None, None),
        P(("scen", "arc")),
        P(("scen", "arc")),
        P("arc"),
        P("scen", "arc"),
        P("scen"),
        P("scen", "arc"),
        P("scen"),
        P(),
    )
    return jax.shard_map(
        per_device,
        mesh=mesh,
        in_specs=placed,
        out_specs=(P("scen", "arc"), P(("scen", "arc")), P(), P()),
        check_vma=False,
    )
```
